512 devices in a mesh: row: 32 (over x_lo, z, core), tm: 16 (over y, x_hi).
Axes of the slice: x: 4 (x_hi: 2, x_lo: 2; x = x_hi * 2 + x_lo), y: 8, z: 8, core: 2. Of those that a mesh axis runs over, the one named last changes fastest.
Arguments:
- snapshots: float32 [16384, 16384], P('row', 'tm'), may hold values from -40 to 40
- weights: float32 [16384], P('row'), may hold values from 0.25 to 4
- block_delay: int32 [128], P('tm'), may hold values from 0 to 64, as said below
Outputs:
- csd: float32 [128, 2, 128, 128], P('row', None, 'tm')
The draws below stay inside these ranges and needn't reach their ends.
Inputs may be any that keep to these rules, and one draw needn't show every extreme that they name: `block_delay`: block b starts at snapshot b * 128 plus its delay, counted cyclically over the 16384 snapshots; some block has delay 0 and some has delay 64.
All inputs are finite; a program needn't handle non-finite values.
Results may differ from the reference program's by a relative error of at most 0.004.
Values may be sent and summed in bfloat16 or wider, within the bound.
No kernel may reach another device: no remote copies, remote signals or barrier semaphores. Data moves between devices by JAX's collectives and lax.ppermute only.
A program may use at most 64 MiB of HBM per device.

```python
import math
import jax
import jax.numpy as jnp
from jax import lax

NFFT = 256
NF = 128
HOP = 128
JIT = 64
NT = 16384
NBLK = 128
NG = 16384


def draw_snapshots(key, part):
    key = jax.random.fold_in(key, 1)
    k_noise, k_rows, k_cols = jax.random.split(key, 3)
    row_scale = jnp.exp(jax.random.uniform(k_rows, (NG, 1), jnp.float32, -1.15, 1.15))
    col_scale = jnp.exp(jax.random.uniform(k_cols, (1, NT), jnp.float32, -1.15, 1.15))
    noise = jax.random.truncated_normal(k_noise, -4.0, 4.0, (NG, NT), jnp.float32)
    return (noise * row_scale * col_scale).astype(jnp.float32)


def draw_block_delay(key, part):
    key = jax.random.fold_in(key, 2)
    k_values, k_place = jax.random.split(key, 2)
    delays = jax.random.randint(k_values, (NBLK,), 0, JIT + 1, jnp.int32)
    place = jax.random.randint(k_place, (), 0, NBLK, jnp.int32)
    positions = jnp.arange(NBLK, dtype=jnp.int32)
    delays = jnp.where(positions == place, JIT, delays)
    delays = jnp.where(positions == (place + NBLK // 2) % NBLK, 0, delays)
    return delays.astype(jnp.int32)


def levels(key, dims, pieces, low, largest):
    level, own = 1.0, jax.random.fold_in(key, 6)
    for dim, blocks in pieces:
        heights = jnp.exp(jax.random.uniform(jax.random.fold_in(own, dim), (blocks,), jnp.float32, low / len(pieces), largest / len(pieces)))
        level = level * jnp.repeat(heights, dims[dim] // blocks).reshape([-1 if axis == dim else 1 for axis in range(len(dims))])
    return level


def setup_inputs(seed: int = 0) -> dict:
    seeds = jax.random.split(jax.random.key(seed), 4)
    snapshots = draw_snapshots(jax.random.fold_in(seeds[3], 71), 0)
    weights = jnp.clip(jnp.exp(math.log(4.0) - 2.7725887 * jax.random.uniform(seeds[1], (NG,), jnp.float32) ** levels(seeds[1], (NG,), ((0, 32),), -0.2, 0.2)), 0.25, 4.0)
    block_delay = draw_block_delay(jax.random.fold_in(seeds[3], 71), 0)
    return {"snapshots": snapshots, "weights": weights, "block_delay": block_delay}


def dft_table(length, freqs):
    time_index = jnp.arange(length, dtype=jnp.int32)
    freq_index = jnp.arange(freqs, dtype=jnp.int32)
    phase_steps = time_index[:, None] * freq_index[None, :] % length
    angles = 2.0 * jnp.pi * phase_steps.astype(jnp.float32) / length
    window = jnp.sin(jnp.pi * time_index.astype(jnp.float32) / length) ** 2
    window_norm = jnp.sqrt(jnp.sum(window * window))
    dft_matrix = jnp.concatenate([window[:, None] * jnp.cos(angles), -window[:, None] * jnp.sin(angles)], axis=1) / window_norm
    return dft_matrix.astype(jnp.bfloat16)

def reference(snapshots, weights, block_delay):
    dft_matrix = dft_table(NFFT, NF).astype(jnp.float32)
    rounded = snapshots.astype(jnp.bfloat16)
    row_scale = jnp.sqrt(weights / NG)
    offsets = jnp.arange(NFFT, dtype=jnp.int32)

    def one_block(block):
        start_at = block * HOP + block_delay[block]
        column_ids = ((start_at + offsets) % NT).astype(jnp.int32)
        segment = jnp.take(rounded, column_ids, axis=1).astype(jnp.float32)
        spectrum = jnp.dot(segment, dft_matrix, preferred_element_type=jnp.float32)
        spectrum = (spectrum * row_scale[:, None]).astype(jnp.bfloat16)
        return spectrum.T
    spectra = lax.map(one_block, jnp.arange(NBLK, dtype=jnp.int32))

    def one_freq(freq):
        real_rows = lax.dynamic_index_in_dim(spectra, freq, 1, keepdims=False)
        imag_rows = lax.dynamic_index_in_dim(spectra, freq + NF, 1, keepdims=False)
        stacked = jnp.stack([real_rows, imag_rows], axis=1).astype(jnp.float32)
        products = jnp.einsum('iag,jbg->abij', stacked, stacked)
        real_part = products[0, 0] + products[1, 1]
        imag_part = products[0, 1] - products[1, 0]
        return jnp.stack([real_part, imag_part], axis=0)
    per_freq = lax.map(one_freq, jnp.arange(NF, dtype=jnp.int32))
    return jnp.transpose(per_freq, (2, 1, 0, 3))
```

```python
import jax
import jax.numpy as jnp
import numpy as np
from jax import lax
from jax.experimental import pallas as pl
from jax.experimental.pallas import tpu as pltpu
from jax.sharding import PartitionSpec as P

NFFT = 256
NF = 128
HOP = 128
RIM = 192
REACH = 384
STRIP = 256


def shifted(array, axis, by):
    count = lax.axis_size(axis)
    return lax.ppermute(array, axis, [(i, (i + by) % count) for i in range(count)])


def dft_rows(groups):
    time_index = np.arange(NFFT)
    angles = 2.0 * np.pi * (time_index[:, None] * np.arange(NF)[None, :] % NFFT) / NFFT
    window = np.sin(np.pi * time_index / NFFT) ** 2
    norm = np.sqrt(np.sum(window * window))
    table = np.stack([window[:, None] * np.cos(angles), -window[:, None] * np.sin(angles)])
    table = (table / norm).reshape(2, NFFT, groups, NF // groups)
    rows = table.transpose(2, 0, 3, 1).reshape(2 * NF, NFFT)
    rows = np.pad(rows, ((0, 0), (0, REACH - NFFT)))
    return jnp.asarray(rows, jnp.float32).astype(jnp.bfloat16)


def dft_kernel(total_rows, delay_ref, table_ref, weight_ref, snap_ref, rim_ref, out_ref, shifted_ref, data_ref):
    strip, span = snap_ref.shape
    blocks = delay_ref.shape[0]
    groups, _, pairs, _ = out_ref.shape

    @pl.when(pl.program_id(0) == 0)
    def _():
        table = table_ref[...].astype(jnp.float32)
        for block in range(blocks):
            moved = pltpu.roll(table, delay_ref[block], 1)
            shifted_ref[block] = moved.astype(jnp.bfloat16)

    data_ref[:, :span] = snap_ref[...].astype(jnp.bfloat16)
    data_ref[:, span:] = jnp.concatenate(
        [rim_ref[...], jnp.zeros((strip, data_ref.shape[1] - span - RIM), jnp.bfloat16)], axis=1
    )
    scale = jnp.sqrt(weight_ref[...] / total_rows)
    for block in range(blocks):
        spectrum = lax.dot_general(
            shifted_ref[block],
            data_ref[:, block * HOP : block * HOP + REACH],
            (((1,), (1,)), ((), ())),
            preferred_element_type=jnp.float32,
        )
        spectrum = (spectrum * scale).astype(jnp.bfloat16)
        out_ref[:, block] = spectrum.reshape(groups, pairs, strip)


def block_spectra(snapshots, rim, weights, block_delay, groups, total_rows):
    rows, span = snapshots.shape
    blocks = span // HOP
    pairs = 2 * NF // groups
    return pl.pallas_call(
        lambda *refs: dft_kernel(total_rows, *refs),
        grid=(rows // STRIP,),
        in_specs=[
            pl.BlockSpec(memory_space=pltpu.SMEM),
            pl.BlockSpec((2 * NF, REACH), lambda s: (0, 0)),
            pl.BlockSpec((1, STRIP), lambda s: (0, s)),
            pl.BlockSpec((STRIP, span), lambda s: (s, 0)),
            pl.BlockSpec((STRIP, RIM), lambda s: (s, 0)),
        ],
        out_specs=pl.BlockSpec((groups, blocks, pairs, STRIP), lambda s: (0, 0, 0, s)),
        out_shape=jax.ShapeDtypeStruct((groups, blocks, pairs, rows), jnp.bfloat16),
        scratch_shapes=[
            pltpu.VMEM((blocks, 2 * NF, REACH), jnp.bfloat16),
            pltpu.VMEM((STRIP, span + REACH - HOP), jnp.bfloat16),
        ],
        compiler_params=pltpu.CompilerParams(vmem_limit_bytes=32 * 1024 * 1024),
        name="dft",
    )(block_delay, dft_rows(groups), weights.reshape(1, rows), snapshots, rim)


def csd_kernel(order_ref, got_ref, out_ref, sorted_ref):
    step = pl.program_id(0)
    some, pairs, rows = got_ref.shape
    freqs = pairs // 2
    every = sorted_ref.shape[1]
    chunk = got_ref[...].reshape(some * pairs, rows)
    by_pair = lax.dot_general(
        order_ref[...], chunk, (((1,), (0,)), ((), ())), preferred_element_type=jnp.float32
    )
    start = pl.multiple_of(step * some, some)
    sorted_ref[:, pl.ds(start, some), :] = by_pair.astype(jnp.bfloat16).reshape(pairs, some, rows)

    @pl.when(step == pl.num_programs(0) - 1)
    def _():
        real, imag = [], []
        for freq in range(freqs):
            both = sorted_ref[2 * freq : 2 * freq + 2].reshape(2 * every, rows)
            power = lax.dot_general(
                both, both, (((1,), (1,)), ((), ())), preferred_element_type=jnp.float32
            )
            real.append(power[:every, :every] + power[every:, every:])
            imag.append(power[:every, every:] - power[every:, :every])
            if freq % 4 == 3:
                for part, quad in ((0, real), (1, imag)):
                    place = part * freqs * 4 + (freq - 3) * 4
                    low, high = split_quads(quad)
                    out_ref[:, 0, place : place + 16, :] = low.astype(jnp.bfloat16)
                    out_ref[:, 1, place : place + 16, :] = high.astype(jnp.bfloat16)
                real, imag = [], []


def split_quads(mats):
    eights = [m.reshape(m.shape[0] // 8, 8, m.shape[1]) for m in mats]
    upper = lax.broadcasted_iota(jnp.int32, eights[0].shape, 1) < 4
    low, high = [], []
    for a, b in (eights[:2], eights[2:]):
        low.append(jnp.where(upper, a, pltpu.roll(b, 4, 1)))
        high.append(jnp.where(upper, pltpu.roll(a, 4, 1), b))
    return jnp.concatenate(low, axis=1), jnp.concatenate(high, axis=1)


def cross_power(received):
    every, pairs, rows = received.shape
    freqs = pairs // 2
    some = 2 * NF // pairs
    source = np.arange(some * pairs).reshape(some, 2, freqs).transpose(2, 1, 0).reshape(-1)
    order = jnp.asarray(np.eye(some * pairs)[source], jnp.bfloat16)
    return pl.pallas_call(
        csd_kernel,
        grid=(every // some,),
        in_specs=[
            pl.BlockSpec((some * pairs, some * pairs), lambda s: (0, 0)),
            pl.BlockSpec((some, pairs, rows), lambda s: (s, 0, 0)),
        ],
        out_specs=pl.BlockSpec((every // 8, 2, 8 * freqs, every), lambda s: (0, 0, 0, 0)),
        out_shape=jax.ShapeDtypeStruct((every // 8, 2, 8 * freqs, every), jnp.bfloat16),
        scratch_shapes=[pltpu.VMEM((pairs, every, rows), jnp.bfloat16)],
        compiler_params=pltpu.CompilerParams(vmem_limit_bytes=32 * 1024 * 1024),
        name="csd",
    )(order, received)


def total_kernel(got_ref, out_ref, sum_ref):
    sum_ref[...] = jnp.sum(got_ref[...].astype(jnp.float32), axis=0)
    own, parts, freqs, _ = out_ref.shape
    for part in range(parts):
        for freq in range(freqs):
            for i in range(own):
                row = (part * freqs + freq) * own + i
                out_ref[i, part, freq : freq + 1, :] = sum_ref[row : row + 1, :]


def totals(got, freqs):
    _, lines, every = got.shape
    own = lines // (2 * freqs)
    return pl.pallas_call(
        total_kernel,
        out_shape=jax.ShapeDtypeStruct((own, 2, freqs, every), jnp.float32),
        scratch_shapes=[pltpu.VMEM((lines, every), jnp.float32)],
        name="total",
    )(got)


def body(snapshots, weights, block_delay):
    time_groups = lax.axis_size("tm")
    row_groups = lax.axis_size("row")
    grid_rows = snapshots.shape[0]
    freqs = NF // time_groups
    rim = shifted(snapshots[:, :RIM].astype(jnp.bfloat16), "tm", -1)
    spectra = block_spectra(
        snapshots, rim, weights, block_delay, time_groups, grid_rows * row_groups
    )
    received = lax.all_to_all(spectra, "tm", split_axis=0, concat_axis=0, tiled=True)
    received = received.reshape(-1, 2 * freqs, grid_rows)
    partial_csd = cross_power(received)
    every = received.shape[0]
    partial_csd = partial_csd.reshape(row_groups, 8 * freqs, every)
    got = lax.all_to_all(partial_csd, "row", split_axis=0, concat_axis=0, tiled=True)
    return totals(got, freqs)


def solution(mesh):
    placed = (P("row", "tm"), P("row"), P("tm"))
    return jax.shard_map(
        body, mesh=mesh, in_specs=placed, out_specs=P("row", None, "tm", None), check_vma=False
    )
```

```python
import jax
import jax.numpy as jnp
import numpy as np
from jax import lax
from jax.experimental import pallas as pl
from jax.experimental.pallas import tpu as pltpu
from jax.sharding import Mesh
from jax.sharding import PartitionSpec as P

NFFT = 256
NF = 128
HOP = 128
RIM = 192
REACH = 384
STRIP = 256
CORES = 2
VMEM = 56 * 1024 * 1024


def shifted(array, axis, by):
    count = lax.axis_size(axis)
    return lax.ppermute(array, axis, [(i, (i + by) % count) for i in range(count)])


def dft_rows(groups):
    time_index = np.arange(NFFT)
    angles = 2.0 * np.pi * (time_index[:, None] * np.arange(NF)[None, :] % NFFT) / NFFT
    window = np.sin(np.pi * time_index / NFFT) ** 2
    norm = np.sqrt(np.sum(window * window))
    table = np.stack([window[:, None] * np.cos(angles), -window[:, None] * np.sin(angles)])
    table = (table / norm).reshape(2, NFFT, groups, CORES, NF // groups // CORES)
    rows = table.transpose(3, 2, 0, 4, 1).reshape(2 * NF, NFFT)
    rows = np.pad(rows, ((0, 0), (0, REACH - NFFT)))
    return jnp.asarray(rows, jnp.float32).astype(jnp.bfloat16)


def dft_kernel(first, total_rows, delay_ref, table_ref, weight_ref, snap_ref, *refs):
    rim_ref = refs[0] if len(refs) == 4 else None
    out_ref, shifted_ref, data_ref = refs[-3:]
    strip, span = snap_ref.shape
    targets, block_pairs, _, _ = out_ref.shape

    @pl.when(pl.program_id(0) == 0)
    def _():
        table = table_ref[...].astype(jnp.float32)
        for block in range(2 * block_pairs):
            moved = pltpu.roll(table, delay_ref[first + block], 1)
            shifted_ref[block] = moved.astype(jnp.bfloat16)

    data_ref[:, :span] = snap_ref[...].astype(jnp.bfloat16)
    if rim_ref is not None:
        gap = jnp.zeros((strip, data_ref.shape[1] - span - RIM), jnp.bfloat16)
        data_ref[:, span:] = jnp.concatenate([rim_ref[...], gap], axis=1)
    scale = jnp.sqrt(weight_ref[...] / total_rows)
    for pair in range(block_pairs):
        two = []
        for block in (2 * pair, 2 * pair + 1):
            spectrum = lax.dot_general(
                shifted_ref[block],
                data_ref[:, block * HOP : block * HOP + REACH],
                (((1,), (1,)), ((), ())),
                preferred_element_type=jnp.float32,
            )
            two.append((spectrum * scale).reshape(targets, -1, strip))
        out_ref[:, pair] = jnp.concatenate(two, axis=1).astype(jnp.bfloat16)


def block_spectra(snapshots, rim, weights, block_delay, first, count, targets, table, total_rows):
    rows, width = snapshots.shape
    begin = first * HOP
    span = width - begin if rim is not None else (count - 1) * HOP + REACH
    specs = [
        pl.BlockSpec(memory_space=pltpu.SMEM),
        pl.BlockSpec((2 * NF, REACH), lambda s: (0, 0)),
        pl.BlockSpec((1, STRIP), lambda s: (0, s)),
        pl.BlockSpec((STRIP, span), lambda s: (s, begin // span)),
    ]
    operands = [block_delay, table, weights.reshape(1, rows), snapshots]
    if rim is not None:
        specs.append(pl.BlockSpec((STRIP, RIM), lambda s: (s, 0)))
        operands.append(rim)
    shape = (targets, count // 2, 4 * NF // targets, rows)
    return pl.pallas_call(
        lambda *refs: dft_kernel(first, total_rows, *refs),
        grid=(rows // STRIP,),
        in_specs=specs,
        out_specs=pl.BlockSpec(shape[:3] + (STRIP,), lambda s: (0, 0, 0, s)),
        out_shape=jax.ShapeDtypeStruct(shape, jnp.bfloat16),
        scratch_shapes=[
            pltpu.VMEM((count, 2 * NF, REACH), jnp.bfloat16),
            pltpu.VMEM((STRIP, (count - 1) * HOP + REACH), jnp.bfloat16),
        ],
        compiler_params=pltpu.CompilerParams(vmem_limit_bytes=VMEM),
        cost_estimate=pl.CostEstimate(
            flops=4 * NF * REACH * rows * count,
            bytes_accessed=4 * rows * span + 4 * NF * rows * count,
            transcendentals=0,
        ),
        name="dft_late" if rim is not None else "dft_early",
    )(*operands)


def csd_kernel(order_ref, early_ref, late_ref, out_ref, sorted_ref):
    step = pl.program_id(0)
    cores, lines, every, rows = sorted_ref.shape
    some = every * cores // pl.num_programs(0)
    chunk = jnp.concatenate(
        [early_ref[...].reshape(-1, rows), late_ref[...].reshape(-1, rows)], axis=0
    )
    by_line = lax.dot_general(
        order_ref[...], chunk, (((1,), (0,)), ((), ())), preferred_element_type=jnp.float32
    )
    core = step // (every // some)
    start = pl.multiple_of(step % (every // some) * some, some)
    sorted_ref[core, :, pl.ds(start, some), :] = by_line.astype(jnp.bfloat16).reshape(
        lines, some, rows
    )

    @pl.when(step == pl.num_programs(0) - 1)
    def _():
        real, imag = [], []
        for freq in range(lines // 2):
            power = 0.0
            for c in range(cores):
                both = sorted_ref[c, 2 * freq : 2 * freq + 2].reshape(2 * every, rows)
                power += lax.dot_general(
                    both, both, (((1,), (1,)), ((), ())), preferred_element_type=jnp.float32
                )
            real.append(power[:every, :every] + power[every:, every:])
            imag.append(power[:every, every:] - power[every:, :every])
        for place, quad in ((0, real), (16, imag)):
            low, high = split_quads(quad)
            out_ref[:, 0, place : place + 16, :] = low.astype(jnp.bfloat16)
            out_ref[:, 1, place : place + 16, :] = high.astype(jnp.bfloat16)


def split_quads(mats):
    eights = [m.reshape(m.shape[0] // 8, 8, m.shape[1]) for m in mats]
    upper = lax.broadcasted_iota(jnp.int32, eights[0].shape, 1) < 4
    low, high = [], []
    for a, b in (eights[:2], eights[2:]):
        low.append(jnp.where(upper, a, pltpu.roll(b, 4, 1)))
        high.append(jnp.where(upper, pltpu.roll(a, 4, 1), b))
    return jnp.concatenate(low, axis=1), jnp.concatenate(high, axis=1)


def cross_power(early, late):
    sources, early_pairs, _, rows = early.shape
    late_pairs = late.shape[1]
    groups = sources // CORES
    blocks = 2 * (early_pairs + late_pairs)
    freqs = NF // sources
    every = groups * blocks
    some = 4
    early_rows = np.arange(some * early_pairs * 2 * 2 * freqs)
    late_rows = early_rows.size + np.arange(some * late_pairs * 2 * 2 * freqs)
    source = np.concatenate(
        [
            early_rows.reshape(some, 2 * early_pairs, 2, freqs),
            late_rows.reshape(some, 2 * late_pairs, 2, freqs),
        ],
        axis=1,
    )
    source = source.transpose(3, 2, 0, 1).reshape(-1)
    order = jnp.asarray(np.eye(source.size)[source], jnp.bfloat16)
    shape = (every // 8, 2, 8 * freqs, every)
    return pl.pallas_call(
        csd_kernel,
        grid=(sources // some,),
        in_specs=[
            pl.BlockSpec(order.shape, lambda s: (0, 0)),
            pl.BlockSpec((some,) + early.shape[1:], lambda s: (s, 0, 0, 0)),
            pl.BlockSpec((some,) + late.shape[1:], lambda s: (s, 0, 0, 0)),
        ],
        out_specs=pl.BlockSpec(shape, lambda s: (0, 0, 0, 0)),
        out_shape=jax.ShapeDtypeStruct(shape, jnp.bfloat16),
        scratch_shapes=[pltpu.VMEM((CORES, 2 * freqs, every, rows), jnp.bfloat16)],
        compiler_params=pltpu.CompilerParams(vmem_limit_bytes=32 * 1024 * 1024),
        name="csd",
    )(order, early, late)


def total_kernel(got_ref, out_ref, sum_ref):
    own, parts, freqs, _ = out_ref.shape
    sum_ref[...] = jnp.sum(got_ref[...].astype(jnp.float32), axis=0)
    few = freqs // CORES
    for core in range(CORES):
        for part in range(parts):
            for freq in range(few):
                for i in range(own):
                    row = (part * few + freq) * own + i
                    place = core * few + freq
                    out_ref[i, part, place : place + 1, :] = sum_ref[core, row : row + 1, :]


def totals(got, freqs):
    chips, cores, lines, every = got.shape
    own = lines * cores // (2 * freqs)
    return pl.pallas_call(
        total_kernel,
        out_shape=jax.ShapeDtypeStruct((own, 2, freqs, every), jnp.float32),
        scratch_shapes=[pltpu.VMEM((cores, lines, every), jnp.float32)],
        name="total",
    )(got)


def body(snapshots, weights, block_delay):
    time_groups = lax.axis_size("tm")
    chips = lax.axis_size("chip")
    grid_rows, span = snapshots.shape
    blocks = span // HOP
    early_blocks = (span - REACH) // HOP + 1
    freqs = NF // time_groups
    targets = CORES * time_groups
    total_rows = grid_rows * chips * CORES
    table = dft_rows(time_groups)
    rim = shifted(snapshots[:, :RIM].astype(jnp.bfloat16), "tm", -1)
    received = []
    for first, count, edge in (
        (0, early_blocks, None),
        (early_blocks, blocks - early_blocks, rim),
    ):
        spectra = block_spectra(
            snapshots, edge, weights, block_delay, first, count, targets, table, total_rows
        )
        received.append(
            lax.all_to_all(spectra, ("core", "tm"), split_axis=0, concat_axis=0, tiled=True)
        )
    partial_csd = cross_power(*received)
    partial_csd = partial_csd.reshape(chips * CORES, 4 * freqs, -1)
    got = lax.all_to_all(partial_csd, ("chip", "core"), split_axis=0, concat_axis=0, tiled=True)
    return totals(got.reshape(chips, CORES, 4 * freqs, -1), freqs)


def solution(mesh):
    rows, groups = mesh.devices.shape
    by_core = Mesh(mesh.devices.reshape(rows // CORES, CORES, groups), ("chip", "core", "tm"))
    row = ("chip", "core")
    return jax.shard_map(
        body,
        mesh=by_core,
        in_specs=(P(row, "tm"), P(row), P("tm")),
        out_specs=P(row, None, "tm", None),
        check_vma=False,
    )
```

```python
import jax
import jax.numpy as jnp
import numpy as np
from jax import lax
from jax.experimental import pallas as pl
from jax.experimental.pallas import tpu as pltpu
from jax.sharding import Mesh
from jax.sharding import PartitionSpec as P

NFFT = 256
NF = 128
HOP = 128
RIM = 192
REACH = 384
STRIP = 256
INNER = 4
QUAD = 4
VMEM = 56 * 1024 * 1024


def shifted(array, axis, by):
    count = lax.axis_size(axis)
    return lax.ppermute(array, axis, [(i, (i + by) % count) for i in range(count)])


def dft_rows(groups):
    time_index = np.arange(NFFT)
    angles = 2.0 * np.pi * (time_index[:, None] * np.arange(NF)[None, :] % NFFT) / NFFT
    window = np.sin(np.pi * time_index / NFFT) ** 2
    norm = np.sqrt(np.sum(window * window))
    table = np.stack([window[:, None] * np.cos(angles), -window[:, None] * np.sin(angles)])
    table = (table / norm).reshape(2, NFFT, groups, INNER, NF // groups // INNER)
    rows = table.transpose(3, 2, 0, 4, 1).reshape(2 * NF, NFFT)
    rows = np.pad(rows, ((0, 0), (0, REACH - NFFT)))
    return jnp.asarray(rows, jnp.float32).astype(jnp.bfloat16)


def split_quads(mats):
    eights = [m.reshape(m.shape[0] // 8, 8, m.shape[1]) for m in mats]
    upper = lax.broadcasted_iota(jnp.int32, eights[0].shape, 1) < 4
    low, high = [], []
    for a, b in (eights[:2], eights[2:]):
        low.append(jnp.where(upper, a, pltpu.roll(b, 4, 1)))
        high.append(jnp.where(upper, pltpu.roll(a, 4, 1), b))
    return jnp.concatenate(low, axis=1), jnp.concatenate(high, axis=1)


def dft_kernel(first, total_rows, delay_ref, table_ref, weight_ref, snap_ref, *refs):
    late = first > 0
    shifted_ref, data_ref = refs[-2:]
    rim_ref, out_ref = refs[:2] if late else refs[1::-1]
    strip, span = snap_ref.shape

    @pl.when(pl.program_id(0) == 0)
    def _():
        table = table_ref[...].astype(jnp.float32)
        for block in range(QUAD):
            moved = pltpu.roll(table, delay_ref[first + block], 1)
            shifted_ref[block] = moved.astype(jnp.bfloat16)

    data_ref[:, :span] = snap_ref[...].astype(jnp.bfloat16)
    if late:
        gap = jnp.zeros((strip, data_ref.shape[1] - span - RIM), jnp.bfloat16)
        data_ref[:, span:] = jnp.concatenate([rim_ref[...], gap], axis=1)
    else:
        rim_ref[...] = data_ref[:, :RIM]
    scale = jnp.sqrt(weight_ref[...] / total_rows)
    spectra = []
    for block in range(QUAD):
        spectrum = lax.dot_general(
            shifted_ref[block],
            data_ref[:, block * HOP : block * HOP + REACH],
            (((1,), (1,)), ((), ())),
            preferred_element_type=jnp.float32,
        )
        spectra.append(spectrum * scale)
    low, high = split_quads(spectra)
    out_ref[:, 0] = low.astype(jnp.bfloat16)
    out_ref[:, 1] = high.astype(jnp.bfloat16)


def block_spectra(snapshots, rim, weights, block_delay, first, targets, table, total_rows):
    rows, _ = snapshots.shape
    begin = first * HOP
    width = (QUAD - 1) * HOP + REACH
    span = QUAD * HOP if rim is not None else width
    specs = [
        pl.BlockSpec(memory_space=pltpu.SMEM),
        pl.BlockSpec((2 * NF, REACH), lambda s: (0, 0)),
        pl.BlockSpec((1, STRIP), lambda s: (0, s)),
        pl.BlockSpec((STRIP, span), lambda s: (s, begin // span)),
    ]
    operands = [block_delay, table, weights.reshape(1, rows), snapshots]
    rim_spec = pl.BlockSpec((STRIP, RIM), lambda s: (s, 0))
    shape = (targets // 2, 2, 16, rows)
    out_specs = [pl.BlockSpec(shape[:3] + (STRIP,), lambda s: (0, 0, 0, s))]
    out_shape = [jax.ShapeDtypeStruct(shape, jnp.bfloat16)]
    if rim is not None:
        specs.append(rim_spec)
        operands.append(rim)
    else:
        out_specs.append(rim_spec)
        out_shape.append(jax.ShapeDtypeStruct((rows, RIM), jnp.bfloat16))
    spectra, *edge = pl.pallas_call(
        lambda *refs: dft_kernel(first, total_rows, *refs),
        grid=(rows // STRIP,),
        in_specs=specs,
        out_specs=out_specs,
        out_shape=out_shape,
        scratch_shapes=[
            pltpu.VMEM((QUAD, 2 * NF, REACH), jnp.bfloat16),
            pltpu.VMEM((STRIP, width), jnp.bfloat16),
        ],
        compiler_params=pltpu.CompilerParams(vmem_limit_bytes=VMEM),
        cost_estimate=pl.CostEstimate(
            flops=4 * NF * REACH * rows * QUAD,
            bytes_accessed=4 * rows * span + 4 * NF * rows * QUAD,
            transcendentals=0,
        ),
        name="dft_late" if rim is not None else "dft_early",
    )(*operands)
    return spectra.reshape(targets, 16, rows), edge


def csd_kernel(order_ref, early_ref, late_ref, out_ref, sorted_ref):
    step = pl.program_id(0)
    inner, lines, every, rows = sorted_ref.shape
    some = every * inner // pl.num_programs(0)
    chunk = jnp.concatenate(
        [early_ref[...].reshape(-1, rows), late_ref[...].reshape(-1, rows)], axis=0
    )
    by_line = lax.dot_general(
        order_ref[...], chunk, (((1,), (0,)), ((), ())), preferred_element_type=jnp.float32
    )
    source = step // (every // some)
    start = pl.multiple_of(step % (every // some) * some, some)
    sorted_ref[source, :, pl.ds(start, some), :] = by_line.astype(jnp.bfloat16).reshape(
        lines, some, rows
    )

    @pl.when(step == pl.num_programs(0) - 1)
    def _():
        real, imag = [], []
        for freq in range(lines // 2):
            power = 0.0
            for c in range(inner):
                both = sorted_ref[c, 2 * freq : 2 * freq + 2].reshape(2 * every, rows)
                power += lax.dot_general(
                    both, both, (((1,), (1,)), ((), ())), preferred_element_type=jnp.float32
                )
            real.append(power[:every, :every] + power[every:, every:])
            imag.append(power[:every, every:] - power[every:, :every])
        low, high = split_quads(real + imag)
        out_ref[:, 0] = low.astype(jnp.bfloat16)
        out_ref[:, 1] = high.astype(jnp.bfloat16)


def cross_power(early, late):
    sources, lines, rows = early.shape
    freqs = NF // sources
    every = sources // INNER * 2 * QUAD
    some = 8
    rows_in = np.arange(2 * some * lines).reshape(2, some, QUAD, 2, freqs)
    source = rows_in.transpose(4, 3, 1, 0, 2).reshape(-1)
    order = jnp.asarray(np.eye(source.size)[source], jnp.bfloat16)
    shape = (every // 8, 2, 8 * freqs, every)
    part = pl.BlockSpec((some, lines, rows), lambda s: (s, 0, 0))
    return pl.pallas_call(
        csd_kernel,
        grid=(sources // some,),
        in_specs=[pl.BlockSpec(order.shape, lambda s: (0, 0)), part, part],
        out_specs=pl.BlockSpec(shape, lambda s: (0, 0, 0, 0)),
        out_shape=jax.ShapeDtypeStruct(shape, jnp.bfloat16),
        scratch_shapes=[pltpu.VMEM((INNER, 2 * freqs, every, rows), jnp.bfloat16)],
        compiler_params=pltpu.CompilerParams(vmem_limit_bytes=32 * 1024 * 1024),
        name="csd",
    )(order, early, late)


def total_kernel(got_ref, out_ref, sum_ref):
    own, parts, freqs, _ = out_ref.shape
    sum_ref[...] = jnp.sum(got_ref[...].astype(jnp.float32), axis=0)
    few = freqs // INNER
    for inner in range(INNER):
        for part in range(parts):
            for freq in range(few):
                for i in range(own):
                    row = (part * few + freq) * own + i
                    place = inner * few + freq
                    out_ref[i, part, place : place + 1, :] = sum_ref[inner, row : row + 1, :]


def totals(got, freqs):
    _, inner, lines, every = got.shape
    return pl.pallas_call(
        total_kernel,
        out_shape=jax.ShapeDtypeStruct((QUAD, 2, freqs, every), jnp.float32),
        scratch_shapes=[pltpu.VMEM((inner, lines, every), jnp.float32)],
        name="total",
    )(got)


def body(snapshots, weights, block_delay):
    time_groups = lax.axis_size("tm")
    outer = lax.axis_size("outer")
    total_rows = snapshots.shape[0] * outer * INNER
    freqs = NF // time_groups
    targets = INNER * time_groups
    table = dft_rows(time_groups)

    def exchange(array, axes):
        return lax.all_to_all(array, axes, split_axis=0, concat_axis=0, tiled=True)

    early, (edge,) = block_spectra(
        snapshots, None, weights, block_delay, 0, targets, table, total_rows
    )
    rim = shifted(edge, "tm", -1)
    early_here = exchange(early, ("inner", "tm"))
    late, _ = block_spectra(
        snapshots, rim, weights, block_delay, QUAD, targets, table, total_rows
    )
    late_here = exchange(late, ("inner", "tm"))
    partial_csd = cross_power(early_here, late_here)
    lines = partial_csd.shape[2]
    got = exchange(partial_csd.reshape(outer * INNER, lines, -1), ("outer", "inner"))
    return totals(got.reshape(outer, INNER, lines, -1), freqs)


def solution(mesh):
    rows, groups = mesh.devices.shape
    by_inner = Mesh(mesh.devices.reshape(rows // INNER, INNER, groups), ("outer", "inner", "tm"))
    row = ("outer", "inner")
    return jax.shard_map(
        body,
        mesh=by_inner,
        in_specs=(P(row, "tm"), P(row), P("tm")),
        out_specs=P(row, None, "tm", None),
        check_vma=False,
    )
```

```python
import jax
import jax.numpy as jnp
import numpy as np
from jax import lax
from jax.experimental import pallas as pl
from jax.experimental.pallas import tpu as pltpu
from jax.sharding import Mesh
from jax.sharding import PartitionSpec as P

NFFT = 256
NF = 128
HOP = 128
RIM = 192
REACH = 384
STRIP = 256
CORES = 2
VMEM = 56 * 1024 * 1024


def shifted(array, axis, by):
    count = lax.axis_size(axis)
    return lax.ppermute(array, axis, [(i, (i + by) % count) for i in range(count)])


def dft_rows(groups):
    time_index = np.arange(NFFT)
    angles = 2.0 * np.pi * (time_index[:, None] * np.arange(NF)[None, :] % NFFT) / NFFT
    window = np.sin(np.pi * time_index / NFFT) ** 2
    norm = np.sqrt(np.sum(window * window))
    table = np.stack([window[:, None] * np.cos(angles), -window[:, None] * np.sin(angles)])
    table = (table / norm).reshape(2, NFFT, groups, CORES, NF // groups // CORES)
    rows = table.transpose(3, 2, 0, 4, 1).reshape(2 * NF, NFFT)
    rows = np.pad(rows, ((0, 0), (0, REACH - NFFT)))
    return jnp.asarray(rows, jnp.float32).astype(jnp.bfloat16)


def dft_kernel(first, total_rows, delay_ref, table_ref, weight_ref, snap_ref, *refs):
    late = first > 0
    shifted_ref, data_ref = refs[-2:]
    rim_ref, out_ref = refs[:2] if late else refs[1::-1]
    strip, span = snap_ref.shape
    targets, block_pairs, _, _ = out_ref.shape

    @pl.when(pl.program_id(0) == 0)
    def _():
        table = table_ref[...].astype(jnp.float32)
        for block in range(2 * block_pairs):
            moved = pltpu.roll(table, delay_ref[first + block], 1)
            shifted_ref[block] = moved.astype(jnp.bfloat16)

    data_ref[:, :span] = snap_ref[...].astype(jnp.bfloat16)
    if late:
        gap = jnp.zeros((strip, data_ref.shape[1] - span - RIM), jnp.bfloat16)
        data_ref[:, span:] = jnp.concatenate([rim_ref[...], gap], axis=1)
    else:
        rim_ref[...] = data_ref[:, :RIM]
    scale = jnp.sqrt(weight_ref[...] / total_rows)
    for pair in range(block_pairs):
        two = []
        for block in (2 * pair, 2 * pair + 1):
            spectrum = lax.dot_general(
                shifted_ref[block],
                data_ref[:, block * HOP : block * HOP + REACH],
                (((1,), (1,)), ((), ())),
                preferred_element_type=jnp.float32,
            )
            two.append((spectrum * scale).reshape(targets, -1, strip))
        out_ref[:, pair] = jnp.concatenate(two, axis=1).astype(jnp.bfloat16)


def block_spectra(snapshots, rim, weights, block_delay, first, count, targets, table, total_rows):
    rows, width = snapshots.shape
    begin = first * HOP
    span = width - begin if rim is not None else (count - 1) * HOP + REACH
    specs = [
        pl.BlockSpec(memory_space=pltpu.SMEM),
        pl.BlockSpec((2 * NF, REACH), lambda s: (0, 0)),
        pl.BlockSpec((1, STRIP), lambda s: (0, s)),
        pl.BlockSpec((STRIP, span), lambda s: (s, begin // span)),
    ]
    operands = [block_delay, table, weights.reshape(1, rows), snapshots]
    rim_spec = pl.BlockSpec((STRIP, RIM), lambda s: (s, 0))
    shape = (targets, count // 2, 4 * NF // targets, rows)
    out_specs = [pl.BlockSpec(shape[:3] + (STRIP,), lambda s: (0, 0, 0, s))]
    out_shape = [jax.ShapeDtypeStruct(shape, jnp.bfloat16)]
    if rim is not None:
        specs.append(rim_spec)
        operands.append(rim)
    else:
        out_specs.append(rim_spec)
        out_shape.append(jax.ShapeDtypeStruct((rows, RIM), jnp.bfloat16))
    return pl.pallas_call(
        lambda *refs: dft_kernel(first, total_rows, *refs),
        grid=(rows // STRIP,),
        in_specs=specs,
        out_specs=out_specs,
        out_shape=out_shape,
        scratch_shapes=[
            pltpu.VMEM((count, 2 * NF, REACH), jnp.bfloat16),
            pltpu.VMEM((STRIP, (count - 1) * HOP + REACH), jnp.bfloat16),
        ],
        compiler_params=pltpu.CompilerParams(vmem_limit_bytes=VMEM),
        cost_estimate=pl.CostEstimate(
            flops=4 * NF * REACH * rows * count,
            bytes_accessed=4 * rows * span + 4 * NF * rows * count,
            transcendentals=0,
        ),
        name="dft_late" if rim is not None else "dft_early",
    )(*operands)


def csd_kernel(order_ref, early_ref, late_ref, out_ref, sorted_ref):
    step = pl.program_id(0)
    cores, lines, every, rows = sorted_ref.shape
    some = every * cores // pl.num_programs(0)
    chunk = jnp.concatenate(
        [early_ref[...].reshape(-1, rows), late_ref[...].reshape(-1, rows)], axis=0
    )
    by_line = lax.dot_general(
        order_ref[...], chunk, (((1,), (0,)), ((), ())), preferred_element_type=jnp.float32
    )
    core = step // (every // some)
    start = pl.multiple_of(step % (every // some) * some, some)
    sorted_ref[core, :, pl.ds(start, some), :] = by_line.astype(jnp.bfloat16).reshape(
        lines, some, rows
    )

    @pl.when(step == pl.num_programs(0) - 1)
    def _():
        real, imag = [], []
        for freq in range(lines // 2):
            power = 0.0
            for c in range(cores):
                both = sorted_ref[c, 2 * freq : 2 * freq + 2].reshape(2 * every, rows)
                power += lax.dot_general(
                    both, both, (((1,), (1,)), ((), ())), preferred_element_type=jnp.float32
                )
            real.append(power[:every, :every] + power[every:, every:])
            imag.append(power[:every, every:] - power[every:, :every])
        for place, quad in ((0, real), (16, imag)):
            low, high = split_quads(quad)
            out_ref[:, 0, place : place + 16, :] = low.astype(jnp.bfloat16)
            out_ref[:, 1, place : place + 16, :] = high.astype(jnp.bfloat16)


def split_quads(mats):
    eights = [m.reshape(m.shape[0] // 8, 8, m.shape[1]) for m in mats]
    upper = lax.broadcasted_iota(jnp.int32, eights[0].shape, 1) < 4
    low, high = [], []
    for a, b in (eights[:2], eights[2:]):
        low.append(jnp.where(upper, a, pltpu.roll(b, 4, 1)))
        high.append(jnp.where(upper, pltpu.roll(a, 4, 1), b))
    return jnp.concatenate(low, axis=1), jnp.concatenate(high, axis=1)


def cross_power(early, late):
    sources, early_pairs, _, rows = early.shape
    late_pairs = late.shape[1]
    groups = sources // CORES
    blocks = 2 * (early_pairs + late_pairs)
    freqs = NF // sources
    every = groups * blocks
    some = 4
    early_rows = np.arange(some * early_pairs * 2 * 2 * freqs)
    late_rows = early_rows.size + np.arange(some * late_pairs * 2 * 2 * freqs)
    source = np.concatenate(
        [
            early_rows.reshape(some, 2 * early_pairs, 2, freqs),
            late_rows.reshape(some, 2 * late_pairs, 2, freqs),
        ],
        axis=1,
    )
    source = source.transpose(3, 2, 0, 1).reshape(-1)
    order = jnp.asarray(np.eye(source.size)[source], jnp.bfloat16)
    shape = (every // 8, 2, 8 * freqs, every)
    return pl.pallas_call(
        csd_kernel,
        grid=(sources // some,),
        in_specs=[
            pl.BlockSpec(order.shape, lambda s: (0, 0)),
            pl.BlockSpec((some,) + early.shape[1:], lambda s: (s, 0, 0, 0)),
            pl.BlockSpec((some,) + late.shape[1:], lambda s: (s, 0, 0, 0)),
        ],
        out_specs=pl.BlockSpec(shape, lambda s: (0, 0, 0, 0)),
        out_shape=jax.ShapeDtypeStruct(shape, jnp.bfloat16),
        scratch_shapes=[pltpu.VMEM((CORES, 2 * freqs, every, rows), jnp.bfloat16)],
        compiler_params=pltpu.CompilerParams(vmem_limit_bytes=32 * 1024 * 1024),
        name="csd",
    )(order, early, late)


def total_kernel(got_ref, out_ref, sum_ref):
    own, parts, freqs, _ = out_ref.shape
    sum_ref[...] = jnp.sum(got_ref[...].astype(jnp.float32), axis=0)
    few = freqs // CORES
    for core in range(CORES):
        for part in range(parts):
            for freq in range(few):
                for i in range(own):
                    row = (part * few + freq) * own + i
                    place = core * few + freq
                    out_ref[i, part, place : place + 1, :] = sum_ref[core, row : row + 1, :]


def totals(got, freqs):
    chips, cores, lines, every = got.shape
    own = lines * cores // (2 * freqs)
    return pl.pallas_call(
        total_kernel,
        out_shape=jax.ShapeDtypeStruct((own, 2, freqs, every), jnp.float32),
        scratch_shapes=[pltpu.VMEM((cores, lines, every), jnp.float32)],
        name="total",
    )(got)


def body(snapshots, weights, block_delay):
    time_groups = lax.axis_size("tm")
    chips = lax.axis_size("chip")
    grid_rows, span = snapshots.shape
    blocks = span // HOP
    early_blocks = (span - REACH) // HOP + 1
    freqs = NF // time_groups
    targets = CORES * time_groups
    total_rows = grid_rows * chips * CORES
    table = dft_rows(time_groups)

    def exchange(array, axes):
        return lax.all_to_all(array, axes, split_axis=0, concat_axis=0, tiled=True)

    early, edge = block_spectra(
        snapshots, None, weights, block_delay, 0, early_blocks, targets, table, total_rows
    )
    rim = shifted(edge, "tm", -1)
    early_here = exchange(early, ("core", "tm"))
    (late,) = block_spectra(
        snapshots,
        rim,
        weights,
        block_delay,
        early_blocks,
        blocks - early_blocks,
        targets,
        table,
        total_rows,
    )
    late_here = exchange(late, ("core", "tm"))
    partial_csd = cross_power(early_here, late_here)
    partial_csd = partial_csd.reshape(chips * CORES, 4 * freqs, -1)
    got = exchange(partial_csd, ("chip", "core"))
    return totals(got.reshape(chips, CORES, 4 * freqs, -1), freqs)


def solution(mesh):
    rows, groups = mesh.devices.shape
    by_core = Mesh(mesh.devices.reshape(rows // CORES, CORES, groups), ("chip", "core", "tm"))
    row = ("chip", "core")
    return jax.shard_map(
        body,
        mesh=by_core,
        in_specs=(P(row, "tm"), P(row), P("tm")),
        out_specs=P(row, None, "tm", None),
        check_vma=False,
    )
```

```python
import jax
import jax.numpy as jnp
import numpy as np
from jax import lax
from jax.experimental import pallas as pl
from jax.experimental.pallas import tpu as pltpu
from jax.sharding import Mesh
from jax.sharding import PartitionSpec as P

NFFT = 256
NF = 128
HOP = 128
RIM = 192
REACH = 384
STRIP = 256
CORES = 2
VMEM = 56 * 1024 * 1024


def shifted(array, axis, by):
    count = lax.axis_size(axis)
    return lax.ppermute(array, axis, [(i, (i + by) % count) for i in range(count)])


def dft_rows(groups):
    time_index = np.arange(NFFT)
    angles = 2.0 * np.pi * (time_index[:, None] * np.arange(NF)[None, :] % NFFT) / NFFT
    window = np.sin(np.pi * time_index / NFFT) ** 2
    norm = np.sqrt(np.sum(window * window))
    table = np.stack([window[:, None] * np.cos(angles), -window[:, None] * np.sin(angles)])
    table = (table / norm).reshape(2, NFFT, groups, NF // groups)
    rows = table.transpose(2, 0, 3, 1).reshape(2 * NF, NFFT)
    rows = np.pad(rows, ((0, 0), (0, REACH - NFFT)))
    return jnp.asarray(rows, jnp.float32).astype(jnp.bfloat16)


def dft_kernel(first, total_rows, delay_ref, table_ref, weight_ref, snap_ref, *refs):
    late = first > 0
    shifted_ref, data_ref = refs[-2:]
    rim_ref, out_ref = refs[:2] if late else refs[1::-1]
    strip, span = snap_ref.shape
    targets, blocks, lines, _ = out_ref.shape

    @pl.when(pl.program_id(0) == 0)
    def _():
        table = table_ref[...].astype(jnp.float32)
        for block in range(blocks):
            moved = pltpu.roll(table, delay_ref[first + block], 1)
            shifted_ref[block] = moved.astype(jnp.bfloat16)

    data_ref[:, :span] = snap_ref[...].astype(jnp.bfloat16)
    if late:
        gap = jnp.zeros((strip, data_ref.shape[1] - span - RIM), jnp.bfloat16)
        data_ref[:, span:] = jnp.concatenate([rim_ref[...], gap], axis=1)
    else:
        rim_ref[...] = data_ref[:, :RIM]
    scale = jnp.sqrt(weight_ref[...] / total_rows)
    for block in range(blocks):
        spectrum = lax.dot_general(
            shifted_ref[block],
            data_ref[:, block * HOP : block * HOP + REACH],
            (((1,), (1,)), ((), ())),
            preferred_element_type=jnp.float32,
        )
        spectrum = (spectrum * scale).astype(jnp.bfloat16)
        out_ref[:, block] = spectrum.reshape(targets, lines, strip)


def block_spectra(snapshots, rim, weights, block_delay, first, count, targets, table, total_rows):
    rows, width = snapshots.shape
    begin = first * HOP
    span = width - begin if rim is not None else (count - 1) * HOP + REACH
    specs = [
        pl.BlockSpec(memory_space=pltpu.SMEM),
        pl.BlockSpec((2 * NF, REACH), lambda s: (0, 0)),
        pl.BlockSpec((1, STRIP), lambda s: (0, s)),
        pl.BlockSpec((STRIP, span), lambda s: (s, begin // span)),
    ]
    operands = [block_delay, table, weights.reshape(1, rows), snapshots]
    rim_spec = pl.BlockSpec((STRIP, RIM), lambda s: (s, 0))
    shape = (targets, count, 2 * NF // targets, rows)
    out_specs = [pl.BlockSpec(shape[:3] + (STRIP,), lambda s: (0, 0, 0, s))]
    out_shape = [jax.ShapeDtypeStruct(shape, jnp.bfloat16)]
    if rim is not None:
        specs.append(rim_spec)
        operands.append(rim)
    else:
        out_specs.append(rim_spec)
        out_shape.append(jax.ShapeDtypeStruct((rows, RIM), jnp.bfloat16))
    return pl.pallas_call(
        lambda *refs: dft_kernel(first, total_rows, *refs),
        grid=(rows // STRIP,),
        in_specs=specs,
        out_specs=out_specs,
        out_shape=out_shape,
        scratch_shapes=[
            pltpu.VMEM((count, 2 * NF, REACH), jnp.bfloat16),
            pltpu.VMEM((STRIP, (count - 1) * HOP + REACH), jnp.bfloat16),
        ],
        compiler_params=pltpu.CompilerParams(vmem_limit_bytes=VMEM if rim is None else VMEM // 2),
        cost_estimate=pl.CostEstimate(
            flops=4 * NF * REACH * rows * count,
            bytes_accessed=4 * rows * span + 4 * NF * rows * count,
            transcendentals=0,
        ),
        name="dft_late" if rim is not None else "dft_early",
    )(*operands)


def split_quads(mats):
    eights = [m.reshape(m.shape[0] // 8, 8, m.shape[1]) for m in mats]
    upper = lax.broadcasted_iota(jnp.int32, eights[0].shape, 1) < 4
    low, high = [], []
    for a, b in (eights[:2], eights[2:]):
        low.append(jnp.where(upper, a, pltpu.roll(b, 4, 1)))
        high.append(jnp.where(upper, pltpu.roll(a, 4, 1), b))
    return jnp.concatenate(low, axis=1), jnp.concatenate(high, axis=1)


def csd_kernel(core_ref, order_ref, early_ref, late_ref, own_ref, other_ref, sorted_ref):
    step = pl.program_id(0)
    lines, every, rows = sorted_ref.shape
    some = every // pl.num_programs(0)
    chunk = jnp.concatenate(
        [early_ref[...].reshape(-1, rows), late_ref[...].reshape(-1, rows)], axis=0
    )
    by_line = lax.dot_general(
        order_ref[...], chunk, (((1,), (0,)), ((), ())), preferred_element_type=jnp.float32
    )
    start = pl.multiple_of(step * some, some)
    sorted_ref[:, pl.ds(start, some), :] = by_line.astype(jnp.bfloat16).reshape(lines, some, rows)

    @pl.when(step == pl.num_programs(0) - 1)
    def _():
        freqs = lines // 2
        first_core = core_ref[0] == 0
        quads = ([], [])
        for freq in range(freqs):
            both = sorted_ref[2 * freq : 2 * freq + 2].reshape(2 * every, rows)
            power = lax.dot_general(
                both, both, (((1,), (1,)), ((), ())), preferred_element_type=jnp.float32
            )
            quads[0].append(power[:every, :every] + power[every:, every:])
            quads[1].append(power[:every, every:] - power[every:, :every])
            if freq % 4 == 3:
                for part, quad in enumerate(quads):
                    place = (part * freqs + freq - 3) * 4
                    low, high = split_quads(quad)
                    own_ref[:, place : place + 16, :] = jnp.where(first_core, low, high)
                    other = jnp.where(first_core, high, low)
                    other_ref[:, place : place + 16, :] = other.astype(jnp.bfloat16)
                quads = ([], [])


def cross_power(core, early, late):
    sources, early_blocks, lines, rows = early.shape
    late_blocks = late.shape[1]
    freqs = lines // 2
    blocks = early_blocks + late_blocks
    every = sources * blocks
    some = 2
    early_rows = np.arange(some * early_blocks * lines)
    late_rows = early_rows.size + np.arange(some * late_blocks * lines)
    source = np.concatenate(
        [
            early_rows.reshape(some, early_blocks, 2, freqs),
            late_rows.reshape(some, late_blocks, 2, freqs),
        ],
        axis=1,
    )
    source = source.transpose(3, 2, 0, 1).reshape(-1)
    order = jnp.asarray(np.eye(source.size)[source], jnp.bfloat16)
    shape = (every // 8, 8 * freqs, every)
    whole = pl.BlockSpec(shape, lambda s: (0, 0, 0))
    return pl.pallas_call(
        csd_kernel,
        grid=(sources // some,),
        in_specs=[
            pl.BlockSpec(memory_space=pltpu.SMEM),
            pl.BlockSpec(order.shape, lambda s: (0, 0)),
            pl.BlockSpec((some,) + early.shape[1:], lambda s: (s, 0, 0, 0)),
            pl.BlockSpec((some,) + late.shape[1:], lambda s: (s, 0, 0, 0)),
        ],
        out_specs=[whole, whole],
        out_shape=[
            jax.ShapeDtypeStruct(shape, jnp.float32),
            jax.ShapeDtypeStruct(shape, jnp.bfloat16),
        ],
        scratch_shapes=[pltpu.VMEM((lines, every, rows), jnp.bfloat16)],
        compiler_params=pltpu.CompilerParams(vmem_limit_bytes=32 * 1024 * 1024),
        name="csd",
    )(core, order, early, late)


def behind(array, other):
    anywhere = pl.BlockSpec(memory_space=pl.ANY)
    return pl.pallas_call(
        lambda array_ref, other_ref, out_ref: None,
        in_specs=[anywhere, anywhere],
        out_specs=anywhere,
        out_shape=jax.ShapeDtypeStruct(array.shape, array.dtype),
        input_output_aliases={0: 0},
        name="behind",
    )(array, other)


def total_kernel(got_ref, out_ref, sum_ref):
    own, parts, freqs, _ = out_ref.shape
    sum_ref[...] = jnp.sum(got_ref[...].astype(jnp.float32), axis=0)
    for part in range(parts):
        for freq in range(freqs):
            for i in range(own):
                row = (part * freqs + freq) * own + i
                out_ref[i, part, freq : freq + 1, :] = sum_ref[row : row + 1, :]


def totals(got, freqs):
    _, lines, every = got.shape
    return pl.pallas_call(
        total_kernel,
        out_shape=jax.ShapeDtypeStruct((lines // (2 * freqs), 2, freqs, every), jnp.float32),
        scratch_shapes=[pltpu.VMEM((lines, every), jnp.float32)],
        name="total",
    )(got)


def body(snapshots, weights, block_delay):
    time_groups = lax.axis_size("tm")
    chips = lax.axis_size("chip")
    grid_rows, span = snapshots.shape
    blocks = span // HOP
    early_blocks = (span - REACH) // HOP + 1
    freqs = NF // time_groups
    total_rows = grid_rows * chips * CORES
    table = dft_rows(time_groups)

    def exchange(array, axes):
        return lax.all_to_all(array, axes, split_axis=0, concat_axis=0, tiled=True)

    early, edge = block_spectra(
        snapshots, None, weights, block_delay, 0, early_blocks, time_groups, table, total_rows
    )
    rim = shifted(edge, "tm", -1)
    early_here = exchange(early, "tm")
    (late,) = block_spectra(
        snapshots,
        rim,
        weights,
        block_delay,
        early_blocks,
        blocks - early_blocks,
        time_groups,
        table,
        total_rows,
    )
    late_here = exchange(behind(late, early_here), "tm")
    core = lax.axis_index("core").astype(jnp.int32).reshape(1)
    own, other = cross_power(core, early_here, late_here)
    pair = (own + shifted(other, "core", 1).astype(jnp.float32)).astype(jnp.bfloat16)
    return totals(exchange(pair, "chip"), freqs)


def solution(mesh):
    rows, groups = mesh.devices.shape
    by_core = Mesh(mesh.devices.reshape(rows // CORES, CORES, groups), ("chip", "core", "tm"))
    row = ("chip", "core")
    return jax.shard_map(
        body,
        mesh=by_core,
        in_specs=(P(row, "tm"), P(row), P("tm")),
        out_specs=P(row, None, "tm", None),
        check_vma=False,
    )
```

```python
import jax
import jax.numpy as jnp
import numpy as np
from jax import lax
from jax.experimental import pallas as pl
from jax.experimental.pallas import tpu as pltpu
from jax.sharding import Mesh
from jax.sharding import PartitionSpec as P

NFFT = 256
NF = 128
HOP = 128
RIM = 192
REACH = 384
STRIP = 256
CORES = 2
SPLIT = (5, 10, 11, 6, 8)
WHOLE = (4, 13, 12, 7, 3, 14, 9, 2, 15, 1)
VMEM = 56 * 1024 * 1024


def shifted(array, axis, by):
    count = lax.axis_size(axis)
    return lax.ppermute(array, axis, [(i, (i + by) % count) for i in range(count)])


def dft_rows(groups):
    time_index = np.arange(NFFT)
    angles = 2.0 * np.pi * (time_index[:, None] * np.arange(NF)[None, :] % NFFT) / NFFT
    window = np.sin(np.pi * time_index / NFFT) ** 2
    norm = np.sqrt(np.sum(window * window))
    table = np.stack([window[:, None] * np.cos(angles), -window[:, None] * np.sin(angles)])
    table = (table / norm).reshape(2, NFFT, groups, NF // groups)
    rows = table.transpose(2, 0, 3, 1).reshape(2 * NF, NFFT)
    rows = np.pad(rows, ((0, 0), (0, REACH - NFFT)))
    return jnp.asarray(rows, jnp.float32).astype(jnp.bfloat16)


def relative(groups, here, r):
    return (here // 2 + r // 2) % (groups // 2) * 2 + (here + r) % 2


def sent(array, r):
    groups = lax.axis_size("tm")
    return lax.ppermute(array, "tm", [(i, relative(groups, i, r)) for i in range(groups)])


def dft_kernel(first, blocks, total_rows, targets, delay_ref, here_ref, table_ref, weight_ref, snap_ref, *refs):
    late = first > 0
    table_sorted_ref, shifted_ref, data_ref = refs[-3:]
    if late:
        rim_ref, out_refs = refs[0], refs[-3 - targets : -3]
    else:
        rim_ref, out_refs = refs[-4], refs[-4 - targets : -4]
    strip, span = snap_ref.shape
    lines = table_ref.shape[0] // targets

    @pl.when(pl.program_id(0) == 0)
    def _():
        for r in range(targets):
            start = pl.multiple_of(relative(targets, here_ref[0], r) * lines, lines)
            rows = table_ref[pl.ds(start, lines), :].astype(jnp.float32)
            table_sorted_ref[r * lines : (r + 1) * lines, :] = rows
        for block in range(blocks):
            moved = pltpu.roll(table_sorted_ref[...], delay_ref[first + block], 1)
            shifted_ref[block] = moved.astype(jnp.bfloat16)

    data_ref[:, :span] = snap_ref[...].astype(jnp.bfloat16)
    if late:
        gap = jnp.zeros((strip, data_ref.shape[1] - span - RIM), jnp.bfloat16)
        data_ref[:, span:] = jnp.concatenate([rim_ref[...], gap], axis=1)
    else:
        rim_ref[...] = data_ref[:, :RIM]
    scale = jnp.sqrt(weight_ref[...] / total_rows)
    for block in range(blocks):
        spectrum = lax.dot_general(
            shifted_ref[block],
            data_ref[:, block * HOP : block * HOP + REACH],
            (((1,), (1,)), ((), ())),
            preferred_element_type=jnp.float32,
        )
        spectrum = (spectrum * scale).astype(jnp.bfloat16)
        for r in range(targets):
            out_refs[r][block] = spectrum[r * lines : (r + 1) * lines]


def block_spectra(snapshots, rim, weights, block_delay, here, first, count, blocks, table, total_rows, begun):
    rows, width = snapshots.shape
    targets = lax.axis_size("tm")
    lines = 2 * NF // targets
    begin = first * HOP
    late = rim is not None
    span = width - begin if late else (count - 1) * HOP + REACH
    specs = [
        pl.BlockSpec(memory_space=pltpu.SMEM),
        pl.BlockSpec(memory_space=pltpu.SMEM),
        pl.BlockSpec((2 * NF, REACH), lambda s: (0, 0)),
        pl.BlockSpec((1, STRIP), lambda s: (0, s)),
        pl.BlockSpec((STRIP, span), lambda s: (s, begin // span)),
    ]
    operands = [block_delay, here, table, weights.reshape(1, rows), snapshots]
    rim_spec = pl.BlockSpec((STRIP, RIM), lambda s: (s, 0))
    aliases = {}
    out_specs, out_shape = [], []
    if late:
        specs.append(rim_spec)
        operands.append(rim)
    for r in range(targets):
        full = r not in SPLIT
        part = first // count if full else 0
        out_specs.append(pl.BlockSpec((count, lines, STRIP), lambda s, part=part: (part, 0, s)))
        shape = (blocks if full else count, lines, rows)
        out_shape.append(jax.ShapeDtypeStruct(shape, jnp.bfloat16))
        if late and full:
            aliases[len(operands)] = r
            specs.append(pl.BlockSpec(memory_space=pl.ANY))
            operands.append(begun[r])
    if not late:
        out_specs.append(rim_spec)
        out_shape.append(jax.ShapeDtypeStruct((rows, RIM), jnp.bfloat16))
    return pl.pallas_call(
        lambda *refs: dft_kernel(first, count, total_rows, targets, *refs),
        grid=(rows // STRIP,),
        in_specs=specs,
        out_specs=out_specs,
        out_shape=out_shape,
        input_output_aliases=aliases,
        scratch_shapes=[
            pltpu.VMEM((2 * NF, REACH), jnp.float32),
            pltpu.VMEM((count, 2 * NF, REACH), jnp.bfloat16),
            pltpu.VMEM((STRIP, (count - 1) * HOP + REACH), jnp.bfloat16),
        ],
        compiler_params=pltpu.CompilerParams(vmem_limit_bytes=VMEM),
        cost_estimate=pl.CostEstimate(
            flops=4 * NF * REACH * rows * count,
            bytes_accessed=4 * rows * span + 4 * NF * rows * count,
            transcendentals=0,
        ),
        name="dft_late" if late else "dft_early",
    )(*operands)


def split_quads(mats):
    eights = [m.reshape(m.shape[0] // 8, 8, m.shape[1]) for m in mats]
    upper = lax.broadcasted_iota(jnp.int32, eights[0].shape, 1) < 4
    low, high = [], []
    for a, b in (eights[:2], eights[2:]):
        low.append(jnp.where(upper, a, pltpu.roll(b, 4, 1)))
        high.append(jnp.where(upper, pltpu.roll(a, 4, 1), b))
    return jnp.concatenate(low, axis=1), jnp.concatenate(high, axis=1)


def csd_kernel(layout, core_ref, here_ref, order_ref, *refs):
    own_ref, other_ref, sorted_ref = refs[-3:]
    lines, every, rows = sorted_ref.shape
    some = 2 * every // len(layout)
    for shift in range(0, len(layout), 2):
        pieces = [refs[k][...].reshape(-1, rows) for r in (shift, shift + 1) for k in layout[r]]
        by_line = lax.dot_general(
            order_ref[here_ref[0] % 2],
            jnp.concatenate(pieces, axis=0),
            (((1,), (0,)), ((), ())),
            preferred_element_type=jnp.float32,
        )
        origin = relative(len(layout), here_ref[0], len(layout) - shift) // 2
        start = pl.multiple_of(origin * some, some)
        sorted_ref[:, pl.ds(start, some), :] = by_line.astype(jnp.bfloat16).reshape(lines, some, rows)
    freqs = lines // 2
    first_core = core_ref[0] == 0
    quads = ([], [])
    for freq in range(freqs):
        both = sorted_ref[2 * freq : 2 * freq + 2].reshape(2 * every, rows)
        power = lax.dot_general(
            both, both, (((1,), (1,)), ((), ())), preferred_element_type=jnp.float32
        )
        quads[0].append(power[:every, :every] + power[every:, every:])
        quads[1].append(power[:every, every:] - power[every:, :every])
        if freq % 4 == 3:
            for part, quad in enumerate(quads):
                place = (part * freqs + freq - 3) * 4
                low, high = split_quads(quad)
                own_ref[:, place : place + 16, :] = jnp.where(first_core, low, high)
                other = jnp.where(first_core, high, low)
                other_ref[:, place : place + 16, :] = other.astype(jnp.bfloat16)
            quads = ([], [])


def cross_power(core, here, received, blocks):
    targets = len(received)
    _, lines, rows = received[0][0].shape
    freqs = lines // 2
    every = targets * blocks
    orders = []
    for flip in range(2):
        rows_in = np.arange(2 * blocks * lines).reshape(2, blocks, 2, freqs)
        rows_in = rows_in[::-1] if flip else rows_in
        orders.append(np.eye(rows_in.size)[rows_in.transpose(3, 2, 0, 1).reshape(-1)])
    layout, pieces = [], []
    for parts in received:
        layout.append(range(len(pieces), len(pieces) + len(parts)))
        pieces.extend(parts)
    shape = (every // 8, 8 * freqs, every)
    small = pl.BlockSpec(memory_space=pltpu.SMEM)
    whole = pl.BlockSpec(memory_space=pltpu.VMEM)
    return pl.pallas_call(
        lambda *refs: csd_kernel(layout, *refs),
        in_specs=[small, small, whole] + [whole] * len(pieces),
        out_specs=[whole, whole],
        out_shape=[
            jax.ShapeDtypeStruct(shape, jnp.float32),
            jax.ShapeDtypeStruct(shape, jnp.bfloat16),
        ],
        scratch_shapes=[pltpu.VMEM((lines, every, rows), jnp.bfloat16)],
        compiler_params=pltpu.CompilerParams(vmem_limit_bytes=32 * 1024 * 1024),
        name="csd",
    )(core, here, jnp.asarray(np.stack(orders), jnp.bfloat16), *pieces)


def total_kernel(got_ref, out_ref, sum_ref):
    own, parts, freqs, _ = out_ref.shape
    sum_ref[...] = jnp.sum(got_ref[...].astype(jnp.float32), axis=0)
    for part in range(parts):
        for freq in range(freqs):
            for i in range(own):
                row = (part * freqs + freq) * own + i
                out_ref[i, part, freq : freq + 1, :] = sum_ref[row : row + 1, :]


def totals(got, freqs):
    _, lines, every = got.shape
    return pl.pallas_call(
        total_kernel,
        out_shape=jax.ShapeDtypeStruct((lines // (2 * freqs), 2, freqs, every), jnp.float32),
        scratch_shapes=[pltpu.VMEM((lines, every), jnp.float32)],
        name="total",
    )(got)


def body(snapshots, weights, block_delay):
    groups = lax.axis_size("tm")
    chips = lax.axis_size("chip")
    grid_rows, span = snapshots.shape
    blocks = span // HOP
    early_blocks = (span - REACH) // HOP + 1
    late_blocks = blocks - early_blocks
    total_rows = grid_rows * chips * CORES
    here = lax.axis_index("tm").astype(jnp.int32).reshape(1)

    def spectra(rim, first, count, begun):
        table = dft_rows(groups)
        return block_spectra(
            snapshots, rim, weights, block_delay, here, first, count, blocks, table, total_rows, begun
        )

    *early, edge = spectra(None, 0, early_blocks, None)
    rim = shifted(edge, "tm", -1)
    received = [None] * groups
    for r in SPLIT:
        received[r] = [sent(early[r], r)]
    late = spectra(rim, early_blocks, late_blocks, early)
    received[0] = [late[0]]
    for r in WHOLE:
        received[r] = [sent(late[r], r)]
    for r in SPLIT:
        received[r].append(sent(late[r], r))
    core = lax.axis_index("core").astype(jnp.int32).reshape(1)
    own, other = cross_power(core, here, received, blocks)
    pair = (own + shifted(other, "core", 1).astype(jnp.float32)).astype(jnp.bfloat16)
    got = lax.all_to_all(pair, "chip", split_axis=0, concat_axis=0, tiled=True)
    return totals(got, NF // groups)


def solution(mesh):
    rows, groups = mesh.devices.shape
    by_core = Mesh(mesh.devices.reshape(rows // CORES, CORES, groups), ("chip", "core", "tm"))
    row = ("chip", "core")
    return jax.shard_map(
        body,
        mesh=by_core,
        in_specs=(P(row, "tm"), P(row), P("tm")),
        out_specs=P(row, None, "tm", None),
        check_vma=False,
    )
```

```python
import jax
import jax.numpy as jnp
import numpy as np
from jax import lax
from jax.experimental import pallas as pl
from jax.experimental.pallas import tpu as pltpu
from jax.sharding import Mesh
from jax.sharding import PartitionSpec as P

NFFT = 256
NF = 128
HOP = 128
RIM = 192
REACH = 384
STRIP = 256
CORES = 2
VMEM = 24 * 1024 * 1024


def shifted(array, axis, by):
    count = lax.axis_size(axis)
    return lax.ppermute(array, axis, [(i, (i + by) % count) for i in range(count)])


def dft_rows(groups):
    time_index = np.arange(NFFT)
    angles = 2.0 * np.pi * (time_index[:, None] * np.arange(NF)[None, :] % NFFT) / NFFT
    window = np.sin(np.pi * time_index / NFFT) ** 2
    norm = np.sqrt(np.sum(window * window))
    table = np.stack([window[:, None] * np.cos(angles), -window[:, None] * np.sin(angles)])
    table = (table / norm).reshape(2, NFFT, groups, NF // groups)
    rows = table.transpose(2, 0, 3, 1).reshape(2 * NF, NFFT)
    rows = np.pad(rows, ((0, 0), (0, REACH - NFFT)))
    return jnp.asarray(rows, jnp.float32).astype(jnp.bfloat16)


def early_kernel(total_rows, delay_ref, table_ref, weight_ref, snap_ref, out_ref, tail_ref, late_table_ref, scale_ref, shifted_ref, data_ref):
    strip, _ = snap_ref.shape
    targets, early, lines, _ = out_ref.shape

    @pl.when(pl.program_id(0) == 0)
    def _():
        table = table_ref[...].astype(jnp.float32)
        for block in range(delay_ref.shape[0]):
            moved = pltpu.roll(table, delay_ref[block], 1).astype(jnp.bfloat16)
            if block < early:
                shifted_ref[block] = moved
            else:
                late_table_ref[block - early] = moved

    data_ref[...] = snap_ref[...].astype(jnp.bfloat16)
    tail_ref[...] = data_ref[:, early * HOP :]
    scale = jnp.sqrt(weight_ref[...] / total_rows)
    scale_ref[...] = scale
    for block in range(early):
        spectrum = lax.dot_general(
            shifted_ref[block],
            data_ref[:, block * HOP : block * HOP + REACH],
            (((1,), (1,)), ((), ())),
            preferred_element_type=jnp.float32,
        )
        spectrum = (spectrum * scale).astype(jnp.bfloat16)
        out_ref[:, block] = spectrum.reshape(targets, lines, strip)


def early_spectra(snapshots, weights, block_delay, table, targets, total_rows):
    rows, span = snapshots.shape
    blocks = span // HOP
    early = (span - REACH) // HOP + 1
    lines = 2 * NF // targets
    tail = span - early * HOP
    return pl.pallas_call(
        lambda *refs: early_kernel(total_rows, *refs),
        grid=(rows // STRIP,),
        in_specs=[
            pl.BlockSpec(memory_space=pltpu.SMEM),
            pl.BlockSpec(table.shape, lambda s: (0, 0)),
            pl.BlockSpec((1, STRIP), lambda s: (0, s)),
            pl.BlockSpec((STRIP, span), lambda s: (s, 0)),
        ],
        out_specs=[
            pl.BlockSpec((targets, early, lines, STRIP), lambda s: (0, 0, 0, s)),
            pl.BlockSpec((STRIP, tail), lambda s: (s, 0)),
            pl.BlockSpec((blocks - early,) + table.shape, lambda s: (0, 0, 0)),
            pl.BlockSpec((1, STRIP), lambda s: (0, s)),
        ],
        out_shape=[
            jax.ShapeDtypeStruct((targets, blocks, lines, rows), jnp.bfloat16),
            jax.ShapeDtypeStruct((rows, tail), jnp.bfloat16),
            jax.ShapeDtypeStruct((blocks - early,) + table.shape, jnp.bfloat16),
            jax.ShapeDtypeStruct((1, rows), jnp.float32),
        ],
        scratch_shapes=[
            pltpu.VMEM((early,) + table.shape, jnp.bfloat16),
            pltpu.VMEM((STRIP, span), jnp.bfloat16),
        ],
        compiler_params=pltpu.CompilerParams(vmem_limit_bytes=VMEM),
        cost_estimate=pl.CostEstimate(
            flops=4 * NF * REACH * rows * early,
            bytes_accessed=4 * rows * span + 4 * NF * rows * early,
            transcendentals=0,
        ),
        name="dft_early",
    )(block_delay, table, weights.reshape(1, rows), snapshots)


def late_kernel(table_ref, scale_ref, tail_ref, rim_ref, begun_ref, out_ref, data_ref):
    strip, tail = tail_ref.shape
    targets, late, lines, _ = out_ref.shape
    gap = jnp.zeros((strip, data_ref.shape[1] - tail - RIM), jnp.bfloat16)
    data_ref[:, :tail] = tail_ref[...]
    data_ref[:, tail:] = jnp.concatenate([rim_ref[...], gap], axis=1)
    for block in range(late):
        spectrum = lax.dot_general(
            table_ref[block],
            data_ref[:, block * HOP : block * HOP + REACH],
            (((1,), (1,)), ((), ())),
            preferred_element_type=jnp.float32,
        )
        spectrum = (spectrum * scale_ref[...]).astype(jnp.bfloat16)
        out_ref[:, block] = spectrum.reshape(targets, lines, strip)


def late_spectra(begun, tail, table, scale, rim):
    targets, blocks, lines, rows = begun.shape
    late = table.shape[0]
    return pl.pallas_call(
        late_kernel,
        grid=(rows // STRIP,),
        in_specs=[
            pl.BlockSpec(table.shape, lambda s: (0, 0, 0)),
            pl.BlockSpec((1, STRIP), lambda s: (0, s)),
            pl.BlockSpec((STRIP, tail.shape[1]), lambda s: (s, 0)),
            pl.BlockSpec((STRIP, RIM), lambda s: (s, 0)),
            pl.BlockSpec(memory_space=pl.ANY),
        ],
        out_specs=pl.BlockSpec(
            (targets, late, lines, STRIP), lambda s: (0, blocks // late - 1, 0, s)
        ),
        out_shape=jax.ShapeDtypeStruct(begun.shape, begun.dtype),
        input_output_aliases={4: 0},
        scratch_shapes=[pltpu.VMEM((STRIP, (late - 1) * HOP + REACH), jnp.bfloat16)],
        compiler_params=pltpu.CompilerParams(vmem_limit_bytes=VMEM),
        cost_estimate=pl.CostEstimate(
            flops=4 * NF * REACH * rows * late,
            bytes_accessed=4 * NF * rows * late,
            transcendentals=0,
        ),
        name="dft_late",
    )(table, scale, tail, rim, begun)


def split_quads(mats):
    eights = [m.reshape(m.shape[0] // 8, 8, m.shape[1]) for m in mats]
    upper = lax.broadcasted_iota(jnp.int32, eights[0].shape, 1) < 4
    low, high = [], []
    for a, b in (eights[:2], eights[2:]):
        low.append(jnp.where(upper, a, pltpu.roll(b, 4, 1)))
        high.append(jnp.where(upper, pltpu.roll(a, 4, 1), b))
    return jnp.concatenate(low, axis=1), jnp.concatenate(high, axis=1)


def csd_kernel(core_ref, got_ref, own_ref, other_ref, sorted_ref):
    lines, every, rows = sorted_ref.shape
    sources, blocks, _, _ = got_ref.shape
    freqs = lines // 2
    some = 2 * blocks
    row = lax.broadcasted_iota(jnp.int32, (some * lines, some * lines), 0)
    column = lax.broadcasted_iota(jnp.int32, (some * lines, some * lines), 1)
    part = (row // some) % 2
    freq = row // (2 * some)
    order = ((row % some) * lines + part * freqs + freq == column).astype(jnp.bfloat16)
    for step in range(sources // 2):
        by_line = lax.dot_general(
            order,
            got_ref[2 * step : 2 * step + 2].reshape(some * lines, rows),
            (((1,), (0,)), ((), ())),
            preferred_element_type=jnp.float32,
        )
        by_line = by_line.astype(jnp.bfloat16).reshape(lines, some, rows)
        sorted_ref[:, step * some : (step + 1) * some, :] = by_line
    first_core = core_ref[0] == 0
    quads = ([], [])
    for freq in range(freqs):
        both = sorted_ref[2 * freq : 2 * freq + 2].reshape(2 * every, rows)
        power = lax.dot_general(
            both, both, (((1,), (1,)), ((), ())), preferred_element_type=jnp.float32
        )
        quads[0].append(power[:every, :every] + power[every:, every:])
        quads[1].append(power[:every, every:] - power[every:, :every])
        if freq % 4 == 3:
            for part, quad in enumerate(quads):
                place = (part * freqs + freq - 3) * 4
                low, high = split_quads(quad)
                own_ref[:, place : place + 16, :] = jnp.where(first_core, low, high)
                other = jnp.where(first_core, high, low)
                other_ref[:, place : place + 16, :] = other.astype(jnp.bfloat16)
            quads = ([], [])


def cross_power(core, got):
    sources, blocks, lines, rows = got.shape
    every = sources * blocks
    shape = (every // 8, 4 * lines, every)
    whole = pl.BlockSpec(memory_space=pltpu.VMEM)
    return pl.pallas_call(
        csd_kernel,
        in_specs=[pl.BlockSpec(memory_space=pltpu.SMEM), whole],
        out_specs=[whole, whole],
        out_shape=[
            jax.ShapeDtypeStruct(shape, jnp.float32),
            jax.ShapeDtypeStruct(shape, jnp.bfloat16),
        ],
        scratch_shapes=[pltpu.VMEM((lines, every, rows), jnp.bfloat16)],
        compiler_params=pltpu.CompilerParams(vmem_limit_bytes=VMEM),
        name="csd",
    )(core, got)


def total_kernel(got_ref, out_ref, sum_ref):
    own, parts, freqs, _ = out_ref.shape
    sum_ref[...] = jnp.sum(got_ref[...].astype(jnp.float32), axis=0)
    for part in range(parts):
        for freq in range(freqs):
            for i in range(own):
                row = (part * freqs + freq) * own + i
                out_ref[i, part, freq : freq + 1, :] = sum_ref[row : row + 1, :]


def totals(got, freqs):
    _, lines, every = got.shape
    return pl.pallas_call(
        total_kernel,
        out_shape=jax.ShapeDtypeStruct((lines // (2 * freqs), 2, freqs, every), jnp.float32),
        scratch_shapes=[pltpu.VMEM((lines, every), jnp.float32)],
        name="total",
    )(got)


def body(snapshots, weights, block_delay):
    groups = lax.axis_size("tm")
    total_rows = snapshots.shape[0] * lax.axis_size("chip") * CORES

    def exchange(array, axis):
        return lax.all_to_all(array, axis, split_axis=0, concat_axis=0, tiled=True)

    rim = shifted(snapshots[:, :RIM].astype(jnp.bfloat16), "tm", -1)
    begun = early_spectra(snapshots, weights, block_delay, dft_rows(groups), groups, total_rows)
    spectra = late_spectra(*begun, rim)
    core = lax.axis_index("core").astype(jnp.int32).reshape(1)
    own, other = cross_power(core, exchange(spectra, "tm"))
    pair = (own + shifted(other, "core", 1).astype(jnp.float32)).astype(jnp.bfloat16)
    return totals(exchange(pair, "chip"), NF // groups)


def solution(mesh):
    rows, groups = mesh.devices.shape
    by_core = Mesh(mesh.devices.reshape(rows // CORES, CORES, groups), ("chip", "core", "tm"))
    row = ("chip", "core")
    return jax.shard_map(
        body,
        mesh=by_core,
        in_specs=(P(row, "tm"), P(row), P("tm")),
        out_specs=P(row, None, "tm", None),
        check_vma=False,
    )
```

```python
import jax
import jax.numpy as jnp
import numpy as np
from jax import lax
from jax.experimental import pallas as pl
from jax.experimental.pallas import tpu as pltpu
from jax.sharding import Mesh
from jax.sharding import PartitionSpec as P

NFFT = 256
NF = 128
HOP = 128
RIM = 192
REACH = 384
STRIP = 256
CORES = 2
VMEM = 24 * 1024 * 1024


def shifted(array, axis, by):
    count = lax.axis_size(axis)
    return lax.ppermute(array, axis, [(i, (i + by) % count) for i in range(count)])


def dft_rows(groups):
    time_index = np.arange(NFFT)
    angles = 2.0 * np.pi * (time_index[:, None] * np.arange(NF)[None, :] % NFFT) / NFFT
    window = np.sin(np.pi * time_index / NFFT) ** 2
    norm = np.sqrt(np.sum(window * window))
    table = np.stack([window[:, None] * np.cos(angles), -window[:, None] * np.sin(angles)])
    table = (table / norm).reshape(2, NFFT, groups, CORES, NF // groups // CORES)
    rows = table.transpose(3, 2, 0, 4, 1).reshape(2 * NF, NFFT)
    rows = np.pad(rows, ((0, 0), (0, REACH - NFFT)))
    return jnp.asarray(rows, jnp.float32).astype(jnp.bfloat16)


def fill_pairs(out_ref, table_ref, data_ref, scale):
    targets, pairs, _, strip = out_ref.shape
    for pair in range(pairs):
        two = []
        for block in (2 * pair, 2 * pair + 1):
            spectrum = lax.dot_general(
                table_ref[block],
                data_ref[:, block * HOP : block * HOP + REACH],
                (((1,), (1,)), ((), ())),
                preferred_element_type=jnp.float32,
            )
            two.append((spectrum * scale).reshape(targets, -1, strip))
        out_ref[:, pair] = jnp.concatenate(two, axis=1).astype(jnp.bfloat16)


def early_kernel(total_rows, delay_ref, table_ref, weight_ref, snap_ref, out_ref, tail_ref, late_table_ref, scale_ref, shifted_ref, data_ref):
    early = 2 * out_ref.shape[1]

    @pl.when(pl.program_id(0) == 0)
    def _():
        table = table_ref[...].astype(jnp.float32)
        for block in range(delay_ref.shape[0]):
            moved = pltpu.roll(table, delay_ref[block], 1).astype(jnp.bfloat16)
            if block < early:
                shifted_ref[block] = moved
            else:
                late_table_ref[block - early] = moved

    data_ref[...] = snap_ref[...].astype(jnp.bfloat16)
    tail_ref[...] = data_ref[:, early * HOP :]
    scale = jnp.sqrt(weight_ref[...] / total_rows)
    scale_ref[...] = scale
    fill_pairs(out_ref, shifted_ref, data_ref, scale)


def early_spectra(snapshots, weights, block_delay, table, targets, total_rows):
    rows, span = snapshots.shape
    blocks = span // HOP
    early = (span - REACH) // HOP + 1
    lines = 4 * NF // targets
    tail = span - early * HOP
    return pl.pallas_call(
        lambda *refs: early_kernel(total_rows, *refs),
        grid=(rows // STRIP,),
        in_specs=[
            pl.BlockSpec(memory_space=pltpu.SMEM),
            pl.BlockSpec(table.shape, lambda s: (0, 0)),
            pl.BlockSpec((1, STRIP), lambda s: (0, s)),
            pl.BlockSpec((STRIP, span), lambda s: (s, 0)),
        ],
        out_specs=[
            pl.BlockSpec((targets, early // 2, lines, STRIP), lambda s: (0, 0, 0, s)),
            pl.BlockSpec((STRIP, tail), lambda s: (s, 0)),
            pl.BlockSpec((blocks - early,) + table.shape, lambda s: (0, 0, 0)),
            pl.BlockSpec((1, STRIP), lambda s: (0, s)),
        ],
        out_shape=[
            jax.ShapeDtypeStruct((targets, blocks // 2, lines, rows), jnp.bfloat16),
            jax.ShapeDtypeStruct((rows, tail), jnp.bfloat16),
            jax.ShapeDtypeStruct((blocks - early,) + table.shape, jnp.bfloat16),
            jax.ShapeDtypeStruct((1, rows), jnp.float32),
        ],
        scratch_shapes=[
            pltpu.VMEM((early,) + table.shape, jnp.bfloat16),
            pltpu.VMEM((STRIP, span), jnp.bfloat16),
        ],
        compiler_params=pltpu.CompilerParams(vmem_limit_bytes=VMEM),
        cost_estimate=pl.CostEstimate(
            flops=4 * NF * REACH * rows * early,
            bytes_accessed=4 * rows * span + 4 * NF * rows * early,
            transcendentals=0,
        ),
        name="dft_early",
    )(block_delay, table, weights.reshape(1, rows), snapshots)


def late_kernel(table_ref, scale_ref, tail_ref, rim_ref, begun_ref, out_ref, data_ref):
    strip, tail = tail_ref.shape
    gap = jnp.zeros((strip, data_ref.shape[1] - tail - RIM), jnp.bfloat16)
    data_ref[:, :tail] = tail_ref[...]
    data_ref[:, tail:] = jnp.concatenate([rim_ref[...], gap], axis=1)
    fill_pairs(out_ref, table_ref, data_ref, scale_ref[...])


def late_spectra(begun, tail, table, scale, rim):
    targets, pairs, lines, rows = begun.shape
    late = table.shape[0]
    return pl.pallas_call(
        late_kernel,
        grid=(rows // STRIP,),
        in_specs=[
            pl.BlockSpec(table.shape, lambda s: (0, 0, 0)),
            pl.BlockSpec((1, STRIP), lambda s: (0, s)),
            pl.BlockSpec((STRIP, tail.shape[1]), lambda s: (s, 0)),
            pl.BlockSpec((STRIP, RIM), lambda s: (s, 0)),
            pl.BlockSpec(memory_space=pl.ANY),
        ],
        out_specs=pl.BlockSpec(
            (targets, late // 2, lines, STRIP), lambda s: (0, 2 * pairs // late - 1, 0, s)
        ),
        out_shape=jax.ShapeDtypeStruct(begun.shape, begun.dtype),
        input_output_aliases={4: 0},
        scratch_shapes=[pltpu.VMEM((STRIP, (late - 1) * HOP + REACH), jnp.bfloat16)],
        compiler_params=pltpu.CompilerParams(vmem_limit_bytes=VMEM),
        cost_estimate=pl.CostEstimate(
            flops=4 * NF * REACH * rows * late,
            bytes_accessed=4 * NF * rows * late,
            transcendentals=0,
        ),
        name="dft_late",
    )(table, scale, tail, rim, begun)


def split_quads(mats):
    eights = [m.reshape(m.shape[0] // 8, 8, m.shape[1]) for m in mats]
    upper = lax.broadcasted_iota(jnp.int32, eights[0].shape, 1) < 4
    low, high = [], []
    for a, b in (eights[:2], eights[2:]):
        low.append(jnp.where(upper, a, pltpu.roll(b, 4, 1)))
        high.append(jnp.where(upper, pltpu.roll(a, 4, 1), b))
    return jnp.concatenate(low, axis=1), jnp.concatenate(high, axis=1)


def csd_kernel(got_ref, out_ref, sorted_ref):
    cores, lines, every, rows = sorted_ref.shape
    freqs = lines // 2
    sources = got_ref.shape[0] // cores
    step = 4
    some = step * every // sources
    row = lax.broadcasted_iota(jnp.int32, (some * lines, some * lines), 0)
    column = lax.broadcasted_iota(jnp.int32, (some * lines, some * lines), 1)
    part = (row // some) % 2
    freq = row // (2 * some)
    order = ((row % some) * lines + part * freqs + freq == column).astype(jnp.bfloat16)
    for core in range(cores):
        for k in range(sources // step):
            first = core * sources + k * step
            by_line = lax.dot_general(
                order,
                got_ref[first : first + step].reshape(some * lines, rows),
                (((1,), (0,)), ((), ())),
                preferred_element_type=jnp.float32,
            )
            by_line = by_line.astype(jnp.bfloat16).reshape(lines, some, rows)
            sorted_ref[core, :, k * some : (k + 1) * some, :] = by_line
    real, imag = [], []
    for freq in range(freqs):
        power = 0.0
        for core in range(cores):
            both = sorted_ref[core, 2 * freq : 2 * freq + 2].reshape(2 * every, rows)
            power += lax.dot_general(
                both, both, (((1,), (1,)), ((), ())), preferred_element_type=jnp.float32
            )
        real.append(power[:every, :every] + power[every:, every:])
        imag.append(power[:every, every:] - power[every:, :every])
    for place, quad in ((0, real), (16, imag)):
        low, high = split_quads(quad)
        out_ref[:, 0, place : place + 16, :] = low.astype(jnp.bfloat16)
        out_ref[:, 1, place : place + 16, :] = high.astype(jnp.bfloat16)


def cross_power(got):
    sources, pairs, lines, rows = got.shape
    every = sources // CORES * 2 * pairs
    shape = (every // 8, 2, 2 * lines, every)
    whole = pl.BlockSpec(memory_space=pltpu.VMEM)
    return pl.pallas_call(
        csd_kernel,
        in_specs=[whole],
        out_specs=whole,
        out_shape=jax.ShapeDtypeStruct(shape, jnp.bfloat16),
        scratch_shapes=[pltpu.VMEM((CORES, lines // 2, every, rows), jnp.bfloat16)],
        compiler_params=pltpu.CompilerParams(vmem_limit_bytes=VMEM),
        name="csd",
    )(got)


def total_kernel(got_ref, out_ref, sum_ref):
    own, parts, freqs, _ = out_ref.shape
    sum_ref[...] = jnp.sum(got_ref[...].astype(jnp.float32), axis=0)
    few = freqs // CORES
    for core in range(CORES):
        for part in range(parts):
            for freq in range(few):
                for i in range(own):
                    row = (part * few + freq) * own + i
                    place = core * few + freq
                    out_ref[i, part, place : place + 1, :] = sum_ref[core, row : row + 1, :]


def totals(got, freqs):
    _, cores, lines, every = got.shape
    whole = pl.BlockSpec(memory_space=pltpu.VMEM)
    return pl.pallas_call(
        total_kernel,
        in_specs=[whole],
        out_specs=whole,
        out_shape=jax.ShapeDtypeStruct((lines * cores // (2 * freqs), 2, freqs, every), jnp.float32),
        scratch_shapes=[pltpu.VMEM((cores, lines, every), jnp.float32)],
        compiler_params=pltpu.CompilerParams(vmem_limit_bytes=VMEM),
        name="total",
    )(got)


def body(snapshots, weights, block_delay):
    groups = lax.axis_size("tm")
    chips = lax.axis_size("chip")
    targets = CORES * groups
    total_rows = snapshots.shape[0] * chips * CORES

    def exchange(array, axes):
        return lax.all_to_all(array, axes, split_axis=0, concat_axis=0, tiled=True)

    rim = shifted(snapshots[:, :RIM].astype(jnp.bfloat16), "tm", -1)
    begun = early_spectra(snapshots, weights, block_delay, dft_rows(groups), targets, total_rows)
    spectra = late_spectra(*begun, rim)
    partial_csd = cross_power(exchange(spectra, ("core", "tm")))
    lines, every = partial_csd.shape[2:]
    got = exchange(partial_csd.reshape(chips * CORES, lines, every), ("chip", "core"))
    return totals(got.reshape(chips, CORES, lines, every), NF // groups)


def solution(mesh):
    rows, groups = mesh.devices.shape
    by_core = Mesh(mesh.devices.reshape(rows // CORES, CORES, groups), ("chip", "core", "tm"))
    row = ("chip", "core")
    return jax.shard_map(
        body,
        mesh=by_core,
        in_specs=(P(row, "tm"), P(row), P("tm")),
        out_specs=P(row, None, "tm", None),
        check_vma=False,
    )
```

```python
import jax
import jax.numpy as jnp
import numpy as np
from jax import lax
from jax.experimental import pallas as pl
from jax.experimental.pallas import tpu as pltpu
from jax.sharding import Mesh
from jax.sharding import PartitionSpec as P

NFFT = 256
NF = 128
HOP = 128
RIM = 192
REACH = 384
STRIP = 256
CORES = 2
LANES = 128
VMEM = 24 * 1024 * 1024
LARGE = 56 * 1024 * 1024


def shifted(array, axis, by):
    count = lax.axis_size(axis)
    return lax.ppermute(array, axis, [(i, (i + by) % count) for i in range(count)])


def dft_rows(groups):
    time_index = np.arange(NFFT)
    angles = 2.0 * np.pi * (time_index[:, None] * np.arange(NF)[None, :] % NFFT) / NFFT
    window = np.sin(np.pi * time_index / NFFT) ** 2
    norm = np.sqrt(np.sum(window * window))
    table = np.stack([window[:, None] * np.cos(angles), -window[:, None] * np.sin(angles)])
    table = (table / norm).reshape(2, NFFT, groups, CORES, NF // groups // CORES)
    rows = table.transpose(3, 2, 0, 4, 1).reshape(2 * NF, NFFT)
    rows = np.pad(rows, ((0, 0), (0, REACH - NFFT)))
    return jnp.asarray(rows, jnp.float32).astype(jnp.bfloat16)


def fill_pairs(out_ref, rows, table_ref, data_ref, scale_ref):
    targets = out_ref.shape[0]
    scale = scale_ref[:, rows]
    for pair in range(table_ref.shape[0] // 2):
        two = []
        for block in (2 * pair, 2 * pair + 1):
            spectrum = lax.dot_general(
                table_ref[block],
                data_ref[:, block * HOP : block * HOP + REACH],
                (((1,), (1,)), ((), ())),
                preferred_element_type=jnp.float32,
            )
            two.append((spectrum * scale).reshape(targets, -1, data_ref.shape[0]))
        out_ref[:, pair, :, rows] = jnp.concatenate(two, axis=1).astype(jnp.bfloat16)


def rim_kernel(snap_ref, out_ref):
    rows = snap_ref.shape[0]
    half = RIM - LANES
    out_ref[:rows] = snap_ref[:, :LANES].astype(jnp.bfloat16)
    rest = snap_ref[:, LANES:]
    lane = lax.broadcasted_iota(jnp.int32, (rows // 2, LANES), 1)
    both = jnp.where(lane < half, rest[: rows // 2], pltpu.roll(rest[rows // 2 :], half, 1))
    out_ref[rows:] = both.astype(jnp.bfloat16)


def packed_rim(snapshots):
    rows, _ = snapshots.shape
    return pl.pallas_call(
        rim_kernel,
        grid=(1,),
        in_specs=[pl.BlockSpec((rows, 2 * LANES), lambda s: (0, 0))],
        out_specs=pl.BlockSpec((rows * RIM // LANES, LANES), lambda s: (0, 0)),
        out_shape=jax.ShapeDtypeStruct((rows * RIM // LANES, LANES), jnp.bfloat16),
        compiler_params=pltpu.CompilerParams(vmem_limit_bytes=LARGE),
        name="rim",
    )(snapshots)


def early_kernel(total_rows, delay_ref, table_ref, weight_ref, snap_ref, out_ref, tail_ref, late_table_ref, scale_ref, shifted_ref, data_ref):
    early = 2 * out_ref.shape[1]

    @pl.when(pl.program_id(0) == 0)
    def _():
        table = table_ref[...].astype(jnp.float32)
        for block in range(delay_ref.shape[0]):
            moved = pltpu.roll(table, delay_ref[block], 1).astype(jnp.bfloat16)
            if block < early:
                shifted_ref[block] = moved
            else:
                late_table_ref[block - early] = moved

    data_ref[...] = snap_ref[...].astype(jnp.bfloat16)
    tail_ref[...] = data_ref[:, early * HOP :]
    scale_ref[...] = jnp.sqrt(weight_ref[...] / total_rows)
    fill_pairs(out_ref, slice(None), shifted_ref, data_ref, scale_ref)


def early_spectra(snapshots, weights, block_delay, table, targets, total_rows):
    rows, span = snapshots.shape
    blocks = span // HOP
    early = (span - REACH) // HOP + 1
    lines = 4 * NF // targets
    tail = span - early * HOP
    return pl.pallas_call(
        lambda *refs: early_kernel(total_rows, *refs),
        grid=(rows // STRIP,),
        in_specs=[
            pl.BlockSpec(memory_space=pltpu.SMEM),
            pl.BlockSpec(table.shape, lambda s: (0, 0)),
            pl.BlockSpec((1, STRIP), lambda s: (0, s)),
            pl.BlockSpec((STRIP, span), lambda s: (s, 0)),
        ],
        out_specs=[
            pl.BlockSpec((targets, early // 2, lines, STRIP), lambda s: (0, 0, 0, s)),
            pl.BlockSpec((STRIP, tail), lambda s: (s, 0)),
            pl.BlockSpec((blocks - early,) + table.shape, lambda s: (0, 0, 0)),
            pl.BlockSpec((1, STRIP), lambda s: (0, s)),
        ],
        out_shape=[
            jax.ShapeDtypeStruct((targets, blocks // 2, lines, rows), jnp.bfloat16),
            jax.ShapeDtypeStruct((rows, tail), jnp.bfloat16),
            jax.ShapeDtypeStruct((blocks - early,) + table.shape, jnp.bfloat16),
            jax.ShapeDtypeStruct((1, rows), jnp.float32),
        ],
        scratch_shapes=[
            pltpu.VMEM((early,) + table.shape, jnp.bfloat16),
            pltpu.VMEM((STRIP, span), jnp.bfloat16),
        ],
        compiler_params=pltpu.CompilerParams(vmem_limit_bytes=VMEM),
        cost_estimate=pl.CostEstimate(
            flops=4 * NF * REACH * rows * early,
            bytes_accessed=4 * rows * span + 4 * NF * rows * early,
            transcendentals=0,
        ),
        name="dft_early",
    )(block_delay, table, weights.reshape(1, rows), snapshots)


def late_kernel(table_ref, scale_ref, tail_ref, rim_ref, begun_ref, out_ref, data_ref):
    rows, tail = tail_ref.shape
    strip = data_ref.shape[0]
    rest = rim_ref[rows:].astype(jnp.float32)
    lane = lax.broadcasted_iota(jnp.int32, rest.shape, 1)
    for s in range(rows // strip):
        part = slice(s * strip, (s + 1) * strip)
        mine = rest if s == 0 else pltpu.roll(rest, RIM - LANES, 1)
        mine = jnp.where(lane < RIM - LANES, mine, 0.0).astype(jnp.bfloat16)
        data_ref[:, :tail] = tail_ref[part]
        data_ref[:, tail : tail + LANES] = rim_ref[part]
        data_ref[:, tail + LANES :] = mine
        fill_pairs(out_ref, part, table_ref, data_ref, scale_ref)


def late_spectra(begun, tail, table, scale, rim):
    targets, pairs, lines, rows = begun.shape
    late = table.shape[0]
    whole = pl.BlockSpec(memory_space=pltpu.VMEM)
    return pl.pallas_call(
        late_kernel,
        grid=(1,),
        in_specs=[whole, whole, whole, whole, pl.BlockSpec(memory_space=pl.ANY)],
        out_specs=pl.BlockSpec(
            (targets, late // 2, lines, rows), lambda s: (0, 2 * pairs // late - 1, 0, 0)
        ),
        out_shape=jax.ShapeDtypeStruct(begun.shape, begun.dtype),
        input_output_aliases={4: 0},
        scratch_shapes=[pltpu.VMEM((STRIP, (late - 1) * HOP + REACH), jnp.bfloat16)],
        compiler_params=pltpu.CompilerParams(vmem_limit_bytes=VMEM),
        cost_estimate=pl.CostEstimate(
            flops=4 * NF * REACH * rows * late,
            bytes_accessed=4 * NF * rows * late,
            transcendentals=0,
        ),
        name="dft_late",
    )(table, scale, tail, rim, begun)


def split_quads(mats):
    eights = [m.reshape(m.shape[0] // 8, 8, m.shape[1]) for m in mats]
    upper = lax.broadcasted_iota(jnp.int32, eights[0].shape, 1) < 4
    low, high = [], []
    for a, b in (eights[:2], eights[2:]):
        low.append(jnp.where(upper, a, pltpu.roll(b, 4, 1)))
        high.append(jnp.where(upper, pltpu.roll(a, 4, 1), b))
    return jnp.concatenate(low, axis=1), jnp.concatenate(high, axis=1)


def csd_kernel(got_ref, out_ref, sorted_ref):
    cores, lines, every, rows = sorted_ref.shape
    freqs = lines // 2
    sources = got_ref.shape[0] // cores
    step = 4
    some = step * every // sources
    row = lax.broadcasted_iota(jnp.int32, (some * lines, some * lines), 0)
    column = lax.broadcasted_iota(jnp.int32, (some * lines, some * lines), 1)
    part = (row // some) % 2
    freq = row // (2 * some)
    order = ((row % some) * lines + part * freqs + freq == column).astype(jnp.bfloat16)
    for core in range(cores):
        for k in range(sources // step):
            first = core * sources + k * step
            by_line = lax.dot_general(
                order,
                got_ref[first : first + step].reshape(some * lines, rows),
                (((1,), (0,)), ((), ())),
                preferred_element_type=jnp.float32,
            )
            by_line = by_line.astype(jnp.bfloat16).reshape(lines, some, rows)
            sorted_ref[core, :, k * some : (k + 1) * some, :] = by_line
    real, imag = [], []
    for freq in range(freqs):
        power = 0.0
        for core in range(cores):
            both = sorted_ref[core, 2 * freq : 2 * freq + 2].reshape(2 * every, rows)
            power += lax.dot_general(
                both, both, (((1,), (1,)), ((), ())), preferred_element_type=jnp.float32
            )
        real.append(power[:every, :every] + power[every:, every:])
        imag.append(power[:every, every:] - power[every:, :every])
    for place, quad in ((0, real), (16, imag)):
        low, high = split_quads(quad)
        out_ref[:, 0, place : place + 16, :] = low.astype(jnp.bfloat16)
        out_ref[:, 1, place : place + 16, :] = high.astype(jnp.bfloat16)


def cross_power(got):
    sources, pairs, lines, rows = got.shape
    every = sources // CORES * 2 * pairs
    shape = (every // 8, 2, 2 * lines, every)
    whole = pl.BlockSpec(memory_space=pltpu.VMEM)
    return pl.pallas_call(
        csd_kernel,
        in_specs=[whole],
        out_specs=whole,
        out_shape=jax.ShapeDtypeStruct(shape, jnp.bfloat16),
        scratch_shapes=[pltpu.VMEM((CORES, lines // 2, every, rows), jnp.bfloat16)],
        compiler_params=pltpu.CompilerParams(vmem_limit_bytes=VMEM),
        name="csd",
    )(got)


def total_kernel(got_ref, out_ref, sum_ref):
    own, parts, freqs, _ = out_ref.shape
    sum_ref[...] = jnp.sum(got_ref[...].astype(jnp.float32), axis=0)
    few = freqs // CORES
    for core in range(CORES):
        for part in range(parts):
            for freq in range(few):
                for i in range(own):
                    row = (part * few + freq) * own + i
                    place = core * few + freq
                    out_ref[i, part, place : place + 1, :] = sum_ref[core, row : row + 1, :]


def totals(got, freqs):
    _, cores, lines, every = got.shape
    whole = pl.BlockSpec(memory_space=pltpu.VMEM)
    return pl.pallas_call(
        total_kernel,
        in_specs=[whole],
        out_specs=whole,
        out_shape=jax.ShapeDtypeStruct((lines * cores // (2 * freqs), 2, freqs, every), jnp.float32),
        scratch_shapes=[pltpu.VMEM((cores, lines, every), jnp.float32)],
        compiler_params=pltpu.CompilerParams(vmem_limit_bytes=VMEM),
        name="total",
    )(got)


def body(snapshots, weights, block_delay):
    groups = lax.axis_size("tm")
    chips = lax.axis_size("chip")
    targets = CORES * groups
    total_rows = snapshots.shape[0] * chips * CORES

    def exchange(array, axes):
        return lax.all_to_all(array, axes, split_axis=0, concat_axis=0, tiled=True)

    rim = shifted(packed_rim(snapshots), "tm", -1)
    begun = early_spectra(snapshots, weights, block_delay, dft_rows(groups), targets, total_rows)
    spectra = late_spectra(*begun, rim)
    partial_csd = cross_power(exchange(spectra, ("core", "tm")))
    lines, every = partial_csd.shape[2:]
    got = exchange(partial_csd.reshape(chips * CORES, lines, every), ("chip", "core"))
    return totals(got.reshape(chips, CORES, lines, every), NF // groups)


def solution(mesh):
    rows, groups = mesh.devices.shape
    by_core = Mesh(mesh.devices.reshape(rows // CORES, CORES, groups), ("chip", "core", "tm"))
    row = ("chip", "core")
    return jax.shard_map(
        body,
        mesh=by_core,
        in_specs=(P(row, "tm"), P(row), P("tm")),
        out_specs=P(row, None, "tm", None),
        check_vma=False,
    )
```

```python
import jax
import jax.numpy as jnp
import numpy as np
from jax import lax
from jax.experimental import pallas as pl
from jax.experimental.pallas import tpu as pltpu
from jax.sharding import Mesh
from jax.sharding import PartitionSpec as P

NFFT = 256
NF = 128
HOP = 128
RIM = 192
REACH = 384
STRIP = 256
CORES = 2
LANES = 128
VMEM = 24 * 1024 * 1024
LARGE = 56 * 1024 * 1024


def shifted(array, axis, by):
    count = lax.axis_size(axis)
    return lax.ppermute(array, axis, [(i, (i + by) % count) for i in range(count)])


def dft_rows(groups):
    time_index = np.arange(NFFT)
    angles = 2.0 * np.pi * (time_index[:, None] * np.arange(NF)[None, :] % NFFT) / NFFT
    window = np.sin(np.pi * time_index / NFFT) ** 2
    norm = np.sqrt(np.sum(window * window))
    table = np.stack([window[:, None] * np.cos(angles), -window[:, None] * np.sin(angles)])
    table = (table / norm).reshape(2, NFFT, groups, CORES, NF // groups // CORES)
    rows = table.transpose(3, 2, 0, 4, 1).reshape(2 * NF, NFFT)
    rows = np.pad(rows, ((0, 0), (0, REACH - NFFT)))
    return jnp.asarray(rows, jnp.float32).astype(jnp.bfloat16)


def fill_pairs(out_ref, rows, table_ref, data_ref, scale_ref):
    targets = out_ref.shape[0]
    scale = scale_ref[:, rows]
    for pair in range(table_ref.shape[0] // 2):
        two = []
        for block in (2 * pair, 2 * pair + 1):
            spectrum = lax.dot_general(
                table_ref[block],
                data_ref[:, block * HOP : block * HOP + REACH],
                (((1,), (1,)), ((), ())),
                preferred_element_type=jnp.float32,
            )
            two.append((spectrum * scale).reshape(targets, -1, data_ref.shape[0]))
        out_ref[:, pair, :, rows] = jnp.concatenate(two, axis=1).astype(jnp.bfloat16)


def rim_kernel(snap_ref, out_ref):
    rows = snap_ref.shape[0]
    half = RIM - LANES
    out_ref[:rows] = snap_ref[:, :LANES].astype(jnp.bfloat16)
    rest = snap_ref[:, LANES:]
    lane = lax.broadcasted_iota(jnp.int32, (rows // 2, LANES), 1)
    both = jnp.where(lane < half, rest[: rows // 2], pltpu.roll(rest[rows // 2 :], half, 1))
    out_ref[rows:] = both.astype(jnp.bfloat16)


def packed_rim(snapshots):
    rows, _ = snapshots.shape
    return pl.pallas_call(
        rim_kernel,
        grid=(1,),
        in_specs=[pl.BlockSpec((rows, 2 * LANES), lambda s: (0, 0))],
        out_specs=pl.BlockSpec((rows * RIM // LANES, LANES), lambda s: (0, 0)),
        out_shape=jax.ShapeDtypeStruct((rows * RIM // LANES, LANES), jnp.bfloat16),
        compiler_params=pltpu.CompilerParams(vmem_limit_bytes=LARGE),
        name="rim",
    )(snapshots)


def early_kernel(total_rows, delay_ref, table_ref, weight_ref, snap_ref, out_ref, tail_ref, late_table_ref, scale_ref, shifted_ref, data_ref):
    early = 2 * out_ref.shape[1]

    @pl.when(pl.program_id(0) == 0)
    def _():
        table = table_ref[...].astype(jnp.float32)
        for block in range(delay_ref.shape[0]):
            moved = pltpu.roll(table, delay_ref[block], 1).astype(jnp.bfloat16)
            if block < early:
                shifted_ref[block] = moved
            else:
                late_table_ref[block - early] = moved

    data_ref[...] = snap_ref[...].astype(jnp.bfloat16)
    tail_ref[...] = data_ref[:, early * HOP :]
    scale_ref[...] = jnp.sqrt(weight_ref[...] / total_rows)
    fill_pairs(out_ref, slice(None), shifted_ref, data_ref, scale_ref)


def early_spectra(snapshots, weights, block_delay, table, targets, total_rows):
    rows, span = snapshots.shape
    blocks = span // HOP
    early = (span - REACH) // HOP + 1
    lines = 4 * NF // targets
    tail = span - early * HOP
    return pl.pallas_call(
        lambda *refs: early_kernel(total_rows, *refs),
        grid=(rows // STRIP,),
        in_specs=[
            pl.BlockSpec(memory_space=pltpu.SMEM),
            pl.BlockSpec(table.shape, lambda s: (0, 0)),
            pl.BlockSpec((1, STRIP), lambda s: (0, s)),
            pl.BlockSpec((STRIP, span), lambda s: (s, 0)),
        ],
        out_specs=[
            pl.BlockSpec((targets, early // 2, lines, STRIP), lambda s: (0, 0, 0, s)),
            pl.BlockSpec((STRIP, tail), lambda s: (s, 0)),
            pl.BlockSpec((blocks - early,) + table.shape, lambda s: (0, 0, 0)),
            pl.BlockSpec((1, STRIP), lambda s: (0, s)),
        ],
        out_shape=[
            jax.ShapeDtypeStruct((targets, early // 2, lines, rows), jnp.bfloat16),
            jax.ShapeDtypeStruct((rows, tail), jnp.bfloat16),
            jax.ShapeDtypeStruct((blocks - early,) + table.shape, jnp.bfloat16),
            jax.ShapeDtypeStruct((1, rows), jnp.float32),
        ],
        scratch_shapes=[
            pltpu.VMEM((early,) + table.shape, jnp.bfloat16),
            pltpu.VMEM((STRIP, span), jnp.bfloat16),
        ],
        compiler_params=pltpu.CompilerParams(vmem_limit_bytes=VMEM),
        cost_estimate=pl.CostEstimate(
            flops=4 * NF * REACH * rows * early,
            bytes_accessed=4 * rows * span + 4 * NF * rows * early,
            transcendentals=0,
        ),
        name="dft_early",
    )(block_delay, table, weights.reshape(1, rows), snapshots)


def late_kernel(table_ref, scale_ref, tail_ref, rim_ref, after_ref, out_ref, data_ref):
    rows, tail = tail_ref.shape
    strip = data_ref.shape[0]
    rest = rim_ref[rows:].astype(jnp.float32)
    lane = lax.broadcasted_iota(jnp.int32, rest.shape, 1)
    for s in range(rows // strip):
        part = slice(s * strip, (s + 1) * strip)
        mine = rest if s == 0 else pltpu.roll(rest, RIM - LANES, 1)
        mine = jnp.where(lane < RIM - LANES, mine, 0.0).astype(jnp.bfloat16)
        data_ref[:, :tail] = tail_ref[part]
        data_ref[:, tail : tail + LANES] = rim_ref[part]
        data_ref[:, tail + LANES :] = mine
        fill_pairs(out_ref, part, table_ref, data_ref, scale_ref)


def late_spectra(tail, table, scale, rim, targets, after):
    rows, _ = tail.shape
    late = table.shape[0]
    whole = pl.BlockSpec(memory_space=pltpu.VMEM)
    return pl.pallas_call(
        late_kernel,
        in_specs=[whole, whole, whole, whole, pl.BlockSpec(memory_space=pl.ANY)],
        out_specs=whole,
        out_shape=jax.ShapeDtypeStruct((targets, late // 2, 4 * NF // targets, rows), jnp.bfloat16),
        scratch_shapes=[pltpu.VMEM((STRIP, (late - 1) * HOP + REACH), jnp.bfloat16)],
        compiler_params=pltpu.CompilerParams(vmem_limit_bytes=VMEM),
        cost_estimate=pl.CostEstimate(
            flops=4 * NF * REACH * rows * late,
            bytes_accessed=4 * NF * rows * late,
            transcendentals=0,
        ),
        name="dft_late",
    )(table, scale, tail, rim, after)


def split_quads(mats):
    eights = [m.reshape(m.shape[0] // 8, 8, m.shape[1]) for m in mats]
    upper = lax.broadcasted_iota(jnp.int32, eights[0].shape, 1) < 4
    low, high = [], []
    for a, b in (eights[:2], eights[2:]):
        low.append(jnp.where(upper, a, pltpu.roll(b, 4, 1)))
        high.append(jnp.where(upper, pltpu.roll(a, 4, 1), b))
    return jnp.concatenate(low, axis=1), jnp.concatenate(high, axis=1)


def csd_kernel(early_ref, late_ref, out_ref, sorted_ref):
    cores, lines, every, rows = sorted_ref.shape
    freqs = lines // 2
    sources = early_ref.shape[0] // cores
    early, late = 2 * early_ref.shape[1], 2 * late_ref.shape[1]
    blocks = early + late
    step = 4
    some = step * blocks
    row = lax.broadcasted_iota(jnp.int32, (some * lines, some * lines), 0)
    column = lax.broadcasted_iota(jnp.int32, (some * lines, some * lines), 1)
    source, block = (row % some) // blocks, row % blocks
    part, freq = (row // some) % 2, row // (2 * some)
    place = jnp.where(
        block < early, source * early + block, step * early + source * late + block - early
    )
    order = (place * lines + part * freqs + freq == column).astype(jnp.bfloat16)
    for core in range(cores):
        for k in range(sources // step):
            some_sources = slice(core * sources + k * step, core * sources + (k + 1) * step)
            chunk = [r[some_sources].reshape(-1, rows) for r in (early_ref, late_ref)]
            by_line = lax.dot_general(
                order,
                jnp.concatenate(chunk, axis=0),
                (((1,), (0,)), ((), ())),
                preferred_element_type=jnp.float32,
            )
            by_line = by_line.astype(jnp.bfloat16).reshape(lines, some, rows)
            sorted_ref[core, :, k * some : (k + 1) * some, :] = by_line
    real, imag = [], []
    for freq in range(freqs):
        power = 0.0
        for core in range(cores):
            both = sorted_ref[core, 2 * freq : 2 * freq + 2].reshape(2 * every, rows)
            power += lax.dot_general(
                both, both, (((1,), (1,)), ((), ())), preferred_element_type=jnp.float32
            )
        real.append(power[:every, :every] + power[every:, every:])
        imag.append(power[:every, every:] - power[every:, :every])
    for place, quad in ((0, real), (16, imag)):
        low, high = split_quads(quad)
        out_ref[:, 0, place : place + 16, :] = low.astype(jnp.bfloat16)
        out_ref[:, 1, place : place + 16, :] = high.astype(jnp.bfloat16)


def cross_power(early, late):
    sources, pairs, lines, rows = early.shape
    every = sources // CORES * 2 * (pairs + late.shape[1])
    shape = (every // 8, 2, 2 * lines, every)
    whole = pl.BlockSpec(memory_space=pltpu.VMEM)
    return pl.pallas_call(
        csd_kernel,
        in_specs=[whole, whole],
        out_specs=whole,
        out_shape=jax.ShapeDtypeStruct(shape, jnp.bfloat16),
        scratch_shapes=[pltpu.VMEM((CORES, lines // 2, every, rows), jnp.bfloat16)],
        compiler_params=pltpu.CompilerParams(vmem_limit_bytes=VMEM),
        name="csd",
    )(early, late)


def total_kernel(got_ref, out_ref, sum_ref):
    own, parts, freqs, _ = out_ref.shape
    sum_ref[...] = jnp.sum(got_ref[...].astype(jnp.float32), axis=0)
    few = freqs // CORES
    for core in range(CORES):
        for part in range(parts):
            for freq in range(few):
                for i in range(own):
                    row = (part * few + freq) * own + i
                    place = core * few + freq
                    out_ref[i, part, place : place + 1, :] = sum_ref[core, row : row + 1, :]


def totals(got, freqs):
    _, cores, lines, every = got.shape
    whole = pl.BlockSpec(memory_space=pltpu.VMEM)
    return pl.pallas_call(
        total_kernel,
        in_specs=[whole],
        out_specs=whole,
        out_shape=jax.ShapeDtypeStruct((lines * cores // (2 * freqs), 2, freqs, every), jnp.float32),
        scratch_shapes=[pltpu.VMEM((cores, lines, every), jnp.float32)],
        compiler_params=pltpu.CompilerParams(vmem_limit_bytes=VMEM),
        name="total",
    )(got)


def body(snapshots, weights, block_delay):
    groups = lax.axis_size("tm")
    chips = lax.axis_size("chip")
    targets = CORES * groups
    total_rows = snapshots.shape[0] * chips * CORES

    def exchange(array, axes):
        return lax.all_to_all(array, axes, split_axis=0, concat_axis=0, tiled=True)

    rim = shifted(packed_rim(snapshots), "tm", -1)
    early, *own = early_spectra(
        snapshots, weights, block_delay, dft_rows(groups), targets, total_rows
    )
    early_here = exchange(early, ("core", "tm"))
    late = late_spectra(*own, rim, targets, early_here)
    partial_csd = cross_power(early_here, exchange(late, ("core", "tm")))
    lines, every = partial_csd.shape[2:]
    got = exchange(partial_csd.reshape(chips * CORES, lines, every), ("chip", "core"))
    return totals(got.reshape(chips, CORES, lines, every), NF // groups)


def solution(mesh):
    rows, groups = mesh.devices.shape
    by_core = Mesh(mesh.devices.reshape(rows // CORES, CORES, groups), ("chip", "core", "tm"))
    row = ("chip", "core")
    return jax.shard_map(
        body,
        mesh=by_core,
        in_specs=(P(row, "tm"), P(row), P("tm")),
        out_specs=P(row, None, "tm", None),
        check_vma=False,
    )
```

```python
import jax
import jax.numpy as jnp
import numpy as np
from jax import lax
from jax.experimental import pallas as pl
from jax.experimental.pallas import tpu as pltpu
from jax.sharding import Mesh
from jax.sharding import PartitionSpec as P

NFFT = 256
NF = 128
HOP = 128
RIM = 192
REACH = 384
STRIP = 256
PAIR = 2
LANES = 128
VMEM = 24 * 1024 * 1024
LARGE = 56 * 1024 * 1024


def shifted(array, axis, by):
    count = lax.axis_size(axis)
    return lax.ppermute(array, axis, [(i, (i + by) % count) for i in range(count)])


def dft_rows(groups):
    time_index = np.arange(NFFT)
    angles = 2.0 * np.pi * (time_index[:, None] * np.arange(NF)[None, :] % NFFT) / NFFT
    window = np.sin(np.pi * time_index / NFFT) ** 2
    norm = np.sqrt(np.sum(window * window))
    table = np.stack([window[:, None] * np.cos(angles), -window[:, None] * np.sin(angles)])
    table = (table / norm).reshape(2, NFFT, groups, PAIR, NF // groups // PAIR)
    rows = table.transpose(3, 2, 0, 4, 1).reshape(2 * NF, NFFT)
    rows = np.pad(rows, ((0, 0), (0, REACH - NFFT)))
    return jnp.asarray(rows, jnp.float32).astype(jnp.bfloat16)


def fill_pairs(out_ref, rows, table_ref, data_ref, scale_ref):
    targets = out_ref.shape[0]
    scale = scale_ref[:, rows]
    for pair in range(table_ref.shape[0] // 2):
        two = []
        for block in (2 * pair, 2 * pair + 1):
            spectrum = lax.dot_general(
                table_ref[block],
                data_ref[:, block * HOP : block * HOP + REACH],
                (((1,), (1,)), ((), ())),
                preferred_element_type=jnp.float32,
            )
            two.append((spectrum * scale).reshape(targets, -1, data_ref.shape[0]))
        out_ref[:, pair, :, rows] = jnp.concatenate(two, axis=1).astype(jnp.bfloat16)


def rim_kernel(snap_ref, out_ref):
    rows = snap_ref.shape[0]
    half = RIM - LANES
    out_ref[:rows] = snap_ref[:, :LANES].astype(jnp.bfloat16)
    rest = snap_ref[:, LANES:]
    lane = lax.broadcasted_iota(jnp.int32, (rows // 2, LANES), 1)
    both = jnp.where(lane < half, rest[: rows // 2], pltpu.roll(rest[rows // 2 :], half, 1))
    out_ref[rows:] = both.astype(jnp.bfloat16)


def packed_rim(snapshots):
    rows, _ = snapshots.shape
    return pl.pallas_call(
        rim_kernel,
        grid=(1,),
        in_specs=[pl.BlockSpec((rows, 2 * LANES), lambda s: (0, 0))],
        out_specs=pl.BlockSpec((rows * RIM // LANES, LANES), lambda s: (0, 0)),
        out_shape=jax.ShapeDtypeStruct((rows * RIM // LANES, LANES), jnp.bfloat16),
        compiler_params=pltpu.CompilerParams(vmem_limit_bytes=LARGE),
        name="rim",
    )(snapshots)


def early_kernel(total_rows, delay_ref, table_ref, weight_ref, snap_ref, out_ref, tail_ref, late_table_ref, scale_ref, shifted_ref, data_ref):
    early = 2 * out_ref.shape[1]

    @pl.when(pl.program_id(0) == 0)
    def _():
        table = table_ref[...].astype(jnp.float32)
        for block in range(delay_ref.shape[0]):
            moved = pltpu.roll(table, delay_ref[block], 1).astype(jnp.bfloat16)
            if block < early:
                shifted_ref[block] = moved
            else:
                late_table_ref[block - early] = moved

    data_ref[...] = snap_ref[...].astype(jnp.bfloat16)
    tail_ref[...] = data_ref[:, early * HOP :]
    scale_ref[...] = jnp.sqrt(weight_ref[...] / total_rows)
    fill_pairs(out_ref, slice(None), shifted_ref, data_ref, scale_ref)


def early_spectra(snapshots, weights, block_delay, table, targets, total_rows):
    rows, span = snapshots.shape
    blocks = span // HOP
    early = (span - REACH) // HOP + 1
    lines = 4 * NF // targets
    tail = span - early * HOP
    return pl.pallas_call(
        lambda *refs: early_kernel(total_rows, *refs),
        grid=(rows // STRIP,),
        in_specs=[
            pl.BlockSpec(memory_space=pltpu.SMEM),
            pl.BlockSpec(table.shape, lambda s: (0, 0)),
            pl.BlockSpec((1, STRIP), lambda s: (0, s)),
            pl.BlockSpec((STRIP, span), lambda s: (s, 0)),
        ],
        out_specs=[
            pl.BlockSpec((targets, early // 2, lines, STRIP), lambda s: (0, 0, 0, s)),
            pl.BlockSpec((STRIP, tail), lambda s: (s, 0)),
            pl.BlockSpec((blocks - early,) + table.shape, lambda s: (0, 0, 0)),
            pl.BlockSpec((1, STRIP), lambda s: (0, s)),
        ],
        out_shape=[
            jax.ShapeDtypeStruct((targets, blocks // 2, lines, rows), jnp.bfloat16),
            jax.ShapeDtypeStruct((rows, tail), jnp.bfloat16),
            jax.ShapeDtypeStruct((blocks - early,) + table.shape, jnp.bfloat16),
            jax.ShapeDtypeStruct((1, rows), jnp.float32),
        ],
        scratch_shapes=[
            pltpu.VMEM((early,) + table.shape, jnp.bfloat16),
            pltpu.VMEM((STRIP, span), jnp.bfloat16),
        ],
        compiler_params=pltpu.CompilerParams(vmem_limit_bytes=VMEM),
        cost_estimate=pl.CostEstimate(
            flops=4 * NF * REACH * rows * early,
            bytes_accessed=4 * rows * span + 4 * NF * rows * early,
            transcendentals=0,
        ),
        name="dft_early",
    )(block_delay, table, weights.reshape(1, rows), snapshots)


def late_kernel(table_ref, scale_ref, tail_ref, rim_ref, begun_ref, out_ref, data_ref):
    rows, tail = tail_ref.shape
    strip = data_ref.shape[0]
    rest = rim_ref[rows:].astype(jnp.float32)
    lane = lax.broadcasted_iota(jnp.int32, rest.shape, 1)
    for s in range(rows // strip):
        part = slice(s * strip, (s + 1) * strip)
        mine = rest if s == 0 else pltpu.roll(rest, RIM - LANES, 1)
        mine = jnp.where(lane < RIM - LANES, mine, 0.0).astype(jnp.bfloat16)
        data_ref[:, :tail] = tail_ref[part]
        data_ref[:, tail : tail + LANES] = rim_ref[part]
        data_ref[:, tail + LANES :] = mine
        fill_pairs(out_ref, part, table_ref, data_ref, scale_ref)


def late_spectra(begun, tail, table, scale, rim):
    targets, pairs, lines, rows = begun.shape
    late = table.shape[0]
    whole = pl.BlockSpec(memory_space=pltpu.VMEM)
    return pl.pallas_call(
        late_kernel,
        grid=(1,),
        in_specs=[whole, whole, whole, whole, pl.BlockSpec(memory_space=pl.ANY)],
        out_specs=pl.BlockSpec(
            (targets, late // 2, lines, rows), lambda s: (0, 2 * pairs // late - 1, 0, 0)
        ),
        out_shape=jax.ShapeDtypeStruct(begun.shape, begun.dtype),
        input_output_aliases={4: 0},
        scratch_shapes=[pltpu.VMEM((STRIP, (late - 1) * HOP + REACH), jnp.bfloat16)],
        compiler_params=pltpu.CompilerParams(vmem_limit_bytes=VMEM),
        cost_estimate=pl.CostEstimate(
            flops=4 * NF * REACH * rows * late,
            bytes_accessed=4 * NF * rows * late,
            transcendentals=0,
        ),
        name="dft_late",
    )(table, scale, tail, rim, begun)


def split_quads(mats):
    eights = [m.reshape(m.shape[0] // 8, 8, m.shape[1]) for m in mats]
    upper = lax.broadcasted_iota(jnp.int32, eights[0].shape, 1) < 4
    low, high = [], []
    for a, b in (eights[:2], eights[2:]):
        low.append(jnp.where(upper, a, pltpu.roll(b, 4, 1)))
        high.append(jnp.where(upper, pltpu.roll(a, 4, 1), b))
    return jnp.concatenate(low, axis=1), jnp.concatenate(high, axis=1)


def csd_kernel(got_ref, out_ref, sorted_ref):
    halves, lines, every, rows = sorted_ref.shape
    freqs = lines // 2
    sources = got_ref.shape[0] // halves
    step = 4
    some = step * every // sources
    row = lax.broadcasted_iota(jnp.int32, (some * lines, some * lines), 0)
    column = lax.broadcasted_iota(jnp.int32, (some * lines, some * lines), 1)
    part = (row // some) % 2
    freq = row // (2 * some)
    order = ((row % some) * lines + part * freqs + freq == column).astype(jnp.bfloat16)
    for half in range(halves):
        for k in range(sources // step):
            first = half * sources + k * step
            by_line = lax.dot_general(
                order,
                got_ref[first : first + step].reshape(some * lines, rows),
                (((1,), (0,)), ((), ())),
                preferred_element_type=jnp.float32,
            )
            by_line = by_line.astype(jnp.bfloat16).reshape(lines, some, rows)
            sorted_ref[half, :, k * some : (k + 1) * some, :] = by_line
    real, imag = [], []
    for freq in range(freqs):
        power = 0.0
        for half in range(halves):
            both = sorted_ref[half, 2 * freq : 2 * freq + 2].reshape(2 * every, rows)
            power += lax.dot_general(
                both, both, (((1,), (1,)), ((), ())), preferred_element_type=jnp.float32
            )
        real.append(power[:every, :every] + power[every:, every:])
        imag.append(power[:every, every:] - power[every:, :every])
    for place, quad in ((0, real), (16, imag)):
        low, high = split_quads(quad)
        out_ref[:, 0, place : place + 16, :] = low.astype(jnp.bfloat16)
        out_ref[:, 1, place : place + 16, :] = high.astype(jnp.bfloat16)


def cross_power(got):
    sources, pairs, lines, rows = got.shape
    every = sources // PAIR * 2 * pairs
    shape = (every // 8, 2, 2 * lines, every)
    whole = pl.BlockSpec(memory_space=pltpu.VMEM)
    return pl.pallas_call(
        csd_kernel,
        in_specs=[whole],
        out_specs=whole,
        out_shape=jax.ShapeDtypeStruct(shape, jnp.bfloat16),
        scratch_shapes=[pltpu.VMEM((PAIR, lines // 2, every, rows), jnp.bfloat16)],
        compiler_params=pltpu.CompilerParams(vmem_limit_bytes=VMEM),
        name="csd",
    )(got)


def total_kernel(got_ref, out_ref, sum_ref):
    own, parts, freqs, _ = out_ref.shape
    sum_ref[...] = jnp.sum(got_ref[...].astype(jnp.float32), axis=1)
    few = freqs // PAIR
    for half in range(PAIR):
        for part in range(parts):
            for freq in range(few):
                for i in range(own):
                    row = (part * few + freq) * own + i
                    place = half * few + freq
                    out_ref[i, part, place : place + 1, :] = sum_ref[half, row : row + 1, :]


def totals(got, freqs):
    halves, _, lines, every = got.shape
    whole = pl.BlockSpec(memory_space=pltpu.VMEM)
    return pl.pallas_call(
        total_kernel,
        in_specs=[whole],
        out_specs=whole,
        out_shape=jax.ShapeDtypeStruct((lines * halves // (2 * freqs), 2, freqs, every), jnp.float32),
        scratch_shapes=[pltpu.VMEM((halves, lines, every), jnp.float32)],
        compiler_params=pltpu.CompilerParams(vmem_limit_bytes=VMEM),
        name="total",
    )(got)


def body(snapshots, weights, block_delay):
    groups = lax.axis_size("tm")
    others = lax.axis_size("other")
    targets = PAIR * groups
    total_rows = snapshots.shape[0] * others * PAIR

    def exchange(array, axes):
        return lax.all_to_all(array, axes, split_axis=0, concat_axis=0, tiled=True)

    rim = shifted(packed_rim(snapshots), "tm", -1)
    begun = early_spectra(snapshots, weights, block_delay, dft_rows(groups), targets, total_rows)
    spectra = late_spectra(*begun, rim)
    partial_csd = cross_power(exchange(spectra, ("half", "tm")))
    lines, every = partial_csd.shape[2:]
    got = exchange(partial_csd.reshape(others * PAIR, lines, every), ("half", "other"))
    return totals(got.reshape(PAIR, others, lines, every), NF // groups)


def solution(mesh):
    rows, groups = mesh.devices.shape
    by_half = Mesh(mesh.devices.reshape(PAIR, rows // PAIR, groups), ("half", "other", "tm"))
    row = ("half", "other")
    return jax.shard_map(
        body,
        mesh=by_half,
        in_specs=(P(row, "tm"), P(row), P("tm")),
        out_specs=P(row, None, "tm", None),
        check_vma=False,
    )
```

```python
import jax
import jax.numpy as jnp
import numpy as np
from jax import lax
from jax.experimental import pallas as pl
from jax.experimental.pallas import tpu as pltpu
from jax.sharding import Mesh
from jax.sharding import PartitionSpec as P

NFFT = 256
NF = 128
HOP = 128
RIM = 192
REACH = 384
STRIP = 256
HALVES = 2
CORES = 2
INNER = HALVES * CORES
QUAD = 4
LANES = 128
VMEM = 24 * 1024 * 1024
LARGE = 56 * 1024 * 1024


def shifted(array, axis, by):
    count = lax.axis_size(axis)
    return lax.ppermute(array, axis, [(i, (i + by) % count) for i in range(count)])


def dft_rows(groups):
    time_index = np.arange(NFFT)
    angles = 2.0 * np.pi * (time_index[:, None] * np.arange(NF)[None, :] % NFFT) / NFFT
    window = np.sin(np.pi * time_index / NFFT) ** 2
    norm = np.sqrt(np.sum(window * window))
    table = np.stack([window[:, None] * np.cos(angles), -window[:, None] * np.sin(angles)])
    table = (table / norm).reshape(2, NFFT, groups, INNER, NF // groups // INNER)
    rows = table.transpose(3, 2, 0, 4, 1).reshape(2 * NF, NFFT)
    rows = np.pad(rows, ((0, 0), (0, REACH - NFFT)))
    return jnp.asarray(rows, jnp.float32).astype(jnp.bfloat16)


def split_quads(mats):
    eights = [m.reshape(m.shape[0] // 8, 8, m.shape[1]) for m in mats]
    upper = lax.broadcasted_iota(jnp.int32, eights[0].shape, 1) < 4
    low, high = [], []
    for a, b in (eights[:2], eights[2:]):
        low.append(jnp.where(upper, a, pltpu.roll(b, 4, 1)))
        high.append(jnp.where(upper, pltpu.roll(a, 4, 1), b))
    return jnp.concatenate(low, axis=1), jnp.concatenate(high, axis=1)


def spectrum(block, table_ref, data_ref, scale):
    products = lax.dot_general(
        table_ref[block],
        data_ref[:, block * HOP : block * HOP + REACH],
        (((1,), (1,)), ((), ())),
        preferred_element_type=jnp.float32,
    )
    return products * scale


def put_quad(out_ref, tile, rows, spectra):
    low, high = split_quads(spectra)
    out_ref[:, 0, tile, :, rows] = low.astype(jnp.bfloat16)
    out_ref[:, 1, tile, :, rows] = high.astype(jnp.bfloat16)


def rim_kernel(snap_ref, out_ref):
    rows = snap_ref.shape[0]
    half = RIM - LANES
    out_ref[:rows] = snap_ref[:, :LANES].astype(jnp.bfloat16)
    rest = snap_ref[:, LANES:]
    lane = lax.broadcasted_iota(jnp.int32, (rows // 2, LANES), 1)
    both = jnp.where(lane < half, rest[: rows // 2], pltpu.roll(rest[rows // 2 :], half, 1))
    out_ref[rows:] = both.astype(jnp.bfloat16)


def packed_rim(snapshots):
    rows, _ = snapshots.shape
    return pl.pallas_call(
        rim_kernel,
        grid=(1,),
        in_specs=[pl.BlockSpec((rows, 2 * LANES), lambda s: (0, 0))],
        out_specs=pl.BlockSpec((rows * RIM // LANES, LANES), lambda s: (0, 0)),
        out_shape=jax.ShapeDtypeStruct((rows * RIM // LANES, LANES), jnp.bfloat16),
        compiler_params=pltpu.CompilerParams(vmem_limit_bytes=LARGE),
        name="rim",
    )(snapshots)


def early_kernel(total_rows, delay_ref, table_ref, weight_ref, snap_ref, out_ref, rest_ref, tail_ref, late_table_ref, scale_ref, shifted_ref, data_ref):
    early = shifted_ref.shape[0]

    @pl.when(pl.program_id(0) == 0)
    def _():
        table = table_ref[...].astype(jnp.float32)
        for block in range(delay_ref.shape[0]):
            moved = pltpu.roll(table, delay_ref[block], 1).astype(jnp.bfloat16)
            if block < early:
                shifted_ref[block] = moved
            else:
                late_table_ref[block - early] = moved

    data_ref[...] = snap_ref[...].astype(jnp.bfloat16)
    tail_ref[...] = data_ref[:, early * HOP :]
    scale = jnp.sqrt(weight_ref[...] / total_rows)
    scale_ref[...] = scale
    spectra = [spectrum(block, shifted_ref, data_ref, scale) for block in range(early)]
    put_quad(out_ref, 0, slice(None), spectra[:QUAD])
    for k, one in enumerate(spectra[QUAD:]):
        rest_ref[k] = one.astype(jnp.bfloat16)


def early_spectra(snapshots, weights, block_delay, table, targets, total_rows):
    rows, span = snapshots.shape
    blocks = span // HOP
    early = (span - REACH) // HOP + 1
    tail = span - early * HOP
    shape = (targets // 2, 2, blocks // QUAD, 2 * QUAD * NF // targets, rows)
    return pl.pallas_call(
        lambda *refs: early_kernel(total_rows, *refs),
        grid=(rows // STRIP,),
        in_specs=[
            pl.BlockSpec(memory_space=pltpu.SMEM),
            pl.BlockSpec(table.shape, lambda s: (0, 0)),
            pl.BlockSpec((1, STRIP), lambda s: (0, s)),
            pl.BlockSpec((STRIP, span), lambda s: (s, 0)),
        ],
        out_specs=[
            pl.BlockSpec(shape[:2] + (1, shape[3], STRIP), lambda s: (0, 0, 0, 0, s)),
            pl.BlockSpec((early - QUAD, 2 * NF, STRIP), lambda s: (0, 0, s)),
            pl.BlockSpec((STRIP, tail), lambda s: (s, 0)),
            pl.BlockSpec((blocks - early,) + table.shape, lambda s: (0, 0, 0)),
            pl.BlockSpec((1, STRIP), lambda s: (0, s)),
        ],
        out_shape=[
            jax.ShapeDtypeStruct(shape, jnp.bfloat16),
            jax.ShapeDtypeStruct((early - QUAD, 2 * NF, rows), jnp.bfloat16),
            jax.ShapeDtypeStruct((rows, tail), jnp.bfloat16),
            jax.ShapeDtypeStruct((blocks - early,) + table.shape, jnp.bfloat16),
            jax.ShapeDtypeStruct((1, rows), jnp.float32),
        ],
        scratch_shapes=[
            pltpu.VMEM((early,) + table.shape, jnp.bfloat16),
            pltpu.VMEM((STRIP, span), jnp.bfloat16),
        ],
        compiler_params=pltpu.CompilerParams(vmem_limit_bytes=VMEM),
        cost_estimate=pl.CostEstimate(
            flops=4 * NF * REACH * rows * early,
            bytes_accessed=4 * rows * span + 4 * NF * rows * early,
            transcendentals=0,
        ),
        name="dft_early",
    )(block_delay, table, weights.reshape(1, rows), snapshots)


def late_kernel(rest_ref, table_ref, scale_ref, tail_ref, rim_ref, begun_ref, out_ref, data_ref):
    rows, tail = tail_ref.shape
    strip = data_ref.shape[0]
    late = table_ref.shape[0]
    lower = rim_ref[rows:].astype(jnp.float32)
    lane = lax.broadcasted_iota(jnp.int32, lower.shape, 1)
    for s in range(rows // strip):
        part = slice(s * strip, (s + 1) * strip)
        mine = lower if s == 0 else pltpu.roll(lower, RIM - LANES, 1)
        mine = jnp.where(lane < RIM - LANES, mine, 0.0).astype(jnp.bfloat16)
        data_ref[:, :tail] = tail_ref[part]
        data_ref[:, tail : tail + LANES] = rim_ref[part]
        data_ref[:, tail + LANES :] = mine
        spectra = [rest_ref[k, :, part].astype(jnp.float32) for k in range(QUAD - late)]
        spectra += [spectrum(k, table_ref, data_ref, scale_ref[:, part]) for k in range(late)]
        put_quad(out_ref, 0, part, spectra)


def late_spectra(begun, rest, tail, table, scale, rim):
    rows, _ = tail.shape
    late = table.shape[0]
    whole = pl.BlockSpec(memory_space=pltpu.VMEM)
    return pl.pallas_call(
        late_kernel,
        grid=(1,),
        in_specs=[whole] * 5 + [pl.BlockSpec(memory_space=pl.ANY)],
        out_specs=pl.BlockSpec(
            begun.shape[:2] + (1,) + begun.shape[3:], lambda s: (0, 0, begun.shape[2] - 1, 0, 0)
        ),
        out_shape=jax.ShapeDtypeStruct(begun.shape, begun.dtype),
        input_output_aliases={5: 0},
        scratch_shapes=[pltpu.VMEM((STRIP, (late - 1) * HOP + REACH), jnp.bfloat16)],
        compiler_params=pltpu.CompilerParams(vmem_limit_bytes=VMEM),
        cost_estimate=pl.CostEstimate(
            flops=4 * NF * REACH * rows * late,
            bytes_accessed=4 * NF * rows * QUAD,
            transcendentals=0,
        ),
        name="dft_late",
    )(rest, table, scale, tail, rim, begun)


def csd_kernel(got_ref, out_ref, sorted_ref):
    inner, lines, every, rows = sorted_ref.shape
    freqs = lines // 2
    sources = got_ref.shape[0] // inner
    step = 8
    some = step * every // sources
    row = lax.broadcasted_iota(jnp.int32, (some * lines, some * lines), 0)
    column = lax.broadcasted_iota(jnp.int32, (some * lines, some * lines), 1)
    part = (row // some) % 2
    freq = row // (2 * some)
    order = ((row % some) * lines + part * freqs + freq == column).astype(jnp.bfloat16)
    for k in range(inner):
        for j in range(sources // step):
            first = k * sources + j * step
            by_line = lax.dot_general(
                order,
                got_ref[first : first + step].reshape(some * lines, rows),
                (((1,), (0,)), ((), ())),
                preferred_element_type=jnp.float32,
            )
            by_line = by_line.astype(jnp.bfloat16).reshape(lines, some, rows)
            sorted_ref[k, :, j * some : (j + 1) * some, :] = by_line
    real, imag = [], []
    for freq in range(freqs):
        power = 0.0
        for k in range(inner):
            both = sorted_ref[k, 2 * freq : 2 * freq + 2].reshape(2 * every, rows)
            power += lax.dot_general(
                both, both, (((1,), (1,)), ((), ())), preferred_element_type=jnp.float32
            )
        real.append(power[:every, :every] + power[every:, every:])
        imag.append(power[:every, every:] - power[every:, :every])
    low, high = split_quads(real + imag)
    out_ref[:, 0] = low.astype(jnp.bfloat16)
    out_ref[:, 1] = high.astype(jnp.bfloat16)


def cross_power(got):
    sources, tiles, lines, rows = got.shape
    every = sources // INNER * QUAD * tiles
    shape = (every // 8, 2, lines, every)
    whole = pl.BlockSpec(memory_space=pltpu.VMEM)
    return pl.pallas_call(
        csd_kernel,
        in_specs=[whole],
        out_specs=whole,
        out_shape=jax.ShapeDtypeStruct(shape, jnp.bfloat16),
        scratch_shapes=[pltpu.VMEM((INNER, lines // QUAD, every, rows), jnp.bfloat16)],
        compiler_params=pltpu.CompilerParams(vmem_limit_bytes=VMEM),
        name="csd",
    )(got)


def total_kernel(got_ref, out_ref, sum_ref):
    own, parts, freqs, _ = out_ref.shape
    halves, cores, _, _ = sum_ref.shape
    sum_ref[...] = jnp.sum(got_ref[...].astype(jnp.float32), axis=1)
    few = freqs // (halves * cores)
    for half in range(halves):
        for core in range(cores):
            for part in range(parts):
                for freq in range(few):
                    for i in range(own):
                        row = (part * few + freq) * own + i
                        place = (half * cores + core) * few + freq
                        out_ref[i, part, place : place + 1, :] = sum_ref[half, core, row : row + 1, :]


def totals(got, freqs):
    halves, _, cores, lines, every = got.shape
    whole = pl.BlockSpec(memory_space=pltpu.VMEM)
    return pl.pallas_call(
        total_kernel,
        in_specs=[whole],
        out_specs=whole,
        out_shape=jax.ShapeDtypeStruct((QUAD, 2, freqs, every), jnp.float32),
        scratch_shapes=[pltpu.VMEM((halves, cores, lines, every), jnp.float32)],
        compiler_params=pltpu.CompilerParams(vmem_limit_bytes=VMEM),
        name="total",
    )(got)


def body(snapshots, weights, block_delay):
    groups = lax.axis_size("tm")
    others = lax.axis_size("other")
    targets = INNER * groups
    grid_rows = snapshots.shape[0]

    def exchange(array, axes):
        return lax.all_to_all(array, axes, split_axis=0, concat_axis=0, tiled=True)

    rim = shifted(packed_rim(snapshots), "tm", -1)
    begun = early_spectra(
        snapshots, weights, block_delay, dft_rows(groups), targets, grid_rows * others * INNER
    )
    spectra = late_spectra(*begun, rim).reshape((targets,) + begun[0].shape[2:])
    partial_csd = cross_power(exchange(spectra, ("half", "core", "tm")))
    lines, every = partial_csd.shape[2:]
    got = exchange(partial_csd.reshape(-1, lines, every), ("half", "other", "core"))
    return totals(got.reshape(HALVES, others, CORES, lines, every), NF // groups)


def solution(mesh):
    rows, groups = mesh.devices.shape
    row = ("half", "other", "core")
    split = Mesh(
        mesh.devices.reshape(HALVES, rows // INNER, CORES, groups), row + ("tm",)
    )
    return jax.shard_map(
        body,
        mesh=split,
        in_specs=(P(row, "tm"), P(row), P("tm")),
        out_specs=P(row, None, "tm", None),
        check_vma=False,
    )
```

```python
import jax
import jax.numpy as jnp
import numpy as np
from jax import lax
from jax.experimental import pallas as pl
from jax.experimental.pallas import tpu as pltpu
from jax.sharding import Mesh
from jax.sharding import PartitionSpec as P

NFFT = 256
NF = 128
HOP = 128
RIM = 192
REACH = 384
STRIP = 256
PAIR = 2
LANES = 128
VMEM = 24 * 1024 * 1024
LARGE = 56 * 1024 * 1024


def shifted(array, axis, by):
    count = lax.axis_size(axis)
    return lax.ppermute(array, axis, [(i, (i + by) % count) for i in range(count)])


def dft_rows(groups):
    time_index = np.arange(NFFT)
    angles = 2.0 * np.pi * (time_index[:, None] * np.arange(NF)[None, :] % NFFT) / NFFT
    window = np.sin(np.pi * time_index / NFFT) ** 2
    norm = np.sqrt(np.sum(window * window))
    table = np.stack([window[:, None] * np.cos(angles), -window[:, None] * np.sin(angles)])
    table = (table / norm).reshape(2, NFFT, groups, PAIR, NF // groups // PAIR)
    rows = table.transpose(2, 3, 0, 4, 1).reshape(2 * NF, NFFT)
    rows = np.pad(rows, ((0, 0), (0, REACH - NFFT)))
    return jnp.asarray(rows, jnp.float32).astype(jnp.bfloat16)


def fill_pairs(out_ref, rows, table_ref, data_ref, scale_ref):
    targets = out_ref.shape[0]
    scale = scale_ref[:, rows]
    for pair in range(table_ref.shape[0] // 2):
        two = []
        for block in (2 * pair, 2 * pair + 1):
            spectrum = lax.dot_general(
                table_ref[block],
                data_ref[:, block * HOP : block * HOP + REACH],
                (((1,), (1,)), ((), ())),
                preferred_element_type=jnp.float32,
            )
            two.append((spectrum * scale).reshape(targets, -1, data_ref.shape[0]))
        out_ref[:, pair, :, rows] = jnp.concatenate(two, axis=1).astype(jnp.bfloat16)


def rim_kernel(snap_ref, out_ref):
    rows = snap_ref.shape[0]
    half = RIM - LANES
    out_ref[:rows] = snap_ref[:, :LANES].astype(jnp.bfloat16)
    rest = snap_ref[:, LANES:]
    lane = lax.broadcasted_iota(jnp.int32, (rows // 2, LANES), 1)
    both = jnp.where(lane < half, rest[: rows // 2], pltpu.roll(rest[rows // 2 :], half, 1))
    out_ref[rows:] = both.astype(jnp.bfloat16)


def packed_rim(snapshots):
    rows, _ = snapshots.shape
    return pl.pallas_call(
        rim_kernel,
        grid=(1,),
        in_specs=[pl.BlockSpec((rows, 2 * LANES), lambda s: (0, 0))],
        out_specs=pl.BlockSpec((rows * RIM // LANES, LANES), lambda s: (0, 0)),
        out_shape=jax.ShapeDtypeStruct((rows * RIM // LANES, LANES), jnp.bfloat16),
        compiler_params=pltpu.CompilerParams(vmem_limit_bytes=LARGE),
        name="rim",
    )(snapshots)


def early_kernel(total_rows, delay_ref, table_ref, weight_ref, snap_ref, out_ref, tail_ref, late_table_ref, scale_ref, shifted_ref, data_ref):
    early = 2 * out_ref.shape[1]

    @pl.when(pl.program_id(0) == 0)
    def _():
        table = table_ref[...].astype(jnp.float32)
        for block in range(delay_ref.shape[0]):
            moved = pltpu.roll(table, delay_ref[block], 1).astype(jnp.bfloat16)
            if block < early:
                shifted_ref[block] = moved
            else:
                late_table_ref[block - early] = moved

    data_ref[...] = snap_ref[...].astype(jnp.bfloat16)
    tail_ref[...] = data_ref[:, early * HOP :]
    scale_ref[...] = jnp.sqrt(weight_ref[...] / total_rows)
    fill_pairs(out_ref, slice(None), shifted_ref, data_ref, scale_ref)


def early_spectra(snapshots, weights, block_delay, table, targets, total_rows):
    rows, span = snapshots.shape
    blocks = span // HOP
    early = (span - REACH) // HOP + 1
    lines = 4 * NF // targets
    tail = span - early * HOP
    return pl.pallas_call(
        lambda *refs: early_kernel(total_rows, *refs),
        grid=(rows // STRIP,),
        in_specs=[
            pl.BlockSpec(memory_space=pltpu.SMEM),
            pl.BlockSpec(table.shape, lambda s: (0, 0)),
            pl.BlockSpec((1, STRIP), lambda s: (0, s)),
            pl.BlockSpec((STRIP, span), lambda s: (s, 0)),
        ],
        out_specs=[
            pl.BlockSpec((targets, early // 2, lines, STRIP), lambda s: (0, 0, 0, s)),
            pl.BlockSpec((STRIP, tail), lambda s: (s, 0)),
            pl.BlockSpec((blocks - early,) + table.shape, lambda s: (0, 0, 0)),
            pl.BlockSpec((1, STRIP), lambda s: (0, s)),
        ],
        out_shape=[
            jax.ShapeDtypeStruct((targets, blocks // 2, lines, rows), jnp.bfloat16),
            jax.ShapeDtypeStruct((rows, tail), jnp.bfloat16),
            jax.ShapeDtypeStruct((blocks - early,) + table.shape, jnp.bfloat16),
            jax.ShapeDtypeStruct((1, rows), jnp.float32),
        ],
        scratch_shapes=[
            pltpu.VMEM((early,) + table.shape, jnp.bfloat16),
            pltpu.VMEM((STRIP, span), jnp.bfloat16),
        ],
        compiler_params=pltpu.CompilerParams(vmem_limit_bytes=VMEM),
        cost_estimate=pl.CostEstimate(
            flops=4 * NF * REACH * rows * early,
            bytes_accessed=4 * rows * span + 4 * NF * rows * early,
            transcendentals=0,
        ),
        name="dft_early",
    )(block_delay, table, weights.reshape(1, rows), snapshots)


def late_kernel(table_ref, scale_ref, tail_ref, rim_ref, begun_ref, out_ref, data_ref):
    rows, tail = tail_ref.shape
    strip = data_ref.shape[0]
    rest = rim_ref[rows:].astype(jnp.float32)
    lane = lax.broadcasted_iota(jnp.int32, rest.shape, 1)
    for s in range(rows // strip):
        part = slice(s * strip, (s + 1) * strip)
        mine = rest if s == 0 else pltpu.roll(rest, RIM - LANES, 1)
        mine = jnp.where(lane < RIM - LANES, mine, 0.0).astype(jnp.bfloat16)
        data_ref[:, :tail] = tail_ref[part]
        data_ref[:, tail : tail + LANES] = rim_ref[part]
        data_ref[:, tail + LANES :] = mine
        fill_pairs(out_ref, part, table_ref, data_ref, scale_ref)


def late_spectra(begun, tail, table, scale, rim):
    targets, pairs, lines, rows = begun.shape
    late = table.shape[0]
    whole = pl.BlockSpec(memory_space=pltpu.VMEM)
    return pl.pallas_call(
        late_kernel,
        grid=(1,),
        in_specs=[whole, whole, whole, whole, pl.BlockSpec(memory_space=pl.ANY)],
        out_specs=pl.BlockSpec(
            (targets, late // 2, lines, rows), lambda s: (0, 2 * pairs // late - 1, 0, 0)
        ),
        out_shape=jax.ShapeDtypeStruct(begun.shape, begun.dtype),
        input_output_aliases={4: 0},
        scratch_shapes=[pltpu.VMEM((STRIP, (late - 1) * HOP + REACH), jnp.bfloat16)],
        compiler_params=pltpu.CompilerParams(vmem_limit_bytes=VMEM),
        cost_estimate=pl.CostEstimate(
            flops=4 * NF * REACH * rows * late,
            bytes_accessed=4 * NF * rows * late,
            transcendentals=0,
        ),
        name="dft_late",
    )(table, scale, tail, rim, begun)


def split_quads(mats):
    eights = [m.reshape(m.shape[0] // 8, 8, m.shape[1]) for m in mats]
    upper = lax.broadcasted_iota(jnp.int32, eights[0].shape, 1) < 4
    low, high = [], []
    for a, b in (eights[:2], eights[2:]):
        low.append(jnp.where(upper, a, pltpu.roll(b, 4, 1)))
        high.append(jnp.where(upper, pltpu.roll(a, 4, 1), b))
    return jnp.concatenate(low, axis=1), jnp.concatenate(high, axis=1)


def csd_kernel(got_ref, out_ref, sorted_ref):
    halves, lines, every, rows = sorted_ref.shape
    freqs = lines // 2
    sources = got_ref.shape[0]
    step = 4
    some = step * every // sources
    row = lax.broadcasted_iota(jnp.int32, (some * lines, some * lines), 0)
    column = lax.broadcasted_iota(jnp.int32, (some * lines, some * lines), 1)
    part = (row // some) % 2
    freq = row // (2 * some)
    order = ((row % some) * lines + part * freqs + freq == column).astype(jnp.bfloat16)
    for half in range(halves):
        for k in range(sources // step):
            by_line = lax.dot_general(
                order,
                got_ref[k * step : (k + 1) * step, half].reshape(some * lines, rows),
                (((1,), (0,)), ((), ())),
                preferred_element_type=jnp.float32,
            )
            by_line = by_line.astype(jnp.bfloat16).reshape(lines, some, rows)
            sorted_ref[half, :, k * some : (k + 1) * some, :] = by_line
    real, imag = [], []
    for freq in range(freqs):
        power = 0.0
        for half in range(halves):
            both = sorted_ref[half, 2 * freq : 2 * freq + 2].reshape(2 * every, rows)
            power += lax.dot_general(
                both, both, (((1,), (1,)), ((), ())), preferred_element_type=jnp.float32
            )
        real.append(power[:every, :every] + power[every:, every:])
        imag.append(power[:every, every:] - power[every:, :every])
    for place, quad in ((0, real), (16, imag)):
        low, high = split_quads(quad)
        out_ref[:, 0, place : place + 16, :] = low.astype(jnp.bfloat16)
        out_ref[:, 1, place : place + 16, :] = high.astype(jnp.bfloat16)


def cross_power(got):
    sources, _, pairs, lines, rows = got.shape
    every = sources * 2 * pairs
    shape = (every // 8, 2, 2 * lines, every)
    whole = pl.BlockSpec(memory_space=pltpu.VMEM)
    return pl.pallas_call(
        csd_kernel,
        in_specs=[whole],
        out_specs=whole,
        out_shape=jax.ShapeDtypeStruct(shape, jnp.bfloat16),
        scratch_shapes=[pltpu.VMEM((PAIR, lines // 2, every, rows), jnp.bfloat16)],
        compiler_params=pltpu.CompilerParams(vmem_limit_bytes=VMEM),
        name="csd",
    )(got)


def total_kernel(got_ref, out_ref, sum_ref):
    own, parts, freqs, _ = out_ref.shape
    sum_ref[...] = jnp.sum(got_ref[...].astype(jnp.float32), axis=1)
    few = freqs // PAIR
    for half in range(PAIR):
        for part in range(parts):
            for freq in range(few):
                for i in range(own):
                    row = (part * few + freq) * own + i
                    place = half * few + freq
                    out_ref[i, part, place : place + 1, :] = sum_ref[half, row : row + 1, :]


def totals(got, freqs):
    halves, _, lines, every = got.shape
    whole = pl.BlockSpec(memory_space=pltpu.VMEM)
    return pl.pallas_call(
        total_kernel,
        in_specs=[whole],
        out_specs=whole,
        out_shape=jax.ShapeDtypeStruct((lines * halves // (2 * freqs), 2, freqs, every), jnp.float32),
        scratch_shapes=[pltpu.VMEM((halves, lines, every), jnp.float32)],
        compiler_params=pltpu.CompilerParams(vmem_limit_bytes=VMEM),
        name="total",
    )(got)


def body(snapshots, weights, block_delay):
    groups = lax.axis_size("tm")
    others = lax.axis_size("other")
    targets = PAIR * groups
    total_rows = snapshots.shape[0] * others * PAIR

    def exchange(array, axes):
        return lax.all_to_all(array, axes, split_axis=0, concat_axis=0, tiled=True)

    rim = shifted(packed_rim(snapshots), "tm", -1)
    begun = early_spectra(snapshots, weights, block_delay, dft_rows(groups), targets, total_rows)
    spectra = late_spectra(*begun, rim)
    received = exchange(spectra, ("tm", "half"))
    partial_csd = cross_power(received.reshape((groups, PAIR) + received.shape[1:]))
    lines, every = partial_csd.shape[2:]
    got = exchange(partial_csd.reshape(others * PAIR, lines, every), ("half", "other"))
    return totals(got.reshape(PAIR, others, lines, every), NF // groups)


def solution(mesh):
    rows, groups = mesh.devices.shape
    by_half = Mesh(mesh.devices.reshape(PAIR, rows // PAIR, groups), ("half", "other", "tm"))
    row = ("half", "other")
    return jax.shard_map(
        body,
        mesh=by_half,
        in_specs=(P(row, "tm"), P(row), P("tm")),
        out_specs=P(row, None, "tm", None),
        check_vma=False,
    )
```

```python
import jax
import jax.numpy as jnp
import numpy as np
from jax import lax
from jax.experimental import pallas as pl
from jax.experimental.pallas import tpu as pltpu
from jax.sharding import Mesh
from jax.sharding import PartitionSpec as P

NFFT = 256
NF = 128
HOP = 128
RIM = 192
REACH = 384
STRIP = 256
PAIR = 2
CORES = 2
LANES = 128
VMEM = 24 * 1024 * 1024
LARGE = 56 * 1024 * 1024


def shifted(array, axis, by):
    count = lax.axis_size(axis)
    return lax.ppermute(array, axis, [(i, (i + by) % count) for i in range(count)])


def dft_rows(groups):
    time_index = np.arange(NFFT)
    angles = 2.0 * np.pi * (time_index[:, None] * np.arange(NF)[None, :] % NFFT) / NFFT
    window = np.sin(np.pi * time_index / NFFT) ** 2
    norm = np.sqrt(np.sum(window * window))
    table = np.stack([window[:, None] * np.cos(angles), -window[:, None] * np.sin(angles)])
    table = (table / norm).reshape(2, NFFT, groups, PAIR, NF // groups // PAIR)
    rows = table.transpose(3, 2, 0, 4, 1).reshape(2 * NF, NFFT)
    rows = np.pad(rows, ((0, 0), (0, REACH - NFFT)))
    return jnp.asarray(rows, jnp.float32).astype(jnp.bfloat16)


def fill_pairs(out_ref, rows, table_ref, data_ref, scale_ref):
    targets = out_ref.shape[0]
    scale = scale_ref[:, rows]
    for pair in range(table_ref.shape[0] // 2):
        two = []
        for block in (2 * pair, 2 * pair + 1):
            spectrum = lax.dot_general(
                table_ref[block],
                data_ref[:, block * HOP : block * HOP + REACH],
                (((1,), (1,)), ((), ())),
                preferred_element_type=jnp.float32,
            )
            two.append((spectrum * scale).reshape(targets, -1, data_ref.shape[0]))
        out_ref[:, pair, :, rows] = jnp.concatenate(two, axis=1).astype(jnp.bfloat16)


def rim_kernel(snap_ref, out_ref):
    rows = snap_ref.shape[0]
    half = RIM - LANES
    out_ref[:rows] = snap_ref[:, :LANES].astype(jnp.bfloat16)
    rest = snap_ref[:, LANES:]
    lane = lax.broadcasted_iota(jnp.int32, (rows // 2, LANES), 1)
    both = jnp.where(lane < half, rest[: rows // 2], pltpu.roll(rest[rows // 2 :], half, 1))
    out_ref[rows:] = both.astype(jnp.bfloat16)


def packed_rim(snapshots):
    rows, _ = snapshots.shape
    return pl.pallas_call(
        rim_kernel,
        grid=(1,),
        in_specs=[pl.BlockSpec((rows, 2 * LANES), lambda s: (0, 0))],
        out_specs=pl.BlockSpec((rows * RIM // LANES, LANES), lambda s: (0, 0)),
        out_shape=jax.ShapeDtypeStruct((rows * RIM // LANES, LANES), jnp.bfloat16),
        compiler_params=pltpu.CompilerParams(vmem_limit_bytes=LARGE),
        name="rim",
    )(snapshots)


def early_kernel(total_rows, delay_ref, table_ref, weight_ref, snap_ref, out_ref, tail_ref, late_table_ref, scale_ref, shifted_ref, data_ref):
    early = 2 * out_ref.shape[1]

    @pl.when(pl.program_id(0) == 0)
    def _():
        table = table_ref[...].astype(jnp.float32)
        for block in range(delay_ref.shape[0]):
            moved = pltpu.roll(table, delay_ref[block], 1).astype(jnp.bfloat16)
            if block < early:
                shifted_ref[block] = moved
            else:
                late_table_ref[block - early] = moved

    data_ref[...] = snap_ref[...].astype(jnp.bfloat16)
    tail_ref[...] = data_ref[:, early * HOP :]
    scale_ref[...] = jnp.sqrt(weight_ref[...] / total_rows)
    fill_pairs(out_ref, slice(None), shifted_ref, data_ref, scale_ref)


def early_spectra(snapshots, weights, block_delay, table, targets, total_rows):
    rows, span = snapshots.shape
    blocks = span // HOP
    early = (span - REACH) // HOP + 1
    lines = 4 * NF // targets
    tail = span - early * HOP
    return pl.pallas_call(
        lambda *refs: early_kernel(total_rows, *refs),
        grid=(rows // STRIP,),
        in_specs=[
            pl.BlockSpec(memory_space=pltpu.SMEM),
            pl.BlockSpec(table.shape, lambda s: (0, 0)),
            pl.BlockSpec((1, STRIP), lambda s: (0, s)),
            pl.BlockSpec((STRIP, span), lambda s: (s, 0)),
        ],
        out_specs=[
            pl.BlockSpec((targets, early // 2, lines, STRIP), lambda s: (0, 0, 0, s)),
            pl.BlockSpec((STRIP, tail), lambda s: (s, 0)),
            pl.BlockSpec((blocks - early,) + table.shape, lambda s: (0, 0, 0)),
            pl.BlockSpec((1, STRIP), lambda s: (0, s)),
        ],
        out_shape=[
            jax.ShapeDtypeStruct((targets, blocks // 2, lines, rows), jnp.bfloat16),
            jax.ShapeDtypeStruct((rows, tail), jnp.bfloat16),
            jax.ShapeDtypeStruct((blocks - early,) + table.shape, jnp.bfloat16),
            jax.ShapeDtypeStruct((1, rows), jnp.float32),
        ],
        scratch_shapes=[
            pltpu.VMEM((early,) + table.shape, jnp.bfloat16),
            pltpu.VMEM((STRIP, span), jnp.bfloat16),
        ],
        compiler_params=pltpu.CompilerParams(vmem_limit_bytes=VMEM),
        cost_estimate=pl.CostEstimate(
            flops=4 * NF * REACH * rows * early,
            bytes_accessed=4 * rows * span + 4 * NF * rows * early,
            transcendentals=0,
        ),
        name="dft_early",
    )(block_delay, table, weights.reshape(1, rows), snapshots)


def late_kernel(table_ref, scale_ref, tail_ref, rim_ref, begun_ref, out_ref, data_ref):
    rows, tail = tail_ref.shape
    strip = data_ref.shape[0]
    rest = rim_ref[rows:].astype(jnp.float32)
    lane = lax.broadcasted_iota(jnp.int32, rest.shape, 1)
    for s in range(rows // strip):
        part = slice(s * strip, (s + 1) * strip)
        mine = rest if s == 0 else pltpu.roll(rest, RIM - LANES, 1)
        mine = jnp.where(lane < RIM - LANES, mine, 0.0).astype(jnp.bfloat16)
        data_ref[:, :tail] = tail_ref[part]
        data_ref[:, tail : tail + LANES] = rim_ref[part]
        data_ref[:, tail + LANES :] = mine
        fill_pairs(out_ref, part, table_ref, data_ref, scale_ref)


def late_spectra(begun, tail, table, scale, rim):
    targets, pairs, lines, rows = begun.shape
    late = table.shape[0]
    whole = pl.BlockSpec(memory_space=pltpu.VMEM)
    return pl.pallas_call(
        late_kernel,
        grid=(1,),
        in_specs=[whole, whole, whole, whole, pl.BlockSpec(memory_space=pl.ANY)],
        out_specs=pl.BlockSpec(
            (targets, late // 2, lines, rows), lambda s: (0, 2 * pairs // late - 1, 0, 0)
        ),
        out_shape=jax.ShapeDtypeStruct(begun.shape, begun.dtype),
        input_output_aliases={4: 0},
        scratch_shapes=[pltpu.VMEM((STRIP, (late - 1) * HOP + REACH), jnp.bfloat16)],
        compiler_params=pltpu.CompilerParams(vmem_limit_bytes=VMEM),
        cost_estimate=pl.CostEstimate(
            flops=4 * NF * REACH * rows * late,
            bytes_accessed=4 * NF * rows * late,
            transcendentals=0,
        ),
        name="dft_late",
    )(table, scale, tail, rim, begun)


def split_quads(mats):
    eights = [m.reshape(m.shape[0] // 8, 8, m.shape[1]) for m in mats]
    upper = lax.broadcasted_iota(jnp.int32, eights[0].shape, 1) < 4
    low, high = [], []
    for a, b in (eights[:2], eights[2:]):
        low.append(jnp.where(upper, a, pltpu.roll(b, 4, 1)))
        high.append(jnp.where(upper, pltpu.roll(a, 4, 1), b))
    return jnp.concatenate(low, axis=1), jnp.concatenate(high, axis=1)


def csd_kernel(got_ref, own_ref, other_ref, sorted_ref):
    halves, lines, every, rows = sorted_ref.shape
    freqs = lines // 2
    sources = got_ref.shape[0] // halves
    step = 4
    some = step * every // sources
    row = lax.broadcasted_iota(jnp.int32, (some * lines, some * lines), 0)
    column = lax.broadcasted_iota(jnp.int32, (some * lines, some * lines), 1)
    part = (row // some) % 2
    freq = row // (2 * some)
    order = ((row % some) * lines + part * freqs + freq == column).astype(jnp.bfloat16)
    for half in range(halves):
        for k in range(sources // step):
            first = half * sources + k * step
            by_line = lax.dot_general(
                order,
                got_ref[first : first + step].reshape(some * lines, rows),
                (((1,), (0,)), ((), ())),
                preferred_element_type=jnp.float32,
            )
            by_line = by_line.astype(jnp.bfloat16).reshape(lines, some, rows)
            sorted_ref[half, :, k * some : (k + 1) * some, :] = by_line
    real, imag = [], []
    for freq in range(freqs):
        power = 0.0
        for half in range(halves):
            both = sorted_ref[half, 2 * freq : 2 * freq + 2].reshape(2 * every, rows)
            power += lax.dot_general(
                both, both, (((1,), (1,)), ((), ())), preferred_element_type=jnp.float32
            )
        real.append(power[:every, :every] + power[every:, every:])
        imag.append(power[:every, every:] - power[every:, :every])
    first_core = lax.axis_index("core") == 0
    for place, quad in ((0, real), (16, imag)):
        low, high = split_quads(quad)
        own_ref[:, place : place + 16, :] = jnp.where(first_core, low, high)
        other = jnp.where(first_core, high, low)
        other_ref[:, place : place + 16, :] = other.astype(jnp.bfloat16)


def cross_power(got):
    sources, pairs, lines, rows = got.shape
    every = sources // PAIR * 2 * pairs
    shape = (every // 8, 2 * lines, every)
    whole = pl.BlockSpec(memory_space=pltpu.VMEM)
    return pl.pallas_call(
        csd_kernel,
        in_specs=[whole],
        out_specs=[whole, whole],
        out_shape=[
            jax.ShapeDtypeStruct(shape, jnp.float32),
            jax.ShapeDtypeStruct(shape, jnp.bfloat16),
        ],
        scratch_shapes=[pltpu.VMEM((PAIR, lines // 2, every, rows), jnp.bfloat16)],
        compiler_params=pltpu.CompilerParams(vmem_limit_bytes=VMEM),
        name="csd",
    )(got)


def total_kernel(got_ref, out_ref, sum_ref):
    own, parts, freqs, _ = out_ref.shape
    sum_ref[...] = jnp.sum(got_ref[...].astype(jnp.float32), axis=1)
    few = freqs // PAIR
    for half in range(PAIR):
        for part in range(parts):
            for freq in range(few):
                for i in range(own):
                    row = (part * few + freq) * own + i
                    place = half * few + freq
                    out_ref[i, part, place : place + 1, :] = sum_ref[half, row : row + 1, :]


def totals(got, freqs):
    halves, _, lines, every = got.shape
    whole = pl.BlockSpec(memory_space=pltpu.VMEM)
    return pl.pallas_call(
        total_kernel,
        in_specs=[whole],
        out_specs=whole,
        out_shape=jax.ShapeDtypeStruct((lines * halves // (2 * freqs), 2, freqs, every), jnp.float32),
        scratch_shapes=[pltpu.VMEM((halves, lines, every), jnp.float32)],
        compiler_params=pltpu.CompilerParams(vmem_limit_bytes=VMEM),
        name="total",
    )(got)


def body(snapshots, weights, block_delay):
    groups = lax.axis_size("tm")
    chips = lax.axis_size("chip")
    targets = PAIR * groups
    total_rows = snapshots.shape[0] * PAIR * chips * CORES

    def exchange(array, axes):
        return lax.all_to_all(array, axes, split_axis=0, concat_axis=0, tiled=True)

    rim = shifted(packed_rim(snapshots), "tm", -1)
    begun = early_spectra(snapshots, weights, block_delay, dft_rows(groups), targets, total_rows)
    spectra = late_spectra(*begun, rim)
    own, other = cross_power(exchange(spectra, ("half", "tm")))
    pair = (own + shifted(other, "core", 1).astype(jnp.float32)).astype(jnp.bfloat16)
    got = exchange(pair, ("half", "chip"))
    return totals(got.reshape((PAIR, chips) + got.shape[1:]), NF // groups)


def solution(mesh):
    rows, groups = mesh.devices.shape
    row = ("half", "chip", "core")
    split = Mesh(
        mesh.devices.reshape(PAIR, rows // PAIR // CORES, CORES, groups), row + ("tm",)
    )
    return jax.shard_map(
        body,
        mesh=split,
        in_specs=(P(row, "tm"), P(row), P("tm")),
        out_specs=P(row, None, "tm", None),
        check_vma=False,
    )
```

```python
import jax
import jax.numpy as jnp
import numpy as np
from jax import lax
from jax.experimental import pallas as pl
from jax.experimental.pallas import tpu as pltpu
from jax.sharding import Mesh
from jax.sharding import PartitionSpec as P

NFFT = 256
NF = 128
HOP = 128
RIM = 192
REACH = 384
STRIP = 256
PAIR = 2
CORES = 2
LANES = 128
CHUNK = 128
VMEM = 24 * 1024 * 1024
LARGE = 56 * 1024 * 1024


def shifted(array, axis, by):
    count = lax.axis_size(axis)
    return lax.ppermute(array, axis, [(i, (i + by) % count) for i in range(count)])


def dft_rows(groups):
    time_index = np.arange(NFFT)
    angles = 2.0 * np.pi * (time_index[:, None] * np.arange(NF)[None, :] % NFFT) / NFFT
    window = np.sin(np.pi * time_index / NFFT) ** 2
    norm = np.sqrt(np.sum(window * window))
    table = np.stack([window[:, None] * np.cos(angles), -window[:, None] * np.sin(angles)])
    table = (table / norm).reshape(2, NFFT, groups, PAIR, NF // groups // PAIR)
    rows = table.transpose(3, 2, 0, 4, 1).reshape(2 * NF, NFFT)
    rows = np.pad(rows, ((0, 0), (0, REACH - NFFT)))
    return jnp.asarray(rows, jnp.float32).astype(jnp.bfloat16)


def fill_pairs(out_ref, rows, table_ref, data_ref, scale_ref):
    targets = out_ref.shape[0]
    scale = scale_ref[:, rows]
    for pair in range(table_ref.shape[0] // 2):
        two = []
        for block in (2 * pair, 2 * pair + 1):
            spectrum = lax.dot_general(
                table_ref[block],
                data_ref[:, block * HOP : block * HOP + REACH],
                (((1,), (1,)), ((), ())),
                preferred_element_type=jnp.float32,
            )
            two.append((spectrum * scale).reshape(targets, -1, data_ref.shape[0]))
        out_ref[:, pair, :, rows] = jnp.concatenate(two, axis=1).astype(jnp.bfloat16)


def rim_kernel(snap_ref, out_ref):
    rows = snap_ref.shape[0]
    half = RIM - LANES
    out_ref[:rows] = snap_ref[:, :LANES].astype(jnp.bfloat16)
    rest = snap_ref[:, LANES:]
    lane = lax.broadcasted_iota(jnp.int32, (rows // 2, LANES), 1)
    both = jnp.where(lane < half, rest[: rows // 2], pltpu.roll(rest[rows // 2 :], half, 1))
    out_ref[rows:] = both.astype(jnp.bfloat16)


def packed_rim(snapshots):
    rows, _ = snapshots.shape
    packed = CHUNK * RIM // LANES
    return pl.pallas_call(
        rim_kernel,
        grid=(rows // CHUNK,),
        in_specs=[pl.BlockSpec((CHUNK, 2 * LANES), lambda s: (s, 0))],
        out_specs=pl.BlockSpec((packed, LANES), lambda s: (s, 0)),
        out_shape=jax.ShapeDtypeStruct((rows * RIM // LANES, LANES), jnp.bfloat16),
        compiler_params=pltpu.CompilerParams(vmem_limit_bytes=LARGE),
        name="rim",
    )(snapshots)


def early_kernel(total_rows, delay_ref, table_ref, weight_ref, snap_ref, out_ref, tail_ref, late_table_ref, scale_ref, shifted_ref, data_ref):
    early = 2 * out_ref.shape[1]

    @pl.when(pl.program_id(0) == 0)
    def _():
        table = table_ref[...].astype(jnp.float32)
        for block in range(delay_ref.shape[0]):
            moved = pltpu.roll(table, delay_ref[block], 1).astype(jnp.bfloat16)
            if block < early:
                shifted_ref[block] = moved
            else:
                late_table_ref[block - early] = moved

    data_ref[...] = snap_ref[...].astype(jnp.bfloat16)
    tail_ref[...] = data_ref[:, early * HOP :]
    scale_ref[...] = jnp.sqrt(weight_ref[...] / total_rows)
    fill_pairs(out_ref, slice(None), shifted_ref, data_ref, scale_ref)


def early_spectra(snapshots, weights, block_delay, table, targets, total_rows):
    rows, span = snapshots.shape
    blocks = span // HOP
    early = (span - REACH) // HOP + 1
    lines = 4 * NF // targets
    tail = span - early * HOP
    return pl.pallas_call(
        lambda *refs: early_kernel(total_rows, *refs),
        grid=(rows // STRIP,),
        in_specs=[
            pl.BlockSpec(memory_space=pltpu.SMEM),
            pl.BlockSpec(table.shape, lambda s: (0, 0)),
            pl.BlockSpec((1, STRIP), lambda s: (0, s)),
            pl.BlockSpec((STRIP, span), lambda s: (s, 0)),
        ],
        out_specs=[
            pl.BlockSpec((targets, early // 2, lines, STRIP), lambda s: (0, 0, 0, s)),
            pl.BlockSpec((STRIP, tail), lambda s: (s, 0)),
            pl.BlockSpec((blocks - early,) + table.shape, lambda s: (0, 0, 0)),
            pl.BlockSpec((1, STRIP), lambda s: (0, s)),
        ],
        out_shape=[
            jax.ShapeDtypeStruct((targets, blocks // 2, lines, rows), jnp.bfloat16),
            jax.ShapeDtypeStruct((rows, tail), jnp.bfloat16),
            jax.ShapeDtypeStruct((blocks - early,) + table.shape, jnp.bfloat16),
            jax.ShapeDtypeStruct((1, rows), jnp.float32),
        ],
        scratch_shapes=[
            pltpu.VMEM((early,) + table.shape, jnp.bfloat16),
            pltpu.VMEM((STRIP, span), jnp.bfloat16),
        ],
        compiler_params=pltpu.CompilerParams(vmem_limit_bytes=VMEM),
        cost_estimate=pl.CostEstimate(
            flops=4 * NF * REACH * rows * early,
            bytes_accessed=4 * rows * span + 4 * NF * rows * early,
            transcendentals=0,
        ),
        name="dft_early",
    )(block_delay, table, weights.reshape(1, rows), snapshots)


def late_kernel(table_ref, scale_ref, tail_ref, rim_ref, begun_ref, out_ref, data_ref):
    rows, tail = tail_ref.shape
    half = CHUNK // 2
    packed = CHUNK * RIM // LANES
    lane = lax.broadcasted_iota(jnp.int32, (half, LANES), 1)
    strip = data_ref.shape[0]
    for s in range(rows // strip):
        part = slice(s * strip, (s + 1) * strip)
        data_ref[:, :tail] = tail_ref[part]
        for k in range(strip // CHUNK):
            here = (s * strip // CHUNK + k) * packed
            both = rim_ref[here + CHUNK : here + packed].astype(jnp.float32)
            for j, mine in enumerate((both, pltpu.roll(both, RIM - LANES, 1))):
                mine = jnp.where(lane < RIM - LANES, mine, 0.0).astype(jnp.bfloat16)
                data_ref[k * CHUNK + j * half : k * CHUNK + (j + 1) * half, tail + LANES :] = mine
            data_ref[k * CHUNK : (k + 1) * CHUNK, tail : tail + LANES] = rim_ref[here : here + CHUNK]
        fill_pairs(out_ref, part, table_ref, data_ref, scale_ref)


def late_spectra(begun, tail, table, scale, rim):
    targets, pairs, lines, rows = begun.shape
    late = table.shape[0]
    whole = pl.BlockSpec(memory_space=pltpu.VMEM)
    return pl.pallas_call(
        late_kernel,
        grid=(1,),
        in_specs=[whole, whole, whole, whole, pl.BlockSpec(memory_space=pl.ANY)],
        out_specs=pl.BlockSpec(
            (targets, late // 2, lines, rows), lambda s: (0, 2 * pairs // late - 1, 0, 0)
        ),
        out_shape=jax.ShapeDtypeStruct(begun.shape, begun.dtype),
        input_output_aliases={4: 0},
        scratch_shapes=[pltpu.VMEM((STRIP, (late - 1) * HOP + REACH), jnp.bfloat16)],
        compiler_params=pltpu.CompilerParams(vmem_limit_bytes=VMEM),
        cost_estimate=pl.CostEstimate(
            flops=4 * NF * REACH * rows * late,
            bytes_accessed=4 * NF * rows * late,
            transcendentals=0,
        ),
        name="dft_late",
    )(table, scale, tail, rim, begun)


def split_quads(mats):
    eights = [m.reshape(m.shape[0] // 8, 8, m.shape[1]) for m in mats]
    upper = lax.broadcasted_iota(jnp.int32, eights[0].shape, 1) < 4
    low, high = [], []
    for a, b in (eights[:2], eights[2:]):
        low.append(jnp.where(upper, a, pltpu.roll(b, 4, 1)))
        high.append(jnp.where(upper, pltpu.roll(a, 4, 1), b))
    return jnp.concatenate(low, axis=1), jnp.concatenate(high, axis=1)


def csd_kernel(got_ref, own_ref, other_ref, sorted_ref):
    halves, lines, every, rows = sorted_ref.shape
    freqs = lines // 2
    sources = got_ref.shape[0] // halves
    step = 4
    some = step * every // sources
    row = lax.broadcasted_iota(jnp.int32, (some * lines, some * lines), 0)
    column = lax.broadcasted_iota(jnp.int32, (some * lines, some * lines), 1)
    part = (row // some) % 2
    freq = row // (2 * some)
    order = ((row % some) * lines + part * freqs + freq == column).astype(jnp.bfloat16)
    for half in range(halves):
        for k in range(sources // step):
            first = half * sources + k * step
            by_line = lax.dot_general(
                order,
                got_ref[first : first + step].reshape(some * lines, rows),
                (((1,), (0,)), ((), ())),
                preferred_element_type=jnp.float32,
            )
            by_line = by_line.astype(jnp.bfloat16).reshape(lines, some, rows)
            sorted_ref[half, :, k * some : (k + 1) * some, :] = by_line
    real, imag = [], []
    for freq in range(freqs):
        power = 0.0
        for half in range(halves):
            both = sorted_ref[half, 2 * freq : 2 * freq + 2].reshape(2 * every, rows)
            power += lax.dot_general(
                both, both, (((1,), (1,)), ((), ())), preferred_element_type=jnp.float32
            )
        real.append(power[:every, :every] + power[every:, every:])
        imag.append(power[:every, every:] - power[every:, :every])
    first_core = lax.axis_index("core") == 0
    for place, quad in ((0, real), (16, imag)):
        low, high = split_quads(quad)
        own_ref[:, place : place + 16, :] = jnp.where(first_core, low, high)
        other = jnp.where(first_core, high, low)
        other_ref[:, place : place + 16, :] = other.astype(jnp.bfloat16)


def cross_power(got):
    sources, pairs, lines, rows = got.shape
    every = sources // PAIR * 2 * pairs
    shape = (every // 8, 2 * lines, every)
    whole = pl.BlockSpec(memory_space=pltpu.VMEM)
    return pl.pallas_call(
        csd_kernel,
        in_specs=[whole],
        out_specs=[whole, whole],
        out_shape=[
            jax.ShapeDtypeStruct(shape, jnp.float32),
            jax.ShapeDtypeStruct(shape, jnp.bfloat16),
        ],
        scratch_shapes=[pltpu.VMEM((PAIR, lines // 2, every, rows), jnp.bfloat16)],
        compiler_params=pltpu.CompilerParams(vmem_limit_bytes=VMEM),
        name="csd",
    )(got)


def total_kernel(got_ref, out_ref, sum_ref):
    own, parts, freqs, _ = out_ref.shape
    sum_ref[...] = jnp.sum(got_ref[...].astype(jnp.float32), axis=1)
    few = freqs // PAIR
    for half in range(PAIR):
        for part in range(parts):
            for freq in range(few):
                for i in range(own):
                    row = (part * few + freq) * own + i
                    place = half * few + freq
                    out_ref[i, part, place : place + 1, :] = sum_ref[half, row : row + 1, :]


def totals(got, freqs):
    halves, _, lines, every = got.shape
    whole = pl.BlockSpec(memory_space=pltpu.VMEM)
    return pl.pallas_call(
        total_kernel,
        in_specs=[whole],
        out_specs=whole,
        out_shape=jax.ShapeDtypeStruct((lines * halves // (2 * freqs), 2, freqs, every), jnp.float32),
        scratch_shapes=[pltpu.VMEM((halves, lines, every), jnp.float32)],
        compiler_params=pltpu.CompilerParams(vmem_limit_bytes=VMEM),
        name="total",
    )(got)


def body(snapshots, weights, block_delay):
    groups = lax.axis_size("tm")
    chips = lax.axis_size("chip")
    targets = PAIR * groups
    total_rows = snapshots.shape[0] * PAIR * chips * CORES

    def exchange(array, axes):
        return lax.all_to_all(array, axes, split_axis=0, concat_axis=0, tiled=True)

    rim = shifted(packed_rim(snapshots), "tm", -1)
    begun = early_spectra(snapshots, weights, block_delay, dft_rows(groups), targets, total_rows)
    spectra = late_spectra(*begun, rim)
    own, other = cross_power(exchange(spectra, ("half", "tm")))
    pair = (own + shifted(other, "core", 1).astype(jnp.float32)).astype(jnp.bfloat16)
    got = exchange(pair, ("half", "chip"))
    return totals(got.reshape((PAIR, chips) + got.shape[1:]), NF // groups)


def solution(mesh):
    rows, groups = mesh.devices.shape
    row = ("half", "chip", "core")
    split = Mesh(
        mesh.devices.reshape(PAIR, rows // PAIR // CORES, CORES, groups), row + ("tm",)
    )
    return jax.shard_map(
        body,
        mesh=split,
        in_specs=(P(row, "tm"), P(row), P("tm")),
        out_specs=P(row, None, "tm", None),
        check_vma=False,
    )
```

```python
import jax
import jax.numpy as jnp
import numpy as np
from jax import lax
from jax.experimental import pallas as pl
from jax.experimental.pallas import tpu as pltpu
from jax.sharding import Mesh
from jax.sharding import PartitionSpec as P

NFFT = 256
NF = 128
HOP = 128
RIM = 192
REACH = 384
STRIP = 256
PAIR = 2
CORES = 2
LANES = 128
VMEM = 24 * 1024 * 1024


def shifted(array, axis, by):
    count = lax.axis_size(axis)
    return lax.ppermute(array, axis, [(i, (i + by) % count) for i in range(count)])


def dft_rows(groups):
    time_index = np.arange(NFFT)
    angles = 2.0 * np.pi * (time_index[:, None] * np.arange(NF)[None, :] % NFFT) / NFFT
    window = np.sin(np.pi * time_index / NFFT) ** 2
    norm = np.sqrt(np.sum(window * window))
    table = np.stack([window[:, None] * np.cos(angles), -window[:, None] * np.sin(angles)])
    table = (table / norm).reshape(2, NFFT, groups, PAIR, NF // groups // PAIR)
    rows = table.transpose(3, 2, 0, 4, 1).reshape(2 * NF, NFFT)
    rows = np.pad(rows, ((0, 0), (0, REACH - NFFT)))
    return jnp.asarray(rows, jnp.float32).astype(jnp.bfloat16)


def fill_pairs(out_ref, rows, table_ref, data_ref, scale_ref):
    targets = out_ref.shape[0]
    scale = scale_ref[:, rows]
    for pair in range(table_ref.shape[0] // 2):
        two = []
        for block in (2 * pair, 2 * pair + 1):
            spectrum = lax.dot_general(
                table_ref[block],
                data_ref[:, block * HOP : block * HOP + REACH],
                (((1,), (1,)), ((), ())),
                preferred_element_type=jnp.float32,
            )
            two.append((spectrum * scale).reshape(targets, -1, data_ref.shape[0]))
        out_ref[:, pair, :, rows] = jnp.concatenate(two, axis=1).astype(jnp.bfloat16)


def rim_kernel(edge_ref, out_ref):
    rows = edge_ref.shape[0]
    out_ref[:rows] = edge_ref[:, :LANES]
    rest = edge_ref[:, LANES:].astype(jnp.float32)
    both = jnp.concatenate([rest[: rows // 2], rest[rows // 2 :]], axis=1)
    out_ref[rows:] = both.astype(jnp.bfloat16)


def packed_rim(edge):
    rows, _ = edge.shape
    whole = pl.BlockSpec(memory_space=pltpu.VMEM)
    return pl.pallas_call(
        rim_kernel,
        in_specs=[whole],
        out_specs=whole,
        out_shape=jax.ShapeDtypeStruct((rows * RIM // LANES, LANES), jnp.bfloat16),
        compiler_params=pltpu.CompilerParams(vmem_limit_bytes=VMEM),
        name="rim",
    )(edge)


def early_kernel(total_rows, delay_ref, table_ref, weight_ref, snap_ref, out_ref, tail_ref, late_table_ref, scale_ref, shifted_ref, data_ref):
    early = 2 * out_ref.shape[1]

    @pl.when(pl.program_id(0) == 0)
    def _():
        table = table_ref[...].astype(jnp.float32)
        for block in range(delay_ref.shape[0]):
            moved = pltpu.roll(table, delay_ref[block], 1).astype(jnp.bfloat16)
            if block < early:
                shifted_ref[block] = moved
            else:
                late_table_ref[block - early] = moved

    data_ref[...] = snap_ref[...].astype(jnp.bfloat16)
    tail_ref[...] = data_ref[:, early * HOP :]
    scale_ref[...] = jnp.sqrt(weight_ref[...] / total_rows)
    fill_pairs(out_ref, slice(None), shifted_ref, data_ref, scale_ref)


def early_spectra(snapshots, weights, block_delay, table, targets, total_rows):
    rows, span = snapshots.shape
    blocks = span // HOP
    early = (span - REACH) // HOP + 1
    lines = 4 * NF // targets
    tail = span - early * HOP
    return pl.pallas_call(
        lambda *refs: early_kernel(total_rows, *refs),
        grid=(rows // STRIP,),
        in_specs=[
            pl.BlockSpec(memory_space=pltpu.SMEM),
            pl.BlockSpec(table.shape, lambda s: (0, 0)),
            pl.BlockSpec((1, STRIP), lambda s: (0, s)),
            pl.BlockSpec((STRIP, span), lambda s: (s, 0)),
        ],
        out_specs=[
            pl.BlockSpec((targets, early // 2, lines, STRIP), lambda s: (0, 0, 0, s)),
            pl.BlockSpec((STRIP, tail), lambda s: (s, 0)),
            pl.BlockSpec((blocks - early,) + table.shape, lambda s: (0, 0, 0)),
            pl.BlockSpec((1, STRIP), lambda s: (0, s)),
        ],
        out_shape=[
            jax.ShapeDtypeStruct((targets, blocks // 2, lines, rows), jnp.bfloat16),
            jax.ShapeDtypeStruct((rows, tail), jnp.bfloat16),
            jax.ShapeDtypeStruct((blocks - early,) + table.shape, jnp.bfloat16),
            jax.ShapeDtypeStruct((1, rows), jnp.float32),
        ],
        scratch_shapes=[
            pltpu.VMEM((early,) + table.shape, jnp.bfloat16),
            pltpu.VMEM((STRIP, span), jnp.bfloat16),
        ],
        compiler_params=pltpu.CompilerParams(vmem_limit_bytes=VMEM),
        cost_estimate=pl.CostEstimate(
            flops=4 * NF * REACH * rows * early,
            bytes_accessed=4 * rows * span + 4 * NF * rows * early,
            transcendentals=0,
        ),
        name="dft_early",
    )(block_delay, table, weights.reshape(1, rows), snapshots)


def late_kernel(table_ref, scale_ref, tail_ref, rim_ref, begun_ref, out_ref, data_ref):
    rows, tail = tail_ref.shape
    strip = data_ref.shape[0]
    rest = rim_ref[rows:].astype(jnp.float32)
    lane = lax.broadcasted_iota(jnp.int32, rest.shape, 1)
    for s in range(rows // strip):
        part = slice(s * strip, (s + 1) * strip)
        mine = rest if s == 0 else pltpu.roll(rest, RIM - LANES, 1)
        mine = jnp.where(lane < RIM - LANES, mine, 0.0).astype(jnp.bfloat16)
        data_ref[:, :tail] = tail_ref[part]
        data_ref[:, tail : tail + LANES] = rim_ref[part]
        data_ref[:, tail + LANES :] = mine
        fill_pairs(out_ref, part, table_ref, data_ref, scale_ref)


def late_spectra(begun, tail, table, scale, rim):
    targets, pairs, lines, rows = begun.shape
    late = table.shape[0]
    whole = pl.BlockSpec(memory_space=pltpu.VMEM)
    return pl.pallas_call(
        late_kernel,
        grid=(1,),
        in_specs=[whole, whole, whole, whole, pl.BlockSpec(memory_space=pl.ANY)],
        out_specs=pl.BlockSpec(
            (targets, late // 2, lines, rows), lambda s: (0, 2 * pairs // late - 1, 0, 0)
        ),
        out_shape=jax.ShapeDtypeStruct(begun.shape, begun.dtype),
        input_output_aliases={4: 0},
        scratch_shapes=[pltpu.VMEM((STRIP, (late - 1) * HOP + REACH), jnp.bfloat16)],
        compiler_params=pltpu.CompilerParams(vmem_limit_bytes=VMEM),
        cost_estimate=pl.CostEstimate(
            flops=4 * NF * REACH * rows * late,
            bytes_accessed=4 * NF * rows * late,
            transcendentals=0,
        ),
        name="dft_late",
    )(table, scale, tail, rim, begun)


def split_quads(mats):
    eights = [m.reshape(m.shape[0] // 8, 8, m.shape[1]) for m in mats]
    upper = lax.broadcasted_iota(jnp.int32, eights[0].shape, 1) < 4
    low, high = [], []
    for a, b in (eights[:2], eights[2:]):
        low.append(jnp.where(upper, a, pltpu.roll(b, 4, 1)))
        high.append(jnp.where(upper, pltpu.roll(a, 4, 1), b))
    return jnp.concatenate(low, axis=1), jnp.concatenate(high, axis=1)


def csd_kernel(got_ref, own_ref, other_ref, sorted_ref):
    halves, lines, every, rows = sorted_ref.shape
    freqs = lines // 2
    sources = got_ref.shape[0] // halves
    step = 4
    some = step * every // sources
    row = lax.broadcasted_iota(jnp.int32, (some * lines, some * lines), 0)
    column = lax.broadcasted_iota(jnp.int32, (some * lines, some * lines), 1)
    part = (row // some) % 2
    freq = row // (2 * some)
    order = ((row % some) * lines + part * freqs + freq == column).astype(jnp.bfloat16)
    for half in range(halves):
        for k in range(sources // step):
            first = half * sources + k * step
            by_line = lax.dot_general(
                order,
                got_ref[first : first + step].reshape(some * lines, rows),
                (((1,), (0,)), ((), ())),
                preferred_element_type=jnp.float32,
            )
            by_line = by_line.astype(jnp.bfloat16).reshape(lines, some, rows)
            sorted_ref[half, :, k * some : (k + 1) * some, :] = by_line
    real, imag = [], []
    for freq in range(freqs):
        power = 0.0
        for half in range(halves):
            both = sorted_ref[half, 2 * freq : 2 * freq + 2].reshape(2 * every, rows)
            power += lax.dot_general(
                both, both, (((1,), (1,)), ((), ())), preferred_element_type=jnp.float32
            )
        real.append(power[:every, :every] + power[every:, every:])
        imag.append(power[:every, every:] - power[every:, :every])
    first_core = lax.axis_index("core") == 0
    for place, quad in ((0, real), (16, imag)):
        low, high = split_quads(quad)
        own_ref[:, place : place + 16, :] = jnp.where(first_core, low, high)
        other = jnp.where(first_core, high, low)
        other_ref[:, place : place + 16, :] = other.astype(jnp.bfloat16)


def cross_power(got):
    sources, pairs, lines, rows = got.shape
    every = sources // PAIR * 2 * pairs
    shape = (every // 8, 2 * lines, every)
    whole = pl.BlockSpec(memory_space=pltpu.VMEM)
    return pl.pallas_call(
        csd_kernel,
        in_specs=[whole],
        out_specs=[whole, whole],
        out_shape=[
            jax.ShapeDtypeStruct(shape, jnp.float32),
            jax.ShapeDtypeStruct(shape, jnp.bfloat16),
        ],
        scratch_shapes=[pltpu.VMEM((PAIR, lines // 2, every, rows), jnp.bfloat16)],
        compiler_params=pltpu.CompilerParams(vmem_limit_bytes=VMEM),
        name="csd",
    )(got)


def total_kernel(got_ref, out_ref, sum_ref):
    own, parts, freqs, _ = out_ref.shape
    sum_ref[...] = jnp.sum(got_ref[...].astype(jnp.float32), axis=1)
    few = freqs // PAIR
    for half in range(PAIR):
        for part in range(parts):
            for freq in range(few):
                for i in range(own):
                    row = (part * few + freq) * own + i
                    place = half * few + freq
                    out_ref[i, part, place : place + 1, :] = sum_ref[half, row : row + 1, :]


def totals(got, freqs):
    halves, _, lines, every = got.shape
    whole = pl.BlockSpec(memory_space=pltpu.VMEM)
    return pl.pallas_call(
        total_kernel,
        in_specs=[whole],
        out_specs=whole,
        out_shape=jax.ShapeDtypeStruct((lines * halves // (2 * freqs), 2, freqs, every), jnp.float32),
        scratch_shapes=[pltpu.VMEM((halves, lines, every), jnp.float32)],
        compiler_params=pltpu.CompilerParams(vmem_limit_bytes=VMEM),
        name="total",
    )(got)


def body(snapshots, weights, block_delay):
    groups = lax.axis_size("tm")
    chips = lax.axis_size("chip")
    targets = PAIR * groups
    total_rows = snapshots.shape[0] * PAIR * chips * CORES

    def exchange(array, axes):
        return lax.all_to_all(array, axes, split_axis=0, concat_axis=0, tiled=True)

    rim = shifted(packed_rim(snapshots[:, :RIM].astype(jnp.bfloat16)), "tm", -1)
    begun = early_spectra(snapshots, weights, block_delay, dft_rows(groups), targets, total_rows)
    spectra = late_spectra(*begun, rim)
    own, other = cross_power(exchange(spectra, ("half", "tm")))
    pair = (own + shifted(other, "core", 1).astype(jnp.float32)).astype(jnp.bfloat16)
    got = exchange(pair, ("half", "chip"))
    return totals(got.reshape((PAIR, chips) + got.shape[1:]), NF // groups)


def solution(mesh):
    rows, groups = mesh.devices.shape
    row = ("half", "chip", "core")
    split = Mesh(
        mesh.devices.reshape(PAIR, rows // PAIR // CORES, CORES, groups), row + ("tm",)
    )
    return jax.shard_map(
        body,
        mesh=split,
        in_specs=(P(row, "tm"), P(row), P("tm")),
        out_specs=P(row, None, "tm", None),
        check_vma=False,
    )
```

```python
import jax
import jax.numpy as jnp
import numpy as np
from jax import lax
from jax.experimental import pallas as pl
from jax.experimental.pallas import tpu as pltpu
from jax.sharding import Mesh
from jax.sharding import PartitionSpec as P

NFFT = 256
NF = 128
HOP = 128
RIM = 192
REACH = 384
STRIP = 256
PAIR = 2
CORES = 2
SORTED = 256
LANES = 128
VMEM = 24 * 1024 * 1024


def shifted(array, axis, by):
    count = lax.axis_size(axis)
    return lax.ppermute(array, axis, [(i, (i + by) % count) for i in range(count)])


def dft_rows(groups):
    time_index = np.arange(NFFT)
    angles = 2.0 * np.pi * (time_index[:, None] * np.arange(NF)[None, :] % NFFT) / NFFT
    window = np.sin(np.pi * time_index / NFFT) ** 2
    norm = np.sqrt(np.sum(window * window))
    table = np.stack([window[:, None] * np.cos(angles), -window[:, None] * np.sin(angles)])
    table = (table / norm).reshape(2, NFFT, groups, PAIR, NF // groups // PAIR)
    rows = table.transpose(3, 2, 0, 4, 1).reshape(2 * NF, NFFT)
    rows = np.pad(rows, ((0, 0), (0, REACH - NFFT)))
    return jnp.asarray(rows, jnp.float32).astype(jnp.bfloat16)


def fill_pairs(out_ref, rows, table_ref, data_ref, scale_ref):
    targets = out_ref.shape[0]
    scale = scale_ref[:, rows]
    for pair in range(table_ref.shape[0] // 2):
        two = []
        for block in (2 * pair, 2 * pair + 1):
            spectrum = lax.dot_general(
                table_ref[block],
                data_ref[:, block * HOP : block * HOP + REACH],
                (((1,), (1,)), ((), ())),
                preferred_element_type=jnp.float32,
            )
            two.append((spectrum * scale).reshape(targets, -1, data_ref.shape[0]))
        out_ref[:, pair, :, rows] = jnp.concatenate(two, axis=1).astype(jnp.bfloat16)


def rim_kernel(edge_ref, out_ref):
    rows = edge_ref.shape[0]
    out_ref[:rows] = edge_ref[:, :LANES]
    rest = edge_ref[:, LANES:].astype(jnp.float32)
    both = jnp.concatenate([rest[: rows // 2], rest[rows // 2 :]], axis=1)
    out_ref[rows:] = both.astype(jnp.bfloat16)


def packed_rim(edge):
    rows, _ = edge.shape
    whole = pl.BlockSpec(memory_space=pltpu.VMEM)
    return pl.pallas_call(
        rim_kernel,
        in_specs=[whole],
        out_specs=whole,
        out_shape=jax.ShapeDtypeStruct((rows * RIM // LANES, LANES), jnp.bfloat16),
        compiler_params=pltpu.CompilerParams(vmem_limit_bytes=VMEM),
        name="rim",
    )(edge)


def sorting_matrix(size, lines):
    some, freqs = size // lines, lines // 2
    row = lax.broadcasted_iota(jnp.int32, (size, size), 0)
    column = lax.broadcasted_iota(jnp.int32, (size, size), 1)
    part = (row // some) % 2
    freq = row // (2 * some)
    return ((row % some) * lines + part * freqs + freq == column).astype(jnp.bfloat16)


def early_kernel(total_rows, delay_ref, table_ref, weight_ref, snap_ref, out_ref, tail_ref, late_table_ref, scale_ref, order_ref, shifted_ref, data_ref):
    early = 2 * out_ref.shape[1]

    @pl.when(pl.program_id(0) == 0)
    def _():
        order_ref[...] = sorting_matrix(order_ref.shape[0], out_ref.shape[2] // 2)
        table = table_ref[...].astype(jnp.float32)
        for block in range(delay_ref.shape[0]):
            moved = pltpu.roll(table, delay_ref[block], 1).astype(jnp.bfloat16)
            if block < early:
                shifted_ref[block] = moved
            else:
                late_table_ref[block - early] = moved

    data_ref[...] = snap_ref[...].astype(jnp.bfloat16)
    tail_ref[...] = data_ref[:, early * HOP :]
    scale_ref[...] = jnp.sqrt(weight_ref[...] / total_rows)
    fill_pairs(out_ref, slice(None), shifted_ref, data_ref, scale_ref)


def early_spectra(snapshots, weights, block_delay, table, targets, total_rows):
    rows, span = snapshots.shape
    blocks = span // HOP
    early = (span - REACH) // HOP + 1
    lines = 4 * NF // targets
    tail = span - early * HOP
    return pl.pallas_call(
        lambda *refs: early_kernel(total_rows, *refs),
        grid=(rows // STRIP,),
        in_specs=[
            pl.BlockSpec(memory_space=pltpu.SMEM),
            pl.BlockSpec(table.shape, lambda s: (0, 0)),
            pl.BlockSpec((1, STRIP), lambda s: (0, s)),
            pl.BlockSpec((STRIP, span), lambda s: (s, 0)),
        ],
        out_specs=[
            pl.BlockSpec((targets, early // 2, lines, STRIP), lambda s: (0, 0, 0, s)),
            pl.BlockSpec((STRIP, tail), lambda s: (s, 0)),
            pl.BlockSpec((blocks - early,) + table.shape, lambda s: (0, 0, 0)),
            pl.BlockSpec((1, STRIP), lambda s: (0, s)),
            pl.BlockSpec((SORTED, SORTED), lambda s: (0, 0)),
        ],
        out_shape=[
            jax.ShapeDtypeStruct((targets, blocks // 2, lines, rows), jnp.bfloat16),
            jax.ShapeDtypeStruct((rows, tail), jnp.bfloat16),
            jax.ShapeDtypeStruct((blocks - early,) + table.shape, jnp.bfloat16),
            jax.ShapeDtypeStruct((1, rows), jnp.float32),
            jax.ShapeDtypeStruct((SORTED, SORTED), jnp.bfloat16),
        ],
        scratch_shapes=[
            pltpu.VMEM((early,) + table.shape, jnp.bfloat16),
            pltpu.VMEM((STRIP, span), jnp.bfloat16),
        ],
        compiler_params=pltpu.CompilerParams(vmem_limit_bytes=VMEM),
        cost_estimate=pl.CostEstimate(
            flops=4 * NF * REACH * rows * early,
            bytes_accessed=4 * rows * span + 4 * NF * rows * early,
            transcendentals=0,
        ),
        name="dft_early",
    )(block_delay, table, weights.reshape(1, rows), snapshots)


def late_kernel(table_ref, scale_ref, tail_ref, rim_ref, begun_ref, out_ref, data_ref):
    rows, tail = tail_ref.shape
    strip = data_ref.shape[0]
    rest = rim_ref[rows:].astype(jnp.float32)
    lane = lax.broadcasted_iota(jnp.int32, rest.shape, 1)
    for s in range(rows // strip):
        part = slice(s * strip, (s + 1) * strip)
        mine = rest if s == 0 else pltpu.roll(rest, RIM - LANES, 1)
        mine = jnp.where(lane < RIM - LANES, mine, 0.0).astype(jnp.bfloat16)
        data_ref[:, :tail] = tail_ref[part]
        data_ref[:, tail : tail + LANES] = rim_ref[part]
        data_ref[:, tail + LANES :] = mine
        fill_pairs(out_ref, part, table_ref, data_ref, scale_ref)


def late_spectra(begun, tail, table, scale, rim):
    targets, pairs, lines, rows = begun.shape
    late = table.shape[0]
    whole = pl.BlockSpec(memory_space=pltpu.VMEM)
    return pl.pallas_call(
        late_kernel,
        grid=(1,),
        in_specs=[whole, whole, whole, whole, pl.BlockSpec(memory_space=pl.ANY)],
        out_specs=pl.BlockSpec(
            (targets, late // 2, lines, rows), lambda s: (0, 2 * pairs // late - 1, 0, 0)
        ),
        out_shape=jax.ShapeDtypeStruct(begun.shape, begun.dtype),
        input_output_aliases={4: 0},
        scratch_shapes=[pltpu.VMEM((STRIP, (late - 1) * HOP + REACH), jnp.bfloat16)],
        compiler_params=pltpu.CompilerParams(vmem_limit_bytes=VMEM),
        cost_estimate=pl.CostEstimate(
            flops=4 * NF * REACH * rows * late,
            bytes_accessed=4 * NF * rows * late,
            transcendentals=0,
        ),
        name="dft_late",
    )(table, scale, tail, rim, begun)


def split_quads(mats):
    eights = [m.reshape(m.shape[0] // 8, 8, m.shape[1]) for m in mats]
    upper = lax.broadcasted_iota(jnp.int32, eights[0].shape, 1) < 4
    low, high = [], []
    for a, b in (eights[:2], eights[2:]):
        low.append(jnp.where(upper, a, pltpu.roll(b, 4, 1)))
        high.append(jnp.where(upper, pltpu.roll(a, 4, 1), b))
    return jnp.concatenate(low, axis=1), jnp.concatenate(high, axis=1)


def csd_kernel(order_ref, got_ref, own_ref, other_ref, sorted_ref):
    lines, every, _ = sorted_ref.shape
    rows = got_ref.shape[3]
    sources = got_ref.shape[0] // PAIR
    some = SORTED // lines
    step = sources * some // every
    for half in range(PAIR):
        for k in range(sources // step):
            first = half * sources + k * step
            by_line = lax.dot_general(
                order_ref[...],
                got_ref[first : first + step].reshape(some * lines, rows),
                (((1,), (0,)), ((), ())),
                preferred_element_type=jnp.float32,
            )
            by_line = by_line.astype(jnp.bfloat16).reshape(lines, some, rows)
            sorted_ref[:, k * some : (k + 1) * some, half * rows : (half + 1) * rows] = by_line
    real, imag = [], []
    for freq in range(lines // 2):
        both = sorted_ref[2 * freq : 2 * freq + 2].reshape(2 * every, PAIR * rows)
        power = lax.dot_general(
            both, both, (((1,), (1,)), ((), ())), preferred_element_type=jnp.float32
        )
        real.append(power[:every, :every] + power[every:, every:])
        imag.append(power[:every, every:] - power[every:, :every])
    first_core = lax.axis_index("core") == 0
    for place, quad in ((0, real), (16, imag)):
        low, high = split_quads(quad)
        own_ref[:, place : place + 16, :] = jnp.where(first_core, low, high)
        other = jnp.where(first_core, high, low)
        other_ref[:, place : place + 16, :] = other.astype(jnp.bfloat16)


def cross_power(order, got):
    sources, pairs, lines, rows = got.shape
    every = sources // PAIR * 2 * pairs
    shape = (every // 8, 2 * lines, every)
    whole = pl.BlockSpec(memory_space=pltpu.VMEM)
    return pl.pallas_call(
        csd_kernel,
        in_specs=[whole, whole],
        out_specs=[whole, whole],
        out_shape=[
            jax.ShapeDtypeStruct(shape, jnp.float32),
            jax.ShapeDtypeStruct(shape, jnp.bfloat16),
        ],
        scratch_shapes=[pltpu.VMEM((lines // 2, every, PAIR * rows), jnp.bfloat16)],
        compiler_params=pltpu.CompilerParams(vmem_limit_bytes=VMEM),
        name="csd",
    )(order, got)


def total_kernel(got_ref, out_ref, sum_ref):
    own, parts, freqs, _ = out_ref.shape
    sum_ref[...] = jnp.sum(got_ref[...].astype(jnp.float32), axis=1)
    few = freqs // PAIR
    for half in range(PAIR):
        for part in range(parts):
            for freq in range(few):
                for i in range(own):
                    row = (part * few + freq) * own + i
                    place = half * few + freq
                    out_ref[i, part, place : place + 1, :] = sum_ref[half, row : row + 1, :]


def totals(got, freqs):
    halves, _, lines, every = got.shape
    whole = pl.BlockSpec(memory_space=pltpu.VMEM)
    return pl.pallas_call(
        total_kernel,
        in_specs=[whole],
        out_specs=whole,
        out_shape=jax.ShapeDtypeStruct((lines * halves // (2 * freqs), 2, freqs, every), jnp.float32),
        scratch_shapes=[pltpu.VMEM((halves, lines, every), jnp.float32)],
        compiler_params=pltpu.CompilerParams(vmem_limit_bytes=VMEM),
        name="total",
    )(got)


def body(snapshots, weights, block_delay):
    groups = lax.axis_size("tm")
    chips = lax.axis_size("chip")
    targets = PAIR * groups
    total_rows = snapshots.shape[0] * PAIR * chips * CORES

    def exchange(array, axes):
        return lax.all_to_all(array, axes, split_axis=0, concat_axis=0, tiled=True)

    rim = shifted(packed_rim(snapshots[:, :RIM].astype(jnp.bfloat16)), "tm", -1)
    *begun, order = early_spectra(
        snapshots, weights, block_delay, dft_rows(groups), targets, total_rows
    )
    spectra = late_spectra(*begun, rim)
    own, other = cross_power(order, exchange(spectra, ("half", "tm")))
    pair = (own + shifted(other, "core", 1).astype(jnp.float32)).astype(jnp.bfloat16)
    got = exchange(pair, ("half", "chip"))
    return totals(got.reshape((PAIR, chips) + got.shape[1:]), NF // groups)


def solution(mesh):
    rows, groups = mesh.devices.shape
    row = ("half", "chip", "core")
    split = Mesh(
        mesh.devices.reshape(PAIR, rows // PAIR // CORES, CORES, groups), row + ("tm",)
    )
    return jax.shard_map(
        body,
        mesh=split,
        in_specs=(P(row, "tm"), P(row), P("tm")),
        out_specs=P(row, None, "tm", None),
        check_vma=False,
    )
```

```python
import jax
import jax.numpy as jnp
import numpy as np
from jax import lax
from jax.experimental import pallas as pl
from jax.experimental.pallas import tpu as pltpu
from jax.sharding import Mesh
from jax.sharding import PartitionSpec as P

NFFT = 256
NF = 128
HOP = 128
RIM = 192
REACH = 384
STRIP = 256
PAIR = 2
CORES = 2
SORTED = 256
LANES = 128
VMEM = 24 * 1024 * 1024


def shifted(array, axis, by):
    count = lax.axis_size(axis)
    return lax.ppermute(array, axis, [(i, (i + by) % count) for i in range(count)])


def dft_rows(groups):
    time_index = np.arange(NFFT)
    angles = 2.0 * np.pi * (time_index[:, None] * np.arange(NF)[None, :] % NFFT) / NFFT
    window = np.sin(np.pi * time_index / NFFT) ** 2
    norm = np.sqrt(np.sum(window * window))
    table = np.stack([window[:, None] * np.cos(angles), -window[:, None] * np.sin(angles)])
    table = (table / norm).reshape(2, NFFT, groups, PAIR, NF // groups // PAIR)
    rows = table.transpose(2, 3, 0, 4, 1).reshape(2 * NF, NFFT)
    rows = np.pad(rows, ((0, 0), (0, REACH - NFFT)))
    return jnp.asarray(rows, jnp.float32).astype(jnp.bfloat16)


def fill_pairs(out_ref, rows, table_ref, data_ref, scale_ref):
    targets = out_ref.shape[0]
    scale = scale_ref[:, rows]
    for pair in range(table_ref.shape[0] // 2):
        two = []
        for block in (2 * pair, 2 * pair + 1):
            spectrum = lax.dot_general(
                table_ref[block],
                data_ref[:, block * HOP : block * HOP + REACH],
                (((1,), (1,)), ((), ())),
                preferred_element_type=jnp.float32,
            )
            two.append((spectrum * scale).reshape(targets, -1, data_ref.shape[0]))
        out_ref[:, pair, :, rows] = jnp.concatenate(two, axis=1).astype(jnp.bfloat16)


def rim_kernel(edge_ref, out_ref):
    rows = edge_ref.shape[0]
    out_ref[:rows] = edge_ref[:, :LANES]
    rest = edge_ref[:, LANES:].astype(jnp.float32)
    both = jnp.concatenate([rest[: rows // 2], rest[rows // 2 :]], axis=1)
    out_ref[rows:] = both.astype(jnp.bfloat16)


def packed_rim(edge):
    rows, _ = edge.shape
    whole = pl.BlockSpec(memory_space=pltpu.VMEM)
    return pl.pallas_call(
        rim_kernel,
        in_specs=[whole],
        out_specs=whole,
        out_shape=jax.ShapeDtypeStruct((rows * RIM // LANES, LANES), jnp.bfloat16),
        compiler_params=pltpu.CompilerParams(vmem_limit_bytes=VMEM),
        name="rim",
    )(edge)


def sorting_matrix(size, lines):
    some, freqs = size // lines, lines // 2
    row = lax.broadcasted_iota(jnp.int32, (size, size), 0)
    column = lax.broadcasted_iota(jnp.int32, (size, size), 1)
    part = (row // some) % 2
    freq = row // (2 * some)
    return ((row % some) * lines + part * freqs + freq == column).astype(jnp.bfloat16)


def early_kernel(total_rows, delay_ref, table_ref, weight_ref, snap_ref, out_ref, tail_ref, late_table_ref, scale_ref, order_ref, shifted_ref, data_ref):
    early = 2 * out_ref.shape[1]

    @pl.when(pl.program_id(0) == 0)
    def _():
        order_ref[...] = sorting_matrix(order_ref.shape[0], out_ref.shape[2] // 2)
        table = table_ref[...].astype(jnp.float32)
        for block in range(delay_ref.shape[0]):
            moved = pltpu.roll(table, delay_ref[block], 1).astype(jnp.bfloat16)
            if block < early:
                shifted_ref[block] = moved
            else:
                late_table_ref[block - early] = moved

    data_ref[...] = snap_ref[...].astype(jnp.bfloat16)
    tail_ref[...] = data_ref[:, early * HOP :]
    scale_ref[...] = jnp.sqrt(weight_ref[...] / total_rows)
    fill_pairs(out_ref, slice(None), shifted_ref, data_ref, scale_ref)


def early_spectra(snapshots, weights, block_delay, table, targets, total_rows):
    rows, span = snapshots.shape
    blocks = span // HOP
    early = (span - REACH) // HOP + 1
    lines = 4 * NF // targets
    tail = span - early * HOP
    return pl.pallas_call(
        lambda *refs: early_kernel(total_rows, *refs),
        grid=(rows // STRIP,),
        in_specs=[
            pl.BlockSpec(memory_space=pltpu.SMEM),
            pl.BlockSpec(table.shape, lambda s: (0, 0)),
            pl.BlockSpec((1, STRIP), lambda s: (0, s)),
            pl.BlockSpec((STRIP, span), lambda s: (s, 0)),
        ],
        out_specs=[
            pl.BlockSpec((targets, early // 2, lines, STRIP), lambda s: (0, 0, 0, s)),
            pl.BlockSpec((STRIP, tail), lambda s: (s, 0)),
            pl.BlockSpec((blocks - early,) + table.shape, lambda s: (0, 0, 0)),
            pl.BlockSpec((1, STRIP), lambda s: (0, s)),
            pl.BlockSpec((SORTED, SORTED), lambda s: (0, 0)),
        ],
        out_shape=[
            jax.ShapeDtypeStruct((targets, blocks // 2, lines, rows), jnp.bfloat16),
            jax.ShapeDtypeStruct((rows, tail), jnp.bfloat16),
            jax.ShapeDtypeStruct((blocks - early,) + table.shape, jnp.bfloat16),
            jax.ShapeDtypeStruct((1, rows), jnp.float32),
            jax.ShapeDtypeStruct((SORTED, SORTED), jnp.bfloat16),
        ],
        scratch_shapes=[
            pltpu.VMEM((early,) + table.shape, jnp.bfloat16),
            pltpu.VMEM((STRIP, span), jnp.bfloat16),
        ],
        compiler_params=pltpu.CompilerParams(vmem_limit_bytes=VMEM),
        cost_estimate=pl.CostEstimate(
            flops=4 * NF * REACH * rows * early,
            bytes_accessed=4 * rows * span + 4 * NF * rows * early,
            transcendentals=0,
        ),
        name="dft_early",
    )(block_delay, table, weights.reshape(1, rows), snapshots)


def late_kernel(table_ref, scale_ref, tail_ref, rim_ref, begun_ref, out_ref):
    rows, _ = tail_ref.shape
    half = RIM - LANES
    rest = rim_ref[rows:].astype(jnp.float32)
    lane = lax.broadcasted_iota(jnp.int32, (rows, LANES), 1)
    last = jnp.concatenate([rest, pltpu.roll(rest, half, 1)], axis=0)
    last = jnp.where(lane < half, last, 0.0).astype(jnp.bfloat16)
    pieces = [tail_ref[:, :HOP], tail_ref[:, HOP:], rim_ref[:rows], last]
    two = []
    for block in range(table_ref.shape[0]):
        products = lax.dot_general(
            table_ref[block],
            jnp.concatenate(pieces[block : block + REACH // HOP], axis=1),
            (((1,), (1,)), ((), ())),
            preferred_element_type=jnp.float32,
        )
        two.append((products * scale_ref[...]).reshape(out_ref.shape[0], -1, rows))
    out_ref[:, 0] = jnp.concatenate(two, axis=1).astype(jnp.bfloat16)


def late_spectra(begun, tail, table, scale, rim):
    targets, pairs, lines, rows = begun.shape
    late = table.shape[0]
    whole = pl.BlockSpec(memory_space=pltpu.VMEM)
    return pl.pallas_call(
        late_kernel,
        grid=(1,),
        in_specs=[whole, whole, whole, whole, pl.BlockSpec(memory_space=pl.ANY)],
        out_specs=pl.BlockSpec(
            (targets, late // 2, lines, rows), lambda s: (0, 2 * pairs // late - 1, 0, 0)
        ),
        out_shape=jax.ShapeDtypeStruct(begun.shape, begun.dtype),
        input_output_aliases={4: 0},
        compiler_params=pltpu.CompilerParams(vmem_limit_bytes=VMEM),
        cost_estimate=pl.CostEstimate(
            flops=4 * NF * REACH * rows * late,
            bytes_accessed=4 * NF * rows * late,
            transcendentals=0,
        ),
        name="dft_late",
    )(table, scale, tail, rim, begun)


def split_quads(mats):
    eights = [m.reshape(m.shape[0] // 8, 8, m.shape[1]) for m in mats]
    upper = lax.broadcasted_iota(jnp.int32, eights[0].shape, 1) < 4
    low, high = [], []
    for a, b in (eights[:2], eights[2:]):
        low.append(jnp.where(upper, a, pltpu.roll(b, 4, 1)))
        high.append(jnp.where(upper, pltpu.roll(a, 4, 1), b))
    return jnp.concatenate(low, axis=1), jnp.concatenate(high, axis=1)


def csd_kernel(order_ref, got_ref, own_ref, other_ref, sorted_ref):
    lines, every, _ = sorted_ref.shape
    sources, _, _, _, rows = got_ref.shape
    some = SORTED // lines
    step = sources * some // every
    for half in range(PAIR):
        for k in range(sources // step):
            by_line = lax.dot_general(
                order_ref[...],
                got_ref[k * step : (k + 1) * step, half].reshape(some * lines, rows),
                (((1,), (0,)), ((), ())),
                preferred_element_type=jnp.float32,
            )
            by_line = by_line.astype(jnp.bfloat16).reshape(lines, some, rows)
            sorted_ref[:, k * some : (k + 1) * some, half * rows : (half + 1) * rows] = by_line
    real, imag = [], []
    for freq in range(lines // 2):
        both = sorted_ref[2 * freq : 2 * freq + 2].reshape(2 * every, PAIR * rows)
        power = lax.dot_general(
            both, both, (((1,), (1,)), ((), ())), preferred_element_type=jnp.float32
        )
        real.append(power[:every, :every] + power[every:, every:])
        imag.append(power[:every, every:] - power[every:, :every])
    first_core = lax.axis_index("core") == 0
    for place, quad in ((0, real), (16, imag)):
        low, high = split_quads(quad)
        own_ref[:, place : place + 16, :] = jnp.where(first_core, low, high)
        other = jnp.where(first_core, high, low)
        other_ref[:, place : place + 16, :] = other.astype(jnp.bfloat16)


def cross_power(order, got):
    sources, _, pairs, lines, rows = got.shape
    every = sources * 2 * pairs
    shape = (every // 8, 2 * lines, every)
    whole = pl.BlockSpec(memory_space=pltpu.VMEM)
    return pl.pallas_call(
        csd_kernel,
        in_specs=[whole, whole],
        out_specs=[whole, whole],
        out_shape=[
            jax.ShapeDtypeStruct(shape, jnp.float32),
            jax.ShapeDtypeStruct(shape, jnp.bfloat16),
        ],
        scratch_shapes=[pltpu.VMEM((lines // 2, every, PAIR * rows), jnp.bfloat16)],
        compiler_params=pltpu.CompilerParams(vmem_limit_bytes=VMEM),
        name="csd",
    )(order, got)


def total_kernel(got_ref, out_ref, sum_ref):
    own, parts, freqs, _ = out_ref.shape
    sum_ref[...] = jnp.sum(got_ref[...].astype(jnp.float32), axis=1)
    few = freqs // PAIR
    for half in range(PAIR):
        for part in range(parts):
            for freq in range(few):
                for i in range(own):
                    row = (part * few + freq) * own + i
                    place = half * few + freq
                    out_ref[i, part, place : place + 1, :] = sum_ref[half, row : row + 1, :]


def totals(got, freqs):
    halves, _, lines, every = got.shape
    whole = pl.BlockSpec(memory_space=pltpu.VMEM)
    return pl.pallas_call(
        total_kernel,
        in_specs=[whole],
        out_specs=whole,
        out_shape=jax.ShapeDtypeStruct((lines * halves // (2 * freqs), 2, freqs, every), jnp.float32),
        scratch_shapes=[pltpu.VMEM((halves, lines, every), jnp.float32)],
        compiler_params=pltpu.CompilerParams(vmem_limit_bytes=VMEM),
        name="total",
    )(got)


def body(snapshots, weights, block_delay):
    groups = lax.axis_size("tm")
    chips = lax.axis_size("chip")
    targets = PAIR * groups
    total_rows = snapshots.shape[0] * PAIR * chips * CORES

    def exchange(array, axes):
        return lax.all_to_all(array, axes, split_axis=0, concat_axis=0, tiled=True)

    rim = shifted(packed_rim(snapshots[:, :RIM].astype(jnp.bfloat16)), "tm", -1)
    *begun, order = early_spectra(
        snapshots, weights, block_delay, dft_rows(groups), targets, total_rows
    )
    spectra = late_spectra(*begun, rim)
    received = exchange(spectra, ("tm", "half"))
    received = received.reshape((groups, PAIR) + received.shape[1:])
    own, other = cross_power(order, received)
    pair = (own + shifted(other, "core", 1).astype(jnp.float32)).astype(jnp.bfloat16)
    got = exchange(pair, ("half", "chip"))
    return totals(got.reshape((PAIR, chips) + got.shape[1:]), NF // groups)


def solution(mesh):
    rows, groups = mesh.devices.shape
    row = ("half", "chip", "core")
    split = Mesh(
        mesh.devices.reshape(PAIR, rows // PAIR // CORES, CORES, groups), row + ("tm",)
    )
    return jax.shard_map(
        body,
        mesh=split,
        in_specs=(P(row, "tm"), P(row), P("tm")),
        out_specs=P(row, None, "tm", None),
        check_vma=False,
    )
```

```python
import jax
import jax.numpy as jnp
import numpy as np
from jax import lax
from jax.experimental import pallas as pl
from jax.experimental.pallas import tpu as pltpu
from jax.sharding import Mesh
from jax.sharding import PartitionSpec as P

NFFT = 256
NF = 128
HOP = 128
RIM = 192
REACH = 384
STRIP = 256
PAIR = 2
CORES = 2
LANES = 128
VMEM = 24 * 1024 * 1024


def shifted(array, axis, by):
    count = lax.axis_size(axis)
    return lax.ppermute(array, axis, [(i, (i + by) % count) for i in range(count)])


def dft_rows(groups):
    time_index = np.arange(NFFT)
    angles = 2.0 * np.pi * (time_index[:, None] * np.arange(NF)[None, :] % NFFT) / NFFT
    window = np.sin(np.pi * time_index / NFFT) ** 2
    norm = np.sqrt(np.sum(window * window))
    table = np.stack([window[:, None] * np.cos(angles), -window[:, None] * np.sin(angles)])
    table = (table / norm).reshape(2, NFFT, groups, PAIR, NF // groups // PAIR)
    rows = table.transpose(3, 2, 0, 4, 1).reshape(2 * NF, NFFT)
    rows = np.pad(rows, ((0, 0), (0, REACH - NFFT)))
    return jnp.asarray(rows, jnp.float32).astype(jnp.bfloat16)


def fill_pairs(out_ref, rows, table_ref, data_ref, scale_ref):
    targets = out_ref.shape[0]
    scale = scale_ref[:, rows]
    for pair in range(table_ref.shape[0] // 2):
        two = []
        for block in (2 * pair, 2 * pair + 1):
            spectrum = lax.dot_general(
                table_ref[block],
                data_ref[:, block * HOP : block * HOP + REACH],
                (((1,), (1,)), ((), ())),
                preferred_element_type=jnp.float32,
            )
            two.append((spectrum * scale).reshape(targets, -1, data_ref.shape[0]))
        out_ref[:, pair, :, rows] = jnp.concatenate(two, axis=1).astype(jnp.bfloat16)


def rim_kernel(edge_ref, out_ref):
    rows = edge_ref.shape[0]
    out_ref[:rows] = edge_ref[:, :LANES].astype(jnp.bfloat16)
    rest = edge_ref[:, LANES:]
    half = RIM - LANES
    lane = lax.broadcasted_iota(jnp.int32, (rows // 2, LANES), 1)
    both = jnp.where(lane < half, rest[: rows // 2], pltpu.roll(rest[rows // 2 :], half, 1))
    out_ref[rows:] = both.astype(jnp.bfloat16)


def packed_rim(edge):
    rows, _ = edge.shape
    whole = pl.BlockSpec(memory_space=pltpu.VMEM)
    return pl.pallas_call(
        rim_kernel,
        in_specs=[whole],
        out_specs=whole,
        out_shape=jax.ShapeDtypeStruct((rows * RIM // LANES, LANES), jnp.bfloat16),
        compiler_params=pltpu.CompilerParams(vmem_limit_bytes=VMEM),
        name="rim",
    )(edge)


def early_kernel(total_rows, delay_ref, table_ref, weight_ref, snap_ref, out_ref, tail_ref, late_table_ref, scale_ref, shifted_ref, data_ref):
    early = 2 * out_ref.shape[1]

    @pl.when(pl.program_id(0) == 0)
    def _():
        table = table_ref[...].astype(jnp.float32)
        for block in range(delay_ref.shape[0]):
            moved = pltpu.roll(table, delay_ref[block], 1).astype(jnp.bfloat16)
            if block < early:
                shifted_ref[block] = moved
            else:
                late_table_ref[block - early] = moved

    data_ref[...] = snap_ref[...].astype(jnp.bfloat16)
    tail_ref[...] = data_ref[:, early * HOP :]
    scale_ref[...] = jnp.sqrt(weight_ref[...] / total_rows)
    fill_pairs(out_ref, slice(None), shifted_ref, data_ref, scale_ref)


def early_spectra(snapshots, weights, block_delay, table, targets, total_rows):
    rows, span = snapshots.shape
    blocks = span // HOP
    early = (span - REACH) // HOP + 1
    lines = 4 * NF // targets
    tail = span - early * HOP
    return pl.pallas_call(
        lambda *refs: early_kernel(total_rows, *refs),
        grid=(rows // STRIP,),
        in_specs=[
            pl.BlockSpec(memory_space=pltpu.SMEM),
            pl.BlockSpec(table.shape, lambda s: (0, 0)),
            pl.BlockSpec((1, STRIP), lambda s: (0, s)),
            pl.BlockSpec((STRIP, span), lambda s: (s, 0)),
        ],
        out_specs=[
            pl.BlockSpec((targets, early // 2, lines, STRIP), lambda s: (0, 0, 0, s)),
            pl.BlockSpec((STRIP, tail), lambda s: (s, 0)),
            pl.BlockSpec((blocks - early,) + table.shape, lambda s: (0, 0, 0)),
            pl.BlockSpec((1, STRIP), lambda s: (0, s)),
        ],
        out_shape=[
            jax.ShapeDtypeStruct((targets, blocks // 2, lines, rows), jnp.bfloat16),
            jax.ShapeDtypeStruct((rows, tail), jnp.bfloat16),
            jax.ShapeDtypeStruct((blocks - early,) + table.shape, jnp.bfloat16),
            jax.ShapeDtypeStruct((1, rows), jnp.float32),
        ],
        scratch_shapes=[
            pltpu.VMEM((early,) + table.shape, jnp.bfloat16),
            pltpu.VMEM((STRIP, span), jnp.bfloat16),
        ],
        compiler_params=pltpu.CompilerParams(vmem_limit_bytes=VMEM),
        cost_estimate=pl.CostEstimate(
            flops=4 * NF * REACH * rows * early,
            bytes_accessed=4 * rows * span + 4 * NF * rows * early,
            transcendentals=0,
        ),
        name="dft_early",
    )(block_delay, table, weights.reshape(1, rows), snapshots)


def late_kernel(table_ref, scale_ref, tail_ref, rim_ref, begun_ref, out_ref, data_ref):
    rows, tail = tail_ref.shape
    strip = data_ref.shape[0]
    rest = rim_ref[rows:].astype(jnp.float32)
    lane = lax.broadcasted_iota(jnp.int32, rest.shape, 1)
    for s in range(rows // strip):
        part = slice(s * strip, (s + 1) * strip)
        mine = rest if s == 0 else pltpu.roll(rest, RIM - LANES, 1)
        mine = jnp.where(lane < RIM - LANES, mine, 0.0).astype(jnp.bfloat16)
        data_ref[:, :tail] = tail_ref[part]
        data_ref[:, tail : tail + LANES] = rim_ref[part]
        data_ref[:, tail + LANES :] = mine
        fill_pairs(out_ref, part, table_ref, data_ref, scale_ref)


def late_spectra(begun, tail, table, scale, rim):
    targets, pairs, lines, rows = begun.shape
    late = table.shape[0]
    whole = pl.BlockSpec(memory_space=pltpu.VMEM)
    return pl.pallas_call(
        late_kernel,
        grid=(1,),
        in_specs=[whole, whole, whole, whole, pl.BlockSpec(memory_space=pl.ANY)],
        out_specs=pl.BlockSpec(
            (targets, late // 2, lines, rows), lambda s: (0, 2 * pairs // late - 1, 0, 0)
        ),
        out_shape=jax.ShapeDtypeStruct(begun.shape, begun.dtype),
        input_output_aliases={4: 0},
        scratch_shapes=[pltpu.VMEM((STRIP, (late - 1) * HOP + REACH), jnp.bfloat16)],
        compiler_params=pltpu.CompilerParams(vmem_limit_bytes=VMEM),
        cost_estimate=pl.CostEstimate(
            flops=4 * NF * REACH * rows * late,
            bytes_accessed=4 * NF * rows * late,
            transcendentals=0,
        ),
        name="dft_late",
    )(table, scale, tail, rim, begun)


def split_quads(mats):
    eights = [m.reshape(m.shape[0] // 8, 8, m.shape[1]) for m in mats]
    upper = lax.broadcasted_iota(jnp.int32, eights[0].shape, 1) < 4
    low, high = [], []
    for a, b in (eights[:2], eights[2:]):
        low.append(jnp.where(upper, a, pltpu.roll(b, 4, 1)))
        high.append(jnp.where(upper, pltpu.roll(a, 4, 1), b))
    return jnp.concatenate(low, axis=1), jnp.concatenate(high, axis=1)


def csd_kernel(got_ref, own_ref, other_ref, sorted_ref):
    halves, lines, every, rows = sorted_ref.shape
    freqs = lines // 2
    sources = got_ref.shape[0] // halves
    step = 4
    some = step * every // sources
    row = lax.broadcasted_iota(jnp.int32, (some * lines, some * lines), 0)
    column = lax.broadcasted_iota(jnp.int32, (some * lines, some * lines), 1)
    part = (row // some) % 2
    freq = row // (2 * some)
    order = ((row % some) * lines + part * freqs + freq == column).astype(jnp.bfloat16)
    for half in range(halves):
        for k in range(sources // step):
            first = half * sources + k * step
            by_line = lax.dot_general(
                order,
                got_ref[first : first + step].reshape(some * lines, rows),
                (((1,), (0,)), ((), ())),
                preferred_element_type=jnp.float32,
            )
            by_line = by_line.astype(jnp.bfloat16).reshape(lines, some, rows)
            sorted_ref[half, :, k * some : (k + 1) * some, :] = by_line
    real, imag = [], []
    for freq in range(freqs):
        power = 0.0
        for half in range(halves):
            both = sorted_ref[half, 2 * freq : 2 * freq + 2].reshape(2 * every, rows)
            power += lax.dot_general(
                both, both, (((1,), (1,)), ((), ())), preferred_element_type=jnp.float32
            )
        real.append(power[:every, :every] + power[every:, every:])
        imag.append(power[:every, every:] - power[every:, :every])
    first_core = lax.axis_index("core") == 0
    for place, quad in ((0, real), (16, imag)):
        low, high = split_quads(quad)
        own_ref[:, place : place + 16, :] = jnp.where(first_core, low, high)
        other = jnp.where(first_core, high, low)
        other_ref[:, place : place + 16, :] = other.astype(jnp.bfloat16)


def cross_power(got):
    sources, pairs, lines, rows = got.shape
    every = sources // PAIR * 2 * pairs
    shape = (every // 8, 2 * lines, every)
    whole = pl.BlockSpec(memory_space=pltpu.VMEM)
    return pl.pallas_call(
        csd_kernel,
        in_specs=[whole],
        out_specs=[whole, whole],
        out_shape=[
            jax.ShapeDtypeStruct(shape, jnp.float32),
            jax.ShapeDtypeStruct(shape, jnp.bfloat16),
        ],
        scratch_shapes=[pltpu.VMEM((PAIR, lines // 2, every, rows), jnp.bfloat16)],
        compiler_params=pltpu.CompilerParams(vmem_limit_bytes=VMEM),
        name="csd",
    )(got)


def total_kernel(got_ref, out_ref, sum_ref):
    own, parts, freqs, _ = out_ref.shape
    sum_ref[...] = jnp.sum(got_ref[...].astype(jnp.float32), axis=1)
    few = freqs // PAIR
    for half in range(PAIR):
        for part in range(parts):
            for freq in range(few):
                for i in range(own):
                    row = (part * few + freq) * own + i
                    place = half * few + freq
                    out_ref[i, part, place : place + 1, :] = sum_ref[half, row : row + 1, :]


def totals(got, freqs):
    halves, _, lines, every = got.shape
    whole = pl.BlockSpec(memory_space=pltpu.VMEM)
    return pl.pallas_call(
        total_kernel,
        in_specs=[whole],
        out_specs=whole,
        out_shape=jax.ShapeDtypeStruct((lines * halves // (2 * freqs), 2, freqs, every), jnp.float32),
        scratch_shapes=[pltpu.VMEM((halves, lines, every), jnp.float32)],
        compiler_params=pltpu.CompilerParams(vmem_limit_bytes=VMEM),
        name="total",
    )(got)


def body(snapshots, weights, block_delay):
    groups = lax.axis_size("tm")
    chips = lax.axis_size("chip")
    targets = PAIR * groups
    total_rows = snapshots.shape[0] * PAIR * chips * CORES

    def exchange(array, axes):
        return lax.all_to_all(array, axes, split_axis=0, concat_axis=0, tiled=True)

    rim = shifted(packed_rim(snapshots[:, : 2 * LANES]), "tm", -1)
    begun = early_spectra(snapshots, weights, block_delay, dft_rows(groups), targets, total_rows)
    spectra = late_spectra(*begun, rim)
    own, other = cross_power(exchange(spectra, ("half", "tm")))
    pair = (own + shifted(other, "core", 1).astype(jnp.float32)).astype(jnp.bfloat16)
    got = exchange(pair, ("half", "chip"))
    return totals(got.reshape((PAIR, chips) + got.shape[1:]), NF // groups)


def solution(mesh):
    rows, groups = mesh.devices.shape
    row = ("half", "chip", "core")
    split = Mesh(
        mesh.devices.reshape(PAIR, rows // PAIR // CORES, CORES, groups), row + ("tm",)
    )
    return jax.shard_map(
        body,
        mesh=split,
        in_specs=(P(row, "tm"), P(row), P("tm")),
        out_specs=P(row, None, "tm", None),
        check_vma=False,
    )
```

```python
import jax
import jax.numpy as jnp
import numpy as np
from jax import lax
from jax.experimental import pallas as pl
from jax.experimental.pallas import tpu as pltpu
from jax.sharding import Mesh
from jax.sharding import PartitionSpec as P

NFFT = 256
NF = 128
HOP = 128
RIM = 192
REACH = 384
PAIR = 2
CORES = 2
SORTED = 256
LANES = 128
VMEM = 24 * 1024 * 1024


def shifted(array, axis, by):
    count = lax.axis_size(axis)
    return lax.ppermute(array, axis, [(i, (i + by) % count) for i in range(count)])


def dft_rows(groups):
    time_index = np.arange(NFFT)
    angles = 2.0 * np.pi * (time_index[:, None] * np.arange(NF)[None, :] % NFFT) / NFFT
    window = np.sin(np.pi * time_index / NFFT) ** 2
    norm = np.sqrt(np.sum(window * window))
    table = np.stack([window[:, None] * np.cos(angles), -window[:, None] * np.sin(angles)])
    table = (table / norm).reshape(2, NFFT, groups, PAIR, NF // groups // PAIR)
    rows = table.transpose(2, 3, 0, 4, 1).reshape(2 * NF, NFFT)
    rows = np.pad(rows, ((0, 0), (0, REACH - NFFT)))
    return jnp.asarray(rows, jnp.float32).astype(jnp.bfloat16)


def fill_pairs(out_ref, rows, table_ref, data_ref, scale_ref):
    targets = out_ref.shape[0]
    scale = scale_ref[:, rows]
    for pair in range(table_ref.shape[0] // 2):
        two = []
        for block in (2 * pair, 2 * pair + 1):
            spectrum = lax.dot_general(
                table_ref[block],
                data_ref[:, block * HOP : block * HOP + REACH],
                (((1,), (1,)), ((), ())),
                preferred_element_type=jnp.float32,
            )
            two.append((spectrum * scale).reshape(targets, -1, data_ref.shape[0]))
        out_ref[:, pair, :, rows] = jnp.concatenate(two, axis=1).astype(jnp.bfloat16)


def rim_kernel(edge_ref, out_ref):
    rows = edge_ref.shape[0]
    out_ref[:rows] = edge_ref[:, :LANES]
    rest = edge_ref[:, LANES:].astype(jnp.float32)
    both = jnp.concatenate([rest[: rows // 2], rest[rows // 2 :]], axis=1)
    out_ref[rows:] = both.astype(jnp.bfloat16)


def packed_rim(edge):
    rows, _ = edge.shape
    whole = pl.BlockSpec(memory_space=pltpu.VMEM)
    return pl.pallas_call(
        rim_kernel,
        in_specs=[whole],
        out_specs=whole,
        out_shape=jax.ShapeDtypeStruct((rows * RIM // LANES, LANES), jnp.bfloat16),
        compiler_params=pltpu.CompilerParams(vmem_limit_bytes=VMEM),
        name="rim",
    )(edge)


def sorting_matrix(size, lines):
    some, freqs = size // lines, lines // 2
    row = lax.broadcasted_iota(jnp.int32, (size, size), 0)
    column = lax.broadcasted_iota(jnp.int32, (size, size), 1)
    part = (row // some) % 2
    freq = row // (2 * some)
    return ((row % some) * lines + part * freqs + freq == column).astype(jnp.bfloat16)


def early_kernel(delay_ref, table_ref, scale_ref, snap_ref, out_ref, tail_ref, late_table_ref, order_ref, shifted_ref, data_ref):
    early = 2 * out_ref.shape[1]

    order_ref[...] = sorting_matrix(order_ref.shape[0], out_ref.shape[2] // 2)
    table = table_ref[...].astype(jnp.float32)
    for block in range(delay_ref.shape[0]):
        moved = pltpu.roll(table, delay_ref[block], 1).astype(jnp.bfloat16)
        if block < early:
            shifted_ref[block] = moved
        else:
            late_table_ref[block - early] = moved
    data_ref[...] = snap_ref[...].astype(jnp.bfloat16)
    tail_ref[...] = data_ref[:, early * HOP :]
    fill_pairs(out_ref, slice(None), shifted_ref, data_ref, scale_ref)


def early_spectra(snapshots, scale, block_delay, table, targets):
    rows, span = snapshots.shape
    blocks = span // HOP
    early = (span - REACH) // HOP + 1
    lines = 4 * NF // targets
    tail = span - early * HOP
    whole = pl.BlockSpec(memory_space=pltpu.VMEM)
    return pl.pallas_call(
        early_kernel,
        grid=(1,),
        in_specs=[pl.BlockSpec(memory_space=pltpu.SMEM), whole, whole, whole],
        out_specs=[
            pl.BlockSpec((targets, early // 2, lines, rows), lambda s: (0, 0, 0, 0)),
            whole,
            whole,
            whole,
        ],
        out_shape=[
            jax.ShapeDtypeStruct((targets, blocks // 2, lines, rows), jnp.bfloat16),
            jax.ShapeDtypeStruct((rows, tail), jnp.bfloat16),
            jax.ShapeDtypeStruct((blocks - early,) + table.shape, jnp.bfloat16),
            jax.ShapeDtypeStruct((SORTED, SORTED), jnp.bfloat16),
        ],
        scratch_shapes=[
            pltpu.VMEM((early,) + table.shape, jnp.bfloat16),
            pltpu.VMEM((rows, span), jnp.bfloat16),
        ],
        compiler_params=pltpu.CompilerParams(vmem_limit_bytes=VMEM),
        cost_estimate=pl.CostEstimate(
            flops=4 * NF * REACH * rows * early,
            bytes_accessed=4 * rows * span + 4 * NF * rows * early,
            transcendentals=0,
        ),
        name="dft_early",
    )(block_delay, table, scale, snapshots)


def late_kernel(table_ref, scale_ref, tail_ref, rim_ref, begun_ref, out_ref):
    rows, _ = tail_ref.shape
    half = RIM - LANES
    rest = rim_ref[rows:].astype(jnp.float32)
    lane = lax.broadcasted_iota(jnp.int32, (rows, LANES), 1)
    last = jnp.concatenate([rest, pltpu.roll(rest, half, 1)], axis=0)
    last = jnp.where(lane < half, last, 0.0).astype(jnp.bfloat16)
    pieces = [tail_ref[:, :HOP], tail_ref[:, HOP:], rim_ref[:rows], last]
    two = []
    for block in range(table_ref.shape[0]):
        products = lax.dot_general(
            table_ref[block],
            jnp.concatenate(pieces[block : block + REACH // HOP], axis=1),
            (((1,), (1,)), ((), ())),
            preferred_element_type=jnp.float32,
        )
        two.append((products * scale_ref[...]).reshape(out_ref.shape[0], -1, rows))
    out_ref[:, 0] = jnp.concatenate(two, axis=1).astype(jnp.bfloat16)


def late_spectra(begun, tail, table, scale, rim):
    targets, pairs, lines, rows = begun.shape
    late = table.shape[0]
    whole = pl.BlockSpec(memory_space=pltpu.VMEM)
    return pl.pallas_call(
        late_kernel,
        grid=(1,),
        in_specs=[whole, whole, whole, whole, pl.BlockSpec(memory_space=pl.ANY)],
        out_specs=pl.BlockSpec(
            (targets, late // 2, lines, rows), lambda s: (0, 2 * pairs // late - 1, 0, 0)
        ),
        out_shape=jax.ShapeDtypeStruct(begun.shape, begun.dtype),
        input_output_aliases={4: 0},
        compiler_params=pltpu.CompilerParams(vmem_limit_bytes=VMEM),
        cost_estimate=pl.CostEstimate(
            flops=4 * NF * REACH * rows * late,
            bytes_accessed=4 * NF * rows * late,
            transcendentals=0,
        ),
        name="dft_late",
    )(table, scale, tail, rim, begun)


def split_quads(mats):
    eights = [m.reshape(m.shape[0] // 8, 8, m.shape[1]) for m in mats]
    upper = lax.broadcasted_iota(jnp.int32, eights[0].shape, 1) < 4
    low, high = [], []
    for a, b in (eights[:2], eights[2:]):
        low.append(jnp.where(upper, a, pltpu.roll(b, 4, 1)))
        high.append(jnp.where(upper, pltpu.roll(a, 4, 1), b))
    return jnp.concatenate(low, axis=1), jnp.concatenate(high, axis=1)


def csd_kernel(order_ref, got_ref, own_ref, other_ref, sorted_ref):
    lines, every, _ = sorted_ref.shape
    sources, _, _, _, rows = got_ref.shape
    some = SORTED // lines
    step = sources * some // every
    for half in range(PAIR):
        for k in range(sources // step):
            by_line = lax.dot_general(
                order_ref[...],
                got_ref[k * step : (k + 1) * step, half].reshape(some * lines, rows),
                (((1,), (0,)), ((), ())),
                preferred_element_type=jnp.float32,
            )
            by_line = by_line.astype(jnp.bfloat16).reshape(lines, some, rows)
            sorted_ref[:, k * some : (k + 1) * some, half * rows : (half + 1) * rows] = by_line
    real, imag = [], []
    for freq in range(lines // 2):
        both = sorted_ref[2 * freq : 2 * freq + 2].reshape(2 * every, PAIR * rows)
        power = lax.dot_general(
            both, both, (((1,), (1,)), ((), ())), preferred_element_type=jnp.float32
        )
        real.append(power[:every, :every] + power[every:, every:])
        imag.append(power[:every, every:] - power[every:, :every])
    first_core = lax.axis_index("core") == 0
    for place, quad in ((0, real), (16, imag)):
        low, high = split_quads(quad)
        own_ref[:, place : place + 16, :] = jnp.where(first_core, low, high)
        other = jnp.where(first_core, high, low)
        other_ref[:, place : place + 16, :] = other.astype(jnp.bfloat16)


def cross_power(order, got):
    sources, _, pairs, lines, rows = got.shape
    every = sources * 2 * pairs
    shape = (every // 8, 2 * lines, every)
    whole = pl.BlockSpec(memory_space=pltpu.VMEM)
    return pl.pallas_call(
        csd_kernel,
        in_specs=[whole, whole],
        out_specs=[whole, whole],
        out_shape=[
            jax.ShapeDtypeStruct(shape, jnp.float32),
            jax.ShapeDtypeStruct(shape, jnp.bfloat16),
        ],
        scratch_shapes=[pltpu.VMEM((lines // 2, every, PAIR * rows), jnp.bfloat16)],
        compiler_params=pltpu.CompilerParams(vmem_limit_bytes=VMEM),
        name="csd",
    )(order, got)


def total_kernel(got_ref, out_ref, sum_ref):
    own, parts, freqs, _ = out_ref.shape
    sum_ref[...] = jnp.sum(got_ref[...].astype(jnp.float32), axis=1)
    few = freqs // PAIR
    for half in range(PAIR):
        for part in range(parts):
            for freq in range(few):
                for i in range(own):
                    row = (part * few + freq) * own + i
                    place = half * few + freq
                    out_ref[i, part, place : place + 1, :] = sum_ref[half, row : row + 1, :]


def totals(got, freqs):
    halves, _, lines, every = got.shape
    whole = pl.BlockSpec(memory_space=pltpu.VMEM)
    return pl.pallas_call(
        total_kernel,
        in_specs=[whole],
        out_specs=whole,
        out_shape=jax.ShapeDtypeStruct((lines * halves // (2 * freqs), 2, freqs, every), jnp.float32),
        scratch_shapes=[pltpu.VMEM((halves, lines, every), jnp.float32)],
        compiler_params=pltpu.CompilerParams(vmem_limit_bytes=VMEM),
        name="total",
    )(got)


def body(snapshots, weights, block_delay):
    groups = lax.axis_size("tm")
    chips = lax.axis_size("chip")
    targets = PAIR * groups
    total_rows = snapshots.shape[0] * PAIR * chips * CORES

    def exchange(array, axes):
        return lax.all_to_all(array, axes, split_axis=0, concat_axis=0, tiled=True)

    rim = shifted(packed_rim(snapshots[:, :RIM].astype(jnp.bfloat16)), "tm", -1)
    scale = jnp.sqrt(weights / total_rows).reshape(1, -1)
    begun, tail, table, order = early_spectra(
        snapshots, scale, block_delay, dft_rows(groups), targets
    )
    spectra = late_spectra(begun, tail, table, scale, rim)
    received = exchange(spectra, ("tm", "half"))
    received = received.reshape((groups, PAIR) + received.shape[1:])
    own, other = cross_power(order, received)
    pair = (own + shifted(other, "core", 1).astype(jnp.float32)).astype(jnp.bfloat16)
    got = exchange(pair, ("half", "chip"))
    return totals(got.reshape((PAIR, chips) + got.shape[1:]), NF // groups)


def solution(mesh):
    rows, groups = mesh.devices.shape
    row = ("half", "chip", "core")
    split = Mesh(
        mesh.devices.reshape(PAIR, rows // PAIR // CORES, CORES, groups), row + ("tm",)
    )
    return jax.shard_map(
        body,
        mesh=split,
        in_specs=(P(row, "tm"), P(row), P("tm")),
        out_specs=P(row, None, "tm", None),
        check_vma=False,
    )
```

```python
import jax
import jax.numpy as jnp
import numpy as np
from jax import lax
from jax.experimental import pallas as pl
from jax.experimental.pallas import tpu as pltpu
from jax.sharding import Mesh
from jax.sharding import PartitionSpec as P

NFFT = 256
NF = 128
HOP = 128
RIM = 192
REACH = 384
STRIP = 256
PAIR = 2
CORES = 2
LANES = 128
VMEM = 24 * 1024 * 1024


def shifted(array, axis, by):
    count = lax.axis_size(axis)
    return lax.ppermute(array, axis, [(i, (i + by) % count) for i in range(count)])


def dft_rows(groups):
    time_index = np.arange(NFFT)
    angles = 2.0 * np.pi * (time_index[:, None] * np.arange(NF)[None, :] % NFFT) / NFFT
    window = np.sin(np.pi * time_index / NFFT) ** 2
    norm = np.sqrt(np.sum(window * window))
    table = np.stack([window[:, None] * np.cos(angles), -window[:, None] * np.sin(angles)])
    table = (table / norm).reshape(2, NFFT, groups, PAIR, NF // groups // PAIR)
    rows = table.transpose(3, 2, 0, 4, 1).reshape(2 * NF, NFFT)
    rows = np.pad(rows, ((0, 0), (0, REACH - NFFT)))
    return jnp.asarray(rows, jnp.float32).astype(jnp.bfloat16)


def fill_pairs(out_ref, rows, table_ref, data_ref, scale_ref):
    targets = out_ref.shape[0]
    scale = scale_ref[:, rows]
    for pair in range(table_ref.shape[0] // 2):
        two = []
        for block in (2 * pair, 2 * pair + 1):
            spectrum = lax.dot_general(
                table_ref[block],
                data_ref[:, block * HOP : block * HOP + REACH],
                (((1,), (1,)), ((), ())),
                preferred_element_type=jnp.float32,
            )
            two.append((spectrum * scale).reshape(targets, -1, data_ref.shape[0]))
        out_ref[:, pair, :, rows] = jnp.concatenate(two, axis=1).astype(jnp.bfloat16)


def rim_kernel(edge_ref, out_ref):
    rows = edge_ref.shape[0]
    out_ref[:rows] = edge_ref[:, :LANES]
    rest = edge_ref[:, LANES:].astype(jnp.float32)
    both = jnp.concatenate([rest[: rows // 2], rest[rows // 2 :]], axis=1)
    out_ref[rows:] = both.astype(jnp.bfloat16)


def packed_rim(edge):
    rows, _ = edge.shape
    whole = pl.BlockSpec(memory_space=pltpu.VMEM)
    return pl.pallas_call(
        rim_kernel,
        in_specs=[whole],
        out_specs=whole,
        out_shape=jax.ShapeDtypeStruct((rows * RIM // LANES, LANES), jnp.bfloat16),
        compiler_params=pltpu.CompilerParams(vmem_limit_bytes=VMEM),
        name="rim",
    )(edge)


def early_kernel(total_rows, delay_ref, table_ref, weight_ref, snap_ref, out_ref, tail_ref, late_table_ref, scale_ref, shifted_ref, data_ref):
    early = 2 * out_ref.shape[1]

    @pl.when(pl.program_id(0) == 0)
    def _():
        table = table_ref[...].astype(jnp.float32)
        for block in range(delay_ref.shape[0]):
            moved = pltpu.roll(table, delay_ref[block], 1).astype(jnp.bfloat16)
            if block < early:
                shifted_ref[block] = moved
            else:
                late_table_ref[block - early] = moved

    data_ref[...] = snap_ref[...].astype(jnp.bfloat16)
    tail_ref[...] = data_ref[:, early * HOP :]
    scale_ref[...] = jnp.sqrt(weight_ref[...] / total_rows)
    fill_pairs(out_ref, slice(None), shifted_ref, data_ref, scale_ref)


def early_spectra(snapshots, weights, block_delay, table, targets, total_rows):
    rows, span = snapshots.shape
    blocks = span // HOP
    early = (span - REACH) // HOP + 1
    lines = 4 * NF // targets
    tail = span - early * HOP
    return pl.pallas_call(
        lambda *refs: early_kernel(total_rows, *refs),
        grid=(rows // STRIP,),
        in_specs=[
            pl.BlockSpec(memory_space=pltpu.SMEM),
            pl.BlockSpec(table.shape, lambda s: (0, 0)),
            pl.BlockSpec((1, STRIP), lambda s: (0, s)),
            pl.BlockSpec((STRIP, span), lambda s: (s, 0)),
        ],
        out_specs=[
            pl.BlockSpec((targets, early // 2, lines, STRIP), lambda s: (0, 0, 0, s)),
            pl.BlockSpec((STRIP, tail), lambda s: (s, 0)),
            pl.BlockSpec((blocks - early,) + table.shape, lambda s: (0, 0, 0)),
            pl.BlockSpec((1, STRIP), lambda s: (0, s)),
        ],
        out_shape=[
            jax.ShapeDtypeStruct((targets, blocks // 2, lines, rows), jnp.bfloat16),
            jax.ShapeDtypeStruct((rows, tail), jnp.bfloat16),
            jax.ShapeDtypeStruct((blocks - early,) + table.shape, jnp.bfloat16),
            jax.ShapeDtypeStruct((1, rows), jnp.float32),
        ],
        scratch_shapes=[
            pltpu.VMEM((early,) + table.shape, jnp.bfloat16),
            pltpu.VMEM((STRIP, span), jnp.bfloat16),
        ],
        compiler_params=pltpu.CompilerParams(vmem_limit_bytes=VMEM),
        cost_estimate=pl.CostEstimate(
            flops=4 * NF * REACH * rows * early,
            bytes_accessed=4 * rows * span + 4 * NF * rows * early,
            transcendentals=0,
        ),
        name="dft_early",
    )(block_delay, table, weights.reshape(1, rows), snapshots)


def late_kernel(table_ref, scale_ref, tail_ref, rim_ref, begun_ref, out_ref, data_ref):
    rows, tail = tail_ref.shape
    strip = data_ref.shape[0]
    rest = rim_ref[rows:].astype(jnp.float32)
    lane = lax.broadcasted_iota(jnp.int32, rest.shape, 1)
    for s in range(rows // strip):
        part = slice(s * strip, (s + 1) * strip)
        mine = rest if s == 0 else pltpu.roll(rest, RIM - LANES, 1)
        mine = jnp.where(lane < RIM - LANES, mine, 0.0).astype(jnp.bfloat16)
        data_ref[:, :tail] = tail_ref[part]
        data_ref[:, tail : tail + LANES] = rim_ref[part]
        data_ref[:, tail + LANES :] = mine
        fill_pairs(out_ref, part, table_ref, data_ref, scale_ref)


def late_spectra(begun, tail, table, scale, rim):
    targets, pairs, lines, rows = begun.shape
    late = table.shape[0]
    whole = pl.BlockSpec(memory_space=pltpu.VMEM)
    return pl.pallas_call(
        late_kernel,
        grid=(1,),
        in_specs=[whole, whole, whole, whole, pl.BlockSpec(memory_space=pl.ANY)],
        out_specs=pl.BlockSpec(
            (targets, late // 2, lines, rows), lambda s: (0, 2 * pairs // late - 1, 0, 0)
        ),
        out_shape=jax.ShapeDtypeStruct(begun.shape, begun.dtype),
        input_output_aliases={4: 0},
        scratch_shapes=[pltpu.VMEM((STRIP, (late - 1) * HOP + REACH), jnp.bfloat16)],
        compiler_params=pltpu.CompilerParams(vmem_limit_bytes=VMEM),
        cost_estimate=pl.CostEstimate(
            flops=4 * NF * REACH * rows * late,
            bytes_accessed=4 * NF * rows * late,
            transcendentals=0,
        ),
        name="dft_late",
    )(table, scale, tail, rim, begun)


def split_quads(mats):
    eights = [m.reshape(m.shape[0] // 8, 8, m.shape[1]) for m in mats]
    upper = lax.broadcasted_iota(jnp.int32, eights[0].shape, 1) < 4
    low, high = [], []
    for a, b in (eights[:2], eights[2:]):
        low.append(jnp.where(upper, a, pltpu.roll(b, 4, 1)))
        high.append(jnp.where(upper, pltpu.roll(a, 4, 1), b))
    return jnp.concatenate(low, axis=1), jnp.concatenate(high, axis=1)


def csd_kernel(got_ref, out_ref, sorted_ref):
    halves, lines, every, rows = sorted_ref.shape
    freqs = lines // 2
    sources = got_ref.shape[0] // halves
    step = 4
    some = step * every // sources
    row = lax.broadcasted_iota(jnp.int32, (some * lines, some * lines), 0)
    column = lax.broadcasted_iota(jnp.int32, (some * lines, some * lines), 1)
    part = (row // some) % 2
    freq = row // (2 * some)
    order = ((row % some) * lines + part * freqs + freq == column).astype(jnp.bfloat16)
    for half in range(halves):
        for k in range(sources // step):
            first = half * sources + k * step
            by_line = lax.dot_general(
                order,
                got_ref[first : first + step].reshape(some * lines, rows),
                (((1,), (0,)), ((), ())),
                preferred_element_type=jnp.float32,
            )
            by_line = by_line.astype(jnp.bfloat16).reshape(lines, some, rows)
            sorted_ref[half, :, k * some : (k + 1) * some, :] = by_line
    real, imag = [], []
    for freq in range(freqs):
        power = 0.0
        for half in range(halves):
            both = sorted_ref[half, 2 * freq : 2 * freq + 2].reshape(2 * every, rows)
            power += lax.dot_general(
                both, both, (((1,), (1,)), ((), ())), preferred_element_type=jnp.float32
            )
        real.append(power[:every, :every] + power[every:, every:])
        imag.append(power[:every, every:] - power[every:, :every])
    for place, quad in ((0, real), (16, imag)):
        low, high = split_quads(quad)
        out_ref[0, :, place : place + 16, :] = low.astype(jnp.bfloat16)
        out_ref[1, :, place : place + 16, :] = high.astype(jnp.bfloat16)


def cross_power(got):
    sources, pairs, lines, rows = got.shape
    every = sources // PAIR * 2 * pairs
    shape = (CORES, every // 8, 2 * lines, every)
    whole = pl.BlockSpec(memory_space=pltpu.VMEM)
    return pl.pallas_call(
        csd_kernel,
        in_specs=[whole],
        out_specs=whole,
        out_shape=jax.ShapeDtypeStruct(shape, jnp.bfloat16),
        scratch_shapes=[pltpu.VMEM((PAIR, lines // 2, every, rows), jnp.bfloat16)],
        compiler_params=pltpu.CompilerParams(vmem_limit_bytes=VMEM),
        name="csd",
    )(got)


def total_kernel(got_ref, out_ref, sum_ref):
    own, parts, freqs, _ = out_ref.shape
    sum_ref[...] = jnp.sum(got_ref[...].astype(jnp.float32), axis=1)
    few = freqs // PAIR
    for half in range(PAIR):
        for part in range(parts):
            for freq in range(few):
                for i in range(own):
                    row = (part * few + freq) * own + i
                    place = half * few + freq
                    out_ref[i, part, place : place + 1, :] = sum_ref[half, row : row + 1, :]


def totals(got, freqs):
    halves, _, lines, every = got.shape
    whole = pl.BlockSpec(memory_space=pltpu.VMEM)
    return pl.pallas_call(
        total_kernel,
        in_specs=[whole],
        out_specs=whole,
        out_shape=jax.ShapeDtypeStruct((lines * halves // (2 * freqs), 2, freqs, every), jnp.float32),
        scratch_shapes=[pltpu.VMEM((halves, lines, every), jnp.float32)],
        compiler_params=pltpu.CompilerParams(vmem_limit_bytes=VMEM),
        name="total",
    )(got)


def body(snapshots, weights, block_delay):
    groups = lax.axis_size("tm")
    chips = lax.axis_size("chip")
    targets = PAIR * groups
    total_rows = snapshots.shape[0] * PAIR * chips * CORES

    def exchange(array, axes):
        return lax.all_to_all(array, axes, split_axis=0, concat_axis=0, tiled=True)

    rim = shifted(packed_rim(snapshots[:, :RIM].astype(jnp.bfloat16)), "tm", -1)
    begun = early_spectra(snapshots, weights, block_delay, dft_rows(groups), targets, total_rows)
    spectra = late_spectra(*begun, rim)
    halves = exchange(cross_power(exchange(spectra, ("half", "tm"))), "core")
    pair = jnp.sum(halves.astype(jnp.float32), axis=0).astype(jnp.bfloat16)
    got = exchange(pair, ("half", "chip"))
    return totals(got.reshape((PAIR, chips) + got.shape[1:]), NF // groups)


def solution(mesh):
    rows, groups = mesh.devices.shape
    row = ("half", "chip", "core")
    split = Mesh(
        mesh.devices.reshape(PAIR, rows // PAIR // CORES, CORES, groups), row + ("tm",)
    )
    return jax.shard_map(
        body,
        mesh=split,
        in_specs=(P(row, "tm"), P(row), P("tm")),
        out_specs=P(row, None, "tm", None),
        check_vma=False,
    )
```

```python
import jax
import jax.numpy as jnp
import numpy as np
from jax import lax
from jax.experimental import pallas as pl
from jax.experimental.pallas import tpu as pltpu
from jax.sharding import Mesh
from jax.sharding import PartitionSpec as P

NFFT = 256
NF = 128
HOP = 128
RIM = 192
REACH = 384
PAIR = 2
CORES = 2
SORTED = 256
LANES = 128
VMEM = 24 * 1024 * 1024


def shifted(array, axis, by):
    count = lax.axis_size(axis)
    return lax.ppermute(array, axis, [(i, (i + by) % count) for i in range(count)])


def dft_rows(groups):
    time_index = np.arange(NFFT)
    angles = 2.0 * np.pi * (time_index[:, None] * np.arange(NF)[None, :] % NFFT) / NFFT
    window = np.sin(np.pi * time_index / NFFT) ** 2
    norm = np.sqrt(np.sum(window * window))
    table = np.stack([window[:, None] * np.cos(angles), -window[:, None] * np.sin(angles)])
    table = (table / norm).reshape(2, NFFT, groups, PAIR, NF // groups // PAIR)
    rows = table.transpose(3, 2, 0, 4, 1).reshape(2 * NF, NFFT)
    rows = np.pad(rows, ((0, 0), (0, REACH - NFFT)))
    return jnp.asarray(rows, jnp.float32).astype(jnp.bfloat16)


def fill_pairs(out_ref, rows, table_ref, data_ref, scale_ref):
    targets = out_ref.shape[0]
    scale = scale_ref[:, rows]
    for pair in range(table_ref.shape[0] // 2):
        two = []
        for block in (2 * pair, 2 * pair + 1):
            spectrum = lax.dot_general(
                table_ref[block],
                data_ref[:, block * HOP : block * HOP + REACH],
                (((1,), (1,)), ((), ())),
                preferred_element_type=jnp.float32,
            )
            two.append((spectrum * scale).reshape(targets, -1, data_ref.shape[0]))
        out_ref[:, pair, :, rows] = jnp.concatenate(two, axis=1).astype(jnp.bfloat16)


def rim_kernel(edge_ref, out_ref):
    rows = edge_ref.shape[0]
    out_ref[:rows] = edge_ref[:, :LANES]
    rest = edge_ref[:, LANES:].astype(jnp.float32)
    both = jnp.concatenate([rest[: rows // 2], rest[rows // 2 :]], axis=1)
    out_ref[rows:] = both.astype(jnp.bfloat16)


def packed_rim(edge):
    rows, _ = edge.shape
    whole = pl.BlockSpec(memory_space=pltpu.VMEM)
    return pl.pallas_call(
        rim_kernel,
        in_specs=[whole],
        out_specs=whole,
        out_shape=jax.ShapeDtypeStruct((rows * RIM // LANES, LANES), jnp.bfloat16),
        compiler_params=pltpu.CompilerParams(vmem_limit_bytes=VMEM),
        name="rim",
    )(edge)


def sorting_matrix(size, lines):
    some, freqs = size // lines, lines // 2
    row = lax.broadcasted_iota(jnp.int32, (size, size), 0)
    column = lax.broadcasted_iota(jnp.int32, (size, size), 1)
    part = (row // some) % 2
    freq = row // (2 * some)
    return ((row % some) * lines + part * freqs + freq == column).astype(jnp.bfloat16)


def early_kernel(delay_ref, table_ref, scale_ref, snap_ref, out_ref, tail_ref, late_table_ref, order_ref, shifted_ref, data_ref):
    early = 2 * out_ref.shape[1]

    order_ref[...] = sorting_matrix(order_ref.shape[0], out_ref.shape[2] // 2)
    table = table_ref[...].astype(jnp.float32)
    for block in range(delay_ref.shape[0]):
        moved = pltpu.roll(table, delay_ref[block], 1).astype(jnp.bfloat16)
        if block < early:
            shifted_ref[block] = moved
        else:
            late_table_ref[block - early] = moved
    data_ref[...] = snap_ref[...].astype(jnp.bfloat16)
    tail_ref[...] = data_ref[:, early * HOP :]
    fill_pairs(out_ref, slice(None), shifted_ref, data_ref, scale_ref)


def early_spectra(snapshots, scale, block_delay, table, targets):
    rows, span = snapshots.shape
    blocks = span // HOP
    early = (span - REACH) // HOP + 1
    lines = 4 * NF // targets
    tail = span - early * HOP
    whole = pl.BlockSpec(memory_space=pltpu.VMEM)
    return pl.pallas_call(
        early_kernel,
        grid=(1,),
        in_specs=[pl.BlockSpec(memory_space=pltpu.SMEM), whole, whole, whole],
        out_specs=[
            pl.BlockSpec((targets, early // 2, lines, rows), lambda s: (0, 0, 0, 0)),
            whole,
            whole,
            whole,
        ],
        out_shape=[
            jax.ShapeDtypeStruct((targets, blocks // 2, lines, rows), jnp.bfloat16),
            jax.ShapeDtypeStruct((rows, tail), jnp.bfloat16),
            jax.ShapeDtypeStruct((blocks - early,) + table.shape, jnp.bfloat16),
            jax.ShapeDtypeStruct((SORTED, SORTED), jnp.bfloat16),
        ],
        scratch_shapes=[
            pltpu.VMEM((early,) + table.shape, jnp.bfloat16),
            pltpu.VMEM((rows, span), jnp.bfloat16),
        ],
        compiler_params=pltpu.CompilerParams(vmem_limit_bytes=VMEM),
        cost_estimate=pl.CostEstimate(
            flops=4 * NF * REACH * rows * early,
            bytes_accessed=4 * rows * span + 4 * NF * rows * early,
            transcendentals=0,
        ),
        name="dft_early",
    )(block_delay, table, scale, snapshots)


def late_kernel(table_ref, scale_ref, tail_ref, rim_ref, begun_ref, out_ref):
    rows, _ = tail_ref.shape
    half = RIM - LANES
    rest = rim_ref[rows:].astype(jnp.float32)
    lane = lax.broadcasted_iota(jnp.int32, (rows, LANES), 1)
    last = jnp.concatenate([rest, pltpu.roll(rest, half, 1)], axis=0)
    last = jnp.where(lane < half, last, 0.0).astype(jnp.bfloat16)
    pieces = [tail_ref[:, :HOP], tail_ref[:, HOP:], rim_ref[:rows], last]
    two = []
    for block in range(table_ref.shape[0]):
        products = lax.dot_general(
            table_ref[block],
            jnp.concatenate(pieces[block : block + REACH // HOP], axis=1),
            (((1,), (1,)), ((), ())),
            preferred_element_type=jnp.float32,
        )
        two.append((products * scale_ref[...]).reshape(out_ref.shape[0], -1, rows))
    out_ref[:, 0] = jnp.concatenate(two, axis=1).astype(jnp.bfloat16)


def late_spectra(begun, tail, table, scale, rim):
    targets, pairs, lines, rows = begun.shape
    late = table.shape[0]
    whole = pl.BlockSpec(memory_space=pltpu.VMEM)
    return pl.pallas_call(
        late_kernel,
        grid=(1,),
        in_specs=[whole, whole, whole, whole, pl.BlockSpec(memory_space=pl.ANY)],
        out_specs=pl.BlockSpec(
            (targets, late // 2, lines, rows), lambda s: (0, 2 * pairs // late - 1, 0, 0)
        ),
        out_shape=jax.ShapeDtypeStruct(begun.shape, begun.dtype),
        input_output_aliases={4: 0},
        compiler_params=pltpu.CompilerParams(vmem_limit_bytes=VMEM),
        cost_estimate=pl.CostEstimate(
            flops=4 * NF * REACH * rows * late,
            bytes_accessed=4 * NF * rows * late,
            transcendentals=0,
        ),
        name="dft_late",
    )(table, scale, tail, rim, begun)


def split_quads(mats):
    eights = [m.reshape(m.shape[0] // 8, 8, m.shape[1]) for m in mats]
    upper = lax.broadcasted_iota(jnp.int32, eights[0].shape, 1) < 4
    low, high = [], []
    for a, b in (eights[:2], eights[2:]):
        low.append(jnp.where(upper, a, pltpu.roll(b, 4, 1)))
        high.append(jnp.where(upper, pltpu.roll(a, 4, 1), b))
    return jnp.concatenate(low, axis=1), jnp.concatenate(high, axis=1)


def csd_kernel(order_ref, got_ref, own_ref, other_ref, sorted_ref):
    lines, every, _ = sorted_ref.shape
    _, sources, _, _, rows = got_ref.shape
    some = SORTED // lines
    step = sources * some // every
    for half in range(PAIR):
        for k in range(sources // step):
            by_line = lax.dot_general(
                order_ref[...],
                got_ref[half, k * step : (k + 1) * step].reshape(some * lines, rows),
                (((1,), (0,)), ((), ())),
                preferred_element_type=jnp.float32,
            )
            by_line = by_line.astype(jnp.bfloat16).reshape(lines, some, rows)
            sorted_ref[:, k * some : (k + 1) * some, half * rows : (half + 1) * rows] = by_line
    real, imag = [], []
    for freq in range(lines // 2):
        both = sorted_ref[2 * freq : 2 * freq + 2].reshape(2 * every, PAIR * rows)
        power = lax.dot_general(
            both, both, (((1,), (1,)), ((), ())), preferred_element_type=jnp.float32
        )
        real.append(power[:every, :every] + power[every:, every:])
        imag.append(power[:every, every:] - power[every:, :every])
    first_core = lax.axis_index("core") == 0
    for place, quad in ((0, real), (16, imag)):
        low, high = split_quads(quad)
        own_ref[:, place : place + 16, :] = jnp.where(first_core, low, high)
        other = jnp.where(first_core, high, low)
        other_ref[:, place : place + 16, :] = other.astype(jnp.bfloat16)


def cross_power(order, got):
    _, sources, pairs, lines, rows = got.shape
    every = sources * 2 * pairs
    shape = (every // 8, 2 * lines, every)
    whole = pl.BlockSpec(memory_space=pltpu.VMEM)
    return pl.pallas_call(
        csd_kernel,
        in_specs=[whole, whole],
        out_specs=[whole, whole],
        out_shape=[
            jax.ShapeDtypeStruct(shape, jnp.float32),
            jax.ShapeDtypeStruct(shape, jnp.bfloat16),
        ],
        scratch_shapes=[pltpu.VMEM((lines // 2, every, PAIR * rows), jnp.bfloat16)],
        compiler_params=pltpu.CompilerParams(vmem_limit_bytes=VMEM),
        name="csd",
    )(order, got)


def total_kernel(got_ref, out_ref, sum_ref):
    own, parts, freqs, _ = out_ref.shape
    sum_ref[...] = jnp.sum(got_ref[...].astype(jnp.float32), axis=1)
    few = freqs // PAIR
    for half in range(PAIR):
        for part in range(parts):
            for freq in range(few):
                for i in range(own):
                    row = (part * few + freq) * own + i
                    place = half * few + freq
                    out_ref[i, part, place : place + 1, :] = sum_ref[half, row : row + 1, :]


def totals(got, freqs):
    halves, _, lines, every = got.shape
    whole = pl.BlockSpec(memory_space=pltpu.VMEM)
    return pl.pallas_call(
        total_kernel,
        in_specs=[whole],
        out_specs=whole,
        out_shape=jax.ShapeDtypeStruct((lines * halves // (2 * freqs), 2, freqs, every), jnp.float32),
        scratch_shapes=[pltpu.VMEM((halves, lines, every), jnp.float32)],
        compiler_params=pltpu.CompilerParams(vmem_limit_bytes=VMEM),
        name="total",
    )(got)


def body(snapshots, weights, block_delay):
    groups = lax.axis_size("tm")
    chips = lax.axis_size("chip")
    targets = PAIR * groups
    total_rows = snapshots.shape[0] * PAIR * chips * CORES

    def exchange(array, axes):
        return lax.all_to_all(array, axes, split_axis=0, concat_axis=0, tiled=True)

    rim = shifted(packed_rim(snapshots[:, :RIM].astype(jnp.bfloat16)), "tm", -1)
    scale = jnp.sqrt(weights / total_rows).reshape(1, -1)
    begun, tail, table, order = early_spectra(
        snapshots, scale, block_delay, dft_rows(groups), targets
    )
    spectra = late_spectra(begun, tail, table, scale, rim)
    received = exchange(spectra, ("half", "tm"))
    received = received.reshape((PAIR, groups) + received.shape[1:])
    own, other = cross_power(order, received)
    pair = (own + shifted(other, "core", 1).astype(jnp.float32)).astype(jnp.bfloat16)
    got = exchange(pair, ("half", "chip"))
    return totals(got.reshape((PAIR, chips) + got.shape[1:]), NF // groups)


def solution(mesh):
    rows, groups = mesh.devices.shape
    row = ("half", "chip", "core")
    split = Mesh(
        mesh.devices.reshape(PAIR, rows // PAIR // CORES, CORES, groups), row + ("tm",)
    )
    return jax.shard_map(
        body,
        mesh=split,
        in_specs=(P(row, "tm"), P(row), P("tm")),
        out_specs=P(row, None, "tm", None),
        check_vma=False,
    )
```

```python
import jax
import jax.numpy as jnp
import numpy as np
from jax import lax
from jax.experimental import pallas as pl
from jax.experimental.pallas import tpu as pltpu
from jax.sharding import Mesh
from jax.sharding import PartitionSpec as P

NFFT = 256
NF = 128
HOP = 128
RIM = 192
REACH = 384
PAIR = 2
CORES = 2
SORTED = 256
LANES = 128
VMEM = 24 * 1024 * 1024


def shifted(array, axis, by):
    count = lax.axis_size(axis)
    return lax.ppermute(array, axis, [(i, (i + by) % count) for i in range(count)])


def dft_rows(groups):
    time_index = np.arange(NFFT)
    angles = 2.0 * np.pi * (time_index[:, None] * np.arange(NF)[None, :] % NFFT) / NFFT
    window = np.sin(np.pi * time_index / NFFT) ** 2
    norm = np.sqrt(np.sum(window * window))
    table = np.stack([window[:, None] * np.cos(angles), -window[:, None] * np.sin(angles)])
    table = (table / norm).reshape(2, NFFT, groups, PAIR, NF // groups // PAIR)
    rows = table.transpose(3, 2, 0, 4, 1).reshape(2 * NF, NFFT)
    rows = np.pad(rows, ((0, 0), (0, REACH - NFFT)))
    return jnp.asarray(rows, jnp.float32).astype(jnp.bfloat16)


def fill_pairs(out_ref, rows, table_ref, data_ref, scale_ref):
    targets = out_ref.shape[0]
    scale = scale_ref[:, rows]
    for pair in range(table_ref.shape[0] // 2):
        two = []
        for block in (2 * pair, 2 * pair + 1):
            spectrum = lax.dot_general(
                table_ref[block],
                data_ref[:, block * HOP : block * HOP + REACH],
                (((1,), (1,)), ((), ())),
                preferred_element_type=jnp.float32,
            )
            two.append((spectrum * scale).reshape(targets, -1, data_ref.shape[0]))
        out_ref[:, pair, :, rows] = jnp.concatenate(two, axis=1).astype(jnp.bfloat16)


def rim_kernel(edge_ref, out_ref):
    rows = edge_ref.shape[0]
    out_ref[:rows] = edge_ref[:, :LANES]
    rest = edge_ref[:, LANES:].astype(jnp.float32)
    both = jnp.concatenate([rest[: rows // 2], rest[rows // 2 :]], axis=1)
    out_ref[rows:] = both.astype(jnp.bfloat16)


def packed_rim(edge):
    rows, _ = edge.shape
    whole = pl.BlockSpec(memory_space=pltpu.VMEM)
    return pl.pallas_call(
        rim_kernel,
        in_specs=[whole],
        out_specs=whole,
        out_shape=jax.ShapeDtypeStruct((rows * RIM // LANES, LANES), jnp.bfloat16),
        compiler_params=pltpu.CompilerParams(vmem_limit_bytes=VMEM),
        name="rim",
    )(edge)


def sorting_matrix(size, lines):
    some, freqs = size // lines, lines // 2
    row = lax.broadcasted_iota(jnp.int32, (size, size), 0)
    column = lax.broadcasted_iota(jnp.int32, (size, size), 1)
    part = (row // some) % 2
    freq = row // (2 * some)
    return ((row % some) * lines + part * freqs + freq == column).astype(jnp.bfloat16)


def early_kernel(delay_ref, table_ref, scale_ref, snap_ref, out_ref, tail_ref, late_table_ref, order_ref, shifted_ref, data_ref):
    early = 2 * out_ref.shape[1]

    order_ref[...] = sorting_matrix(order_ref.shape[0], out_ref.shape[2] // 2)
    table = table_ref[...].astype(jnp.float32)
    for block in range(delay_ref.shape[0]):
        moved = pltpu.roll(table, delay_ref[block], 1).astype(jnp.bfloat16)
        if block < early:
            shifted_ref[block] = moved
        else:
            late_table_ref[block - early] = moved
    data_ref[...] = snap_ref[...].astype(jnp.bfloat16)
    tail_ref[...] = data_ref[:, early * HOP :]
    fill_pairs(out_ref, slice(None), shifted_ref, data_ref, scale_ref)


def early_spectra(snapshots, scale, block_delay, table, targets):
    rows, span = snapshots.shape
    blocks = span // HOP
    early = (span - REACH) // HOP + 1
    lines = 4 * NF // targets
    tail = span - early * HOP
    whole = pl.BlockSpec(memory_space=pltpu.VMEM)
    return pl.pallas_call(
        early_kernel,
        grid=(1,),
        in_specs=[pl.BlockSpec(memory_space=pltpu.SMEM), whole, whole, whole],
        out_specs=[
            pl.BlockSpec((targets, early // 2, lines, rows), lambda s: (0, 0, 0, 0)),
            whole,
            whole,
            whole,
        ],
        out_shape=[
            jax.ShapeDtypeStruct((targets, blocks // 2, lines, rows), jnp.bfloat16),
            jax.ShapeDtypeStruct((rows, tail), jnp.bfloat16),
            jax.ShapeDtypeStruct((blocks - early,) + table.shape, jnp.bfloat16),
            jax.ShapeDtypeStruct((SORTED, SORTED), jnp.bfloat16),
        ],
        scratch_shapes=[
            pltpu.VMEM((early,) + table.shape, jnp.bfloat16),
            pltpu.VMEM((rows, span), jnp.bfloat16),
        ],
        compiler_params=pltpu.CompilerParams(vmem_limit_bytes=VMEM),
        cost_estimate=pl.CostEstimate(
            flops=4 * NF * REACH * rows * early,
            bytes_accessed=4 * rows * span + 4 * NF * rows * early,
            transcendentals=0,
        ),
        name="dft_early",
    )(block_delay, table, scale, snapshots)


def late_kernel(table_ref, scale_ref, tail_ref, rim_ref, begun_ref, out_ref, made_ref, sems):
    rows, _ = tail_ref.shape
    half = RIM - LANES
    rest = rim_ref[rows:].astype(jnp.float32)
    lane = lax.broadcasted_iota(jnp.int32, (rows, LANES), 1)
    last = jnp.concatenate([rest, pltpu.roll(rest, half, 1)], axis=0)
    last = jnp.where(lane < half, last, 0.0).astype(jnp.bfloat16)
    pieces = [tail_ref[:, :HOP], tail_ref[:, HOP:], rim_ref[:rows], last]
    pairs = out_ref.shape[1]
    steps, targets, _, strip = made_ref.shape
    copies = []
    for s in range(steps):
        part = slice(s * strip, (s + 1) * strip)
        two = []
        for block in range(table_ref.shape[0]):
            products = lax.dot_general(
                table_ref[block],
                jnp.concatenate([p[part] for p in pieces[block : block + REACH // HOP]], axis=1),
                (((1,), (1,)), ((), ())),
                preferred_element_type=jnp.float32,
            )
            two.append((products * scale_ref[:, part]).reshape(targets, -1, strip))
        made_ref[s] = jnp.concatenate(two, axis=1).astype(jnp.bfloat16)
        copies.append(
            pltpu.make_async_copy(
                made_ref.at[s], out_ref.at[:, pairs - 1, :, s * strip : (s + 1) * strip], sems.at[s]
            )
        )
        copies[-1].start()
    for copy in copies:
        copy.wait()


def late_spectra(begun, tail, table, scale, rim):
    targets, pairs, lines, rows = begun.shape
    late = table.shape[0]
    whole = pl.BlockSpec(memory_space=pltpu.VMEM)
    return pl.pallas_call(
        late_kernel,
        in_specs=[whole, whole, whole, whole, pl.BlockSpec(memory_space=pl.ANY)],
        out_specs=pl.BlockSpec(memory_space=pl.ANY),
        out_shape=jax.ShapeDtypeStruct(begun.shape, begun.dtype),
        input_output_aliases={4: 0},
        scratch_shapes=[
            pltpu.VMEM((2, targets, lines, rows // 2), jnp.bfloat16),
            pltpu.SemaphoreType.DMA((2,)),
        ],
        compiler_params=pltpu.CompilerParams(vmem_limit_bytes=VMEM),
        cost_estimate=pl.CostEstimate(
            flops=4 * NF * REACH * rows * late,
            bytes_accessed=4 * NF * rows * late,
            transcendentals=0,
        ),
        name="dft_late",
    )(table, scale, tail, rim, begun)


def split_quads(mats):
    eights = [m.reshape(m.shape[0] // 8, 8, m.shape[1]) for m in mats]
    upper = lax.broadcasted_iota(jnp.int32, eights[0].shape, 1) < 4
    low, high = [], []
    for a, b in (eights[:2], eights[2:]):
        low.append(jnp.where(upper, a, pltpu.roll(b, 4, 1)))
        high.append(jnp.where(upper, pltpu.roll(a, 4, 1), b))
    return jnp.concatenate(low, axis=1), jnp.concatenate(high, axis=1)


def csd_kernel(order_ref, got_ref, own_ref, other_ref, sorted_ref):
    lines, every, _ = sorted_ref.shape
    _, sources, _, _, rows = got_ref.shape
    some = SORTED // lines
    step = sources * some // every
    for half in range(PAIR):
        for k in range(sources // step):
            by_line = lax.dot_general(
                order_ref[...],
                got_ref[half, k * step : (k + 1) * step].reshape(some * lines, rows),
                (((1,), (0,)), ((), ())),
                preferred_element_type=jnp.float32,
            )
            by_line = by_line.astype(jnp.bfloat16).reshape(lines, some, rows)
            sorted_ref[:, k * some : (k + 1) * some, half * rows : (half + 1) * rows] = by_line
    real, imag = [], []
    for freq in range(lines // 2):
        both = sorted_ref[2 * freq : 2 * freq + 2].reshape(2 * every, PAIR * rows)
        power = lax.dot_general(
            both, both, (((1,), (1,)), ((), ())), preferred_element_type=jnp.float32
        )
        real.append(power[:every, :every] + power[every:, every:])
        imag.append(power[:every, every:] - power[every:, :every])
    first_core = lax.axis_index("core") == 0
    for place, quad in ((0, real), (16, imag)):
        low, high = split_quads(quad)
        own_ref[:, place : place + 16, :] = jnp.where(first_core, low, high)
        other = jnp.where(first_core, high, low)
        other_ref[:, place : place + 16, :] = other.astype(jnp.bfloat16)


def cross_power(order, got):
    _, sources, pairs, lines, rows = got.shape
    every = sources * 2 * pairs
    shape = (every // 8, 2 * lines, every)
    whole = pl.BlockSpec(memory_space=pltpu.VMEM)
    return pl.pallas_call(
        csd_kernel,
        in_specs=[whole, whole],
        out_specs=[whole, whole],
        out_shape=[
            jax.ShapeDtypeStruct(shape, jnp.float32),
            jax.ShapeDtypeStruct(shape, jnp.bfloat16),
        ],
        scratch_shapes=[pltpu.VMEM((lines // 2, every, PAIR * rows), jnp.bfloat16)],
        compiler_params=pltpu.CompilerParams(vmem_limit_bytes=VMEM),
        name="csd",
    )(order, got)


def total_kernel(got_ref, out_ref, sum_ref):
    own, parts, freqs, _ = out_ref.shape
    sum_ref[...] = jnp.sum(got_ref[...].astype(jnp.float32), axis=1)
    few = freqs // PAIR
    for half in range(PAIR):
        for part in range(parts):
            for freq in range(few):
                for i in range(own):
                    row = (part * few + freq) * own + i
                    place = half * few + freq
                    out_ref[i, part, place : place + 1, :] = sum_ref[half, row : row + 1, :]


def totals(got, freqs):
    halves, _, lines, every = got.shape
    whole = pl.BlockSpec(memory_space=pltpu.VMEM)
    return pl.pallas_call(
        total_kernel,
        in_specs=[whole],
        out_specs=whole,
        out_shape=jax.ShapeDtypeStruct((lines * halves // (2 * freqs), 2, freqs, every), jnp.float32),
        scratch_shapes=[pltpu.VMEM((halves, lines, every), jnp.float32)],
        compiler_params=pltpu.CompilerParams(vmem_limit_bytes=VMEM),
        name="total",
    )(got)


def body(snapshots, weights, block_delay):
    groups = lax.axis_size("tm")
    chips = lax.axis_size("chip")
    targets = PAIR * groups
    total_rows = snapshots.shape[0] * PAIR * chips * CORES

    def exchange(array, axes):
        return lax.all_to_all(array, axes, split_axis=0, concat_axis=0, tiled=True)

    rim = shifted(packed_rim(snapshots[:, :RIM].astype(jnp.bfloat16)), "tm", -1)
    scale = jnp.sqrt(weights / total_rows).reshape(1, -1)
    begun, tail, table, order = early_spectra(
        snapshots, scale, block_delay, dft_rows(groups), targets
    )
    spectra = late_spectra(begun, tail, table, scale, rim)
    received = exchange(spectra, ("half", "tm"))
    received = received.reshape((PAIR, groups) + received.shape[1:])
    own, other = cross_power(order, received)
    pair = (own + shifted(other, "core", 1).astype(jnp.float32)).astype(jnp.bfloat16)
    got = exchange(pair, ("half", "chip"))
    return totals(got.reshape((PAIR, chips) + got.shape[1:]), NF // groups)


def solution(mesh):
    rows, groups = mesh.devices.shape
    row = ("half", "chip", "core")
    split = Mesh(
        mesh.devices.reshape(PAIR, rows // PAIR // CORES, CORES, groups), row + ("tm",)
    )
    return jax.shard_map(
        body,
        mesh=split,
        in_specs=(P(row, "tm"), P(row), P("tm")),
        out_specs=P(row, None, "tm", None),
        check_vma=False,
    )
```
